32 devices in a mesh: section: 2 (over x), ctx: 16 (over z, y, core).
Axes of the slice: x: 2, y: 2, z: 4, core: 2. Of those that a mesh axis runs over, the one named last changes fastest.
Arguments:
- inputs: bfloat16 [2, 1024, 2048], P('section', None, 'ctx'), may hold values from -6 to 6
- out_grad: bfloat16 [1024, 2048], P(None, 'ctx'), may hold values from -6 to 6
- filters: bfloat16 [2, 1024, 2048], P('section', 'ctx'), may hold values from -0.125 to 0.125
- conv_taps: float32 [2, 3, 7, 1024], P('section'), may hold values from -2.5 to 2.5
Outputs:
- in_grad: bfloat16 [2, 1024, 2048], P('section', None, 'ctx')
- filter_grad: float32 [2, 1024, 2048], P('section', 'ctx')
- tap_grad: float32 [2, 3, 7, 1024], P('section', None, None, 'ctx')
The draws below stay inside these ranges and needn't reach their ends.
All inputs are finite; a program needn't handle non-finite values.
Results may differ from the reference program's by a relative error of at most 0.014.
Values may be sent and summed in bfloat16 or wider, within the bound.
A program may use at most 64 MiB of HBM per device.

```python
import jax
import jax.numpy as jnp

D = 1024
TAPS = 7
TOKENS = 2048
SECTIONS = 2


def steps_of(stream_key, extent, pieces, low, top_value):
    gain, own = 1.0, jax.random.fold_in(stream_key, 6)
    for position, parts in pieces:
        draws = jnp.exp(jax.random.uniform(jax.random.fold_in(own, position), (parts,), jnp.float32, low / len(pieces), top_value / len(pieces)))
        gain = gain * jnp.repeat(draws, extent[position] // parts).reshape([-1 if axis == position else 1 for axis in range(len(extent))])
    return gain


def noise(own_key, extent, deviation, bound, cuts=(), dtype=jnp.bfloat16):
    loudness = steps_of(own_key, extent, cuts, -0.22, 0.18) if cuts else 1.0
    array = jax.random.normal(own_key, extent, jnp.float32) * deviation * loudness
    return jnp.minimum(jnp.maximum(array, -bound), bound).astype(dtype)


def setup_inputs(seed: int = 0) -> dict:
    key_list = jax.random.split(jax.random.key(seed), 5)
    return {
        "inputs": noise(key_list[0], (SECTIONS, D, TOKENS), 1.0, 6.0, ((0, 2), (2, 16))),
        "out_grad": noise(key_list[1], (D, TOKENS), 1.0, 6.0, ((1, 16),)),
        "filters": noise(key_list[2], (SECTIONS, D, TOKENS), TOKENS ** -0.5, 0.125, ((0, 2), (1, 16))),
        "conv_taps": noise(key_list[3], (SECTIONS, 3, TAPS, D), 0.34, 2.5, ((0, 2),), jnp.float32),
    }


def features(padded, weights, length):
    summed = jnp.zeros((3, padded.shape[0], length), jnp.float32)
    for offset in range(7):
        window = padded[:, 6 - offset:6 - offset + length].astype(jnp.float32)
        summed = summed + weights[:, offset, :, None] * window[None]
    return summed.astype(jnp.bfloat16)


def transposed(grad_all, weights):
    length = grad_all.shape[2]
    padded = jnp.pad(grad_all, ((0, 0), (0, 0), (0, 6)))
    summed = jnp.zeros(grad_all.shape[1:], jnp.float32)
    for offset in range(7):
        summed = summed + jnp.sum(weights[:, offset, :, None] * padded[:, :, offset:offset + length], axis=0)
    return summed


def tap_grads(padded, grad_all):
    length = grad_all.shape[2]
    per_offset = []
    for offset in range(7):
        window = padded[:, 6 - offset:6 - offset + length].astype(jnp.float32)
        per_offset.append(jnp.sum(grad_all * window[None], axis=2))
    return jnp.stack(per_offset, axis=1)


def reference(inputs, out_grad, filters, conv_taps):
    section_total = inputs.shape[0]
    length = inputs.shape[2]
    fft_len = 2 * length
    in_list = []
    filter_list = []
    tap_list = []
    carried = out_grad
    for section_idx in range(section_total - 1, -1, -1):
        weights = conv_taps[section_idx]
        padded = jnp.pad(inputs[section_idx], ((0, 0), (6, 0)))
        featured = features(padded, weights, length)
        query_feat = featured[0].astype(jnp.float32)
        key_feat = featured[1].astype(jnp.float32)
        value_feat = featured[2].astype(jnp.float32)
        mixed_kv = key_feat * value_feat
        spec_h = jnp.fft.rfft(filters[section_idx].astype(jnp.float32), n=fft_len, axis=1)
        spec_w = jnp.fft.rfft(mixed_kv, n=fft_len, axis=1)
        convolved = jnp.fft.irfft(spec_h * spec_w, n=fft_len, axis=1)[:, :length]
        grad_in = carried.astype(jnp.float32)
        grad_z = grad_in * query_feat
        grad_q = grad_in * convolved
        spec_dz = jnp.fft.rfft(grad_z, n=fft_len, axis=1)
        grad_w = jnp.fft.irfft(jnp.conj(spec_h) * spec_dz, n=fft_len, axis=1)[:, :length]
        grad_all = jnp.stack([grad_q, grad_w * value_feat, grad_w * key_feat])
        in_grad = transposed(grad_all, weights).astype(jnp.bfloat16)
        filter_grad = jnp.fft.irfft(jnp.conj(spec_w) * spec_dz, n=fft_len, axis=1)[:, :length]
        in_list.insert(0, in_grad)
        filter_list.insert(0, filter_grad)
        tap_list.insert(0, tap_grads(padded, grad_all))
        carried = in_grad
    return (jnp.stack(in_list), jnp.stack(filter_list), jnp.stack(tap_list))
```

```python
import functools
import math

import jax
import jax.numpy as jnp
import ml_dtypes
import numpy as np
from jax import lax
from jax.experimental import pallas as pl
from jax.experimental.pallas import tpu as pltpu
from jax.sharding import PartitionSpec as P

PRECISE = lax.Precision.HIGH


def shifted(block, axis, distance):
    devices = range(lax.axis_size(axis))
    route = [(i - distance, i) for i in devices if i - distance in devices]
    return lax.ppermute(block, axis, route)


def angle_table(row_count, col_count, modulus):
    row_ids = lax.broadcasted_iota(jnp.int32, (row_count, col_count), 0)
    col_ids = lax.broadcasted_iota(jnp.int32, (row_count, col_count), 1)
    product_mod = row_ids * col_ids % modulus
    angles = product_mod.astype(jnp.float32) * (2.0 * math.pi / modulus)
    return (jnp.cos(angles), jnp.sin(angles))


def make_tables(blocks_a, block_b):
    half_a = blocks_a // 2
    total_n = blocks_a * block_b
    return (
        angle_table(blocks_a, half_a, blocks_a),
        angle_table(half_a, blocks_a, blocks_a),
        angle_table(blocks_a, block_b, total_n),
        angle_table(block_b, block_b, block_b),
    )


def forward_spectrum(signal, tables):
    cos_one, sin_one = tables[0]
    cos_tw, sin_tw = tables[2]
    cos_two, sin_two = tables[3]
    channels = signal.shape[0]
    half_a = cos_one.shape[1]
    block_b = cos_two.shape[0]
    shaped = signal.reshape(channels, half_a, block_b)
    real_y = jnp.einsum("ka,cab->ckb", cos_one, shaped, precision=PRECISE)
    imag_y = -jnp.einsum("ka,cab->ckb", sin_one, shaped, precision=PRECISE)
    real_z = real_y * cos_tw + imag_y * sin_tw
    imag_z = imag_y * cos_tw - real_y * sin_tw
    real_x = jnp.einsum("ckb,mb->ckm", real_z, cos_two, precision=PRECISE) + jnp.einsum(
        "ckb,mb->ckm", imag_z, sin_two, precision=PRECISE
    )
    imag_x = jnp.einsum("ckb,mb->ckm", imag_z, cos_two, precision=PRECISE) - jnp.einsum(
        "ckb,mb->ckm", real_z, sin_two, precision=PRECISE
    )
    return (real_x, imag_x)


def inverse_signal(real_x, imag_x, tables):
    cos_one, sin_one = tables[1]
    cos_tw, sin_tw = tables[2]
    cos_two, sin_two = tables[3]
    channels = real_x.shape[0]
    half_a = cos_one.shape[0]
    block_b = cos_two.shape[0]
    total_n = cos_one.shape[1] * block_b
    real_p = jnp.einsum("ckm,mb->ckb", real_x, cos_two, precision=PRECISE) - jnp.einsum(
        "ckm,mb->ckb", imag_x, sin_two, precision=PRECISE
    )
    imag_p = jnp.einsum("ckm,mb->ckb", real_x, sin_two, precision=PRECISE) + jnp.einsum(
        "ckm,mb->ckb", imag_x, cos_two, precision=PRECISE
    )
    real_q = real_p * cos_tw - imag_p * sin_tw
    imag_q = real_p * sin_tw + imag_p * cos_tw
    summed = jnp.einsum("ak,ckb->cab", cos_one, real_q, precision=PRECISE) - jnp.einsum(
        "ak,ckb->cab", sin_one, imag_q, precision=PRECISE
    )
    return summed.reshape(channels, half_a * block_b) / total_n


def times_conj(real_a, imag_a, real_b, imag_b):
    return (real_a * real_b + imag_a * imag_b, real_a * imag_b - imag_a * real_b)


def features(padded, weights, length):
    summed = jnp.zeros((3, padded.shape[0], length), jnp.float32)
    for offset in range(7):
        window = padded[:, 6 - offset : 6 - offset + length].astype(jnp.float32)
        summed = summed + weights[:, offset, :, None] * window[None]
    return summed.astype(jnp.bfloat16)


def transposed(grad_all, weights):
    length = grad_all.shape[2]
    padded = jnp.pad(grad_all, ((0, 0), (0, 0), (0, 6)))
    summed = jnp.zeros(grad_all.shape[1:], jnp.float32)
    for offset in range(7):
        summed = summed + jnp.sum(
            weights[:, offset, :, None] * padded[:, :, offset : offset + length], axis=0
        )
    return summed


def tap_grads(padded, grad_all):
    length = grad_all.shape[2]
    per_offset = []
    for offset in range(7):
        window = padded[:, 6 - offset : 6 - offset + length].astype(jnp.float32)
        per_offset.append(jnp.sum(grad_all * window[None], axis=2))
    return jnp.stack(per_offset, axis=1)


def take_rows(array, first_ch, count, axis_num):
    return lax.dynamic_slice_in_dim(array, first_ch, count, axis_num)


def masked_write(array, update, first_ch, active, axis_num):
    previous = lax.dynamic_slice_in_dim(array, first_ch, update.shape[axis_num], axis_num)
    return lax.dynamic_update_slice_in_dim(
        array, jnp.where(active, update, previous), first_ch, axis_num
    )


def shards(inputs, out_grad, filters, conv_taps):
    x_rows = inputs[0]
    tok_dev = x_rows.shape[1]
    section_count = lax.axis_size("section")
    section_idx = lax.axis_index("section")
    ctx_idx = lax.axis_index("ctx")
    weights = conv_taps[0]
    channels = filters.shape[1]
    length = filters.shape[2]
    blocks_a = 2 * length // tok_dev
    own_taps = lax.dynamic_slice_in_dim(weights, ctx_idx * channels, channels, 2)
    prior_cols = shifted(x_rows[:, tok_dev - 6 :], "ctx", 1)
    featured_rows = features(jnp.concatenate([prior_cols, x_rows], axis=1), weights, tok_dev)
    x_chan, featured, grad_chan = (
        lax.all_to_all(x_rows[None], "ctx", split_axis=1, concat_axis=2, tiled=True),
        lax.all_to_all(featured_rows, "ctx", split_axis=1, concat_axis=2, tiled=True),
        lax.all_to_all(out_grad[None], "ctx", split_axis=1, concat_axis=2, tiled=True),
    )
    x_chan = x_chan[0]
    x_padded = jnp.pad(x_chan, ((0, 0), (6, 0)))
    grad_chan = grad_chan[0]
    tables = make_tables(blocks_a, tok_dev)
    key_full = featured[1].astype(jnp.float32)
    mixed_kv = key_full * featured[2].astype(jnp.float32)
    real_h, imag_h = forward_spectrum(filters[0].astype(jnp.float32), tables)
    real_w, imag_w = forward_spectrum(mixed_kv, tables)
    convolved = inverse_signal(
        real_h * real_w - imag_h * imag_w, real_h * imag_w + imag_h * real_w, tables
    )
    block_ch = 2
    block_count = channels // block_ch
    last_section = section_count - 1
    turns = block_count + section_count - 1
    dx_init = jnp.zeros((channels, length), jnp.bfloat16)

    def advance(turn_idx, carried):
        incoming, dz_all, dx_store, tap_acc = carried
        block_id = turn_idx - (last_section - section_idx)
        active = (block_id >= 0) & (block_id < block_count)
        first_ch = jnp.clip(block_id, 0, block_count - 1) * block_ch
        from_next = take_rows(grad_chan, first_ch, block_ch, 0)
        grad_in = jnp.where(section_idx == last_section, from_next, incoming).astype(jnp.float32)
        feat_blk = take_rows(featured, first_ch, block_ch, 1).astype(jnp.float32)
        grad_z = grad_in * feat_blk[0]
        grad_q = grad_in * take_rows(convolved, first_ch, block_ch, 0)
        real_d, imag_d = forward_spectrum(grad_z, tables)
        real_c, imag_c = times_conj(
            take_rows(real_h, first_ch, block_ch, 0),
            take_rows(imag_h, first_ch, block_ch, 0),
            real_d,
            imag_d,
        )
        grad_w = inverse_signal(real_c, imag_c, tables)
        grad_all = jnp.stack([grad_q, grad_w * feat_blk[2], grad_w * feat_blk[1]])
        in_blk = transposed(grad_all, take_rows(own_taps, first_ch, block_ch, 2)).astype(
            jnp.bfloat16
        )
        tap_new = tap_grads(take_rows(x_padded, first_ch, block_ch, 0), grad_all)
        tap_acc = masked_write(tap_acc, tap_new, first_ch, active, 2)
        dz_all = masked_write(dz_all, grad_z, first_ch, active, 0)
        outgoing = shifted(in_blk, "section", -1)
        dx_store = masked_write(dx_store, in_blk, first_ch, active, 0)
        return (outgoing, dz_all, dx_store, tap_acc)

    start_state = (
        jnp.zeros((block_ch, length), jnp.bfloat16),
        jnp.zeros((channels, length), jnp.float32),
        dx_init,
        jnp.zeros((3, 7, channels), jnp.float32),
    )
    final_state = lax.fori_loop(0, turns, advance, start_state)
    dz_all = final_state[1]
    dx_store = final_state[2]
    tap_acc = final_state[3]
    real_d, imag_d = forward_spectrum(dz_all, tables)
    real_c, imag_c = times_conj(real_w, imag_w, real_d, imag_d)
    filter_grad = inverse_signal(real_c, imag_c, tables)
    in_rows = lax.all_to_all(dx_store, "ctx", split_axis=1, concat_axis=0, tiled=True)
    return (in_rows[None], filter_grad[None], tap_acc[None])


TAPS = 7
GROUP = 16
MESH = pl.DeviceIdType.MESH
F32 = jnp.float32
BF16 = jnp.bfloat16


def right_angle_tables(blocks_a, block_b):
    total_n = blocks_a * block_b
    first_k = np.arange(blocks_a)
    phase_one = 2 * np.pi * np.outer(first_k + 0.25, np.arange(blocks_a)) / blocks_a
    one = np.stack([np.cos(phase_one), -np.sin(phase_one)])
    first = np.einsum("rka,cd->rkcad", one, np.eye(GROUP))
    first = first.reshape(2 * blocks_a * GROUP, blocks_a * GROUP)
    points = first_k[:, None, None] + 0.25 + blocks_a * np.arange(block_b)[None, None, :]
    phase_two = 2 * np.pi * np.arange(block_b)[None, :, None] * points / total_n
    real, imag = np.cos(phase_two), -np.sin(phase_two)
    second = np.concatenate(
        [np.concatenate([real, imag], axis=2), np.concatenate([-imag, real], axis=2)], axis=1
    )
    return tuple(
        array.astype(ml_dtypes.bfloat16)
        for array in (first, first.T / total_n, second, second.transpose(0, 2, 1))
    )


def mixer_kernel(
    sections,
    x_ref,
    og_ref,
    filt_ref,
    tap_ref,
    one_ref,
    one_inv_ref,
    two_ref,
    two_inv_ref,
    ig_out,
    fg_out,
    tg_out,
    xbuf,
    ogbuf,
    hbuf,
    tbuf,
    one_v,
    one_inv_v,
    two_v,
    two_inv_v,
    tapb,
    xs_ref,
    feat,
    sig,
    ybuf,
    spec,
    dspec,
    qbuf,
    cbuf,
    gwbuf,
    gbuf,
    igbuf,
    fgbuf,
    tgbuf,
    x_send,
    x_recv,
    og_send,
    og_recv,
    h_send,
    h_recv,
    t_send,
    t_recv,
    ig_send,
    ig_recv,
    fg_send,
    fg_recv,
    tg_send,
    tg_recv,
    table_sem,
):
    sec = lax.axis_index("section")
    ctx = lax.axis_index("ctx")
    blocks = xbuf.shape[1]
    rows = xbuf.shape[2]
    lanes = xbuf.shape[3]
    groups = rows // GROUP
    other = 1 - sec

    tables = [
        pltpu.make_async_copy(src, dst, table_sem.at[n])
        for n, (src, dst) in enumerate(
            ((one_ref, one_v), (two_ref, two_v), (one_inv_ref, one_inv_v), (two_inv_ref, two_inv_v))
        )
    ]

    barrier = pltpu.get_barrier_semaphore()

    def greet(step, carry):
        to_ctx = lax.rem(ctx + step, blocks)
        pl.semaphore_signal(barrier, inc=1, device_id=(other, to_ctx), device_id_type=MESH)

        @pl.when(step > 0)
        def _():
            pl.semaphore_signal(barrier, inc=1, device_id=(sec, to_ctx), device_id_type=MESH)

        return carry

    lax.fori_loop(0, blocks, greet, 0)
    for table in tables:
        table.start()
    pl.semaphore_wait(barrier, sections * blocks - 1)

    def row_block(to_sec, to_ctx):
        return pl.ds(pl.multiple_of((to_ctx * sections + to_sec) * rows, rows), rows)

    def half(which):
        return pl.ds(pl.multiple_of(which * rows, rows), rows)

    def remote(src, dst, send_sem, recv_sem, to_sec, to_ctx):
        pltpu.make_async_remote_copy(
            src_ref=src,
            dst_ref=dst,
            send_sem=send_sem,
            recv_sem=recv_sem,
            device_id=(to_sec, to_ctx),
            device_id_type=MESH,
        ).start()

    def await_bytes(ref, sem):
        pltpu.make_async_copy(ref, ref, sem).wait()

    remote(filt_ref.at[half(other)], hbuf.at[sec], h_send, h_recv, other, ctx)
    pltpu.make_async_copy(filt_ref.at[half(sec)], hbuf.at[sec], h_recv).start()
    remote(tap_ref.at[half(other)], tbuf.at[sec], t_send, t_recv, other, ctx)
    pltpu.make_async_copy(tap_ref.at[half(sec)], tbuf.at[sec], t_recv).start()

    def send_x(step, carry):
        to_ctx = lax.rem(ctx + step, blocks)
        dst = xbuf.at[sec, ctx]
        remote(x_ref.at[row_block(other, to_ctx)], dst, x_send, x_recv.at[sec], other, to_ctx)

        @pl.when(step > 0)
        def _():
            remote(x_ref.at[row_block(sec, to_ctx)], dst, x_send, x_recv.at[sec], sec, to_ctx)

        return carry

    pltpu.make_async_copy(
        x_ref.at[row_block(sec, ctx)], xbuf.at[sec, ctx], x_recv.at[sec]
    ).start()
    lax.fori_loop(0, blocks, send_x, 0)

    def send_og(step, carry):
        to_ctx = lax.rem(ctx + step, blocks)
        remote(og_ref.at[row_block(sec, to_ctx)], ogbuf.at[ctx], og_send, og_recv, sec, to_ctx)
        return carry

    pltpu.make_async_copy(og_ref.at[row_block(sec, ctx)], ogbuf.at[ctx], og_recv).start()
    lax.fori_loop(1, blocks, send_og, 0)

    def stage_one(blocks_of, first_row):
        cols = jnp.concatenate(
            [blocks_of(g).reshape(blocks * GROUP, lanes) for g in range(groups)], axis=1
        )
        out = jnp.dot(one_v[...], cols, preferred_element_type=F32).astype(BF16)
        out = out.reshape(2, blocks, GROUP, groups * lanes)
        for g in range(groups):
            for part in range(2):
                ybuf[:, pl.ds(first_row + g * GROUP, GROUP), pl.ds(part * lanes, lanes)] = out[
                    part, :, :, g * lanes : (g + 1) * lanes
                ]

    def stage_two(first_row, count, dst):
        def body(k, carry):
            dst[k, pl.ds(first_row, count)] = jnp.dot(
                ybuf[k, pl.ds(first_row, count)], two_v[k], preferred_element_type=F32
            )
            return carry

        lax.fori_loop(0, blocks, body, 0, unroll=4)

    def product(left, right, conj):
        left_r, left_i = left[:, :lanes], left[:, lanes:]
        right_r, right_i = right[:, :lanes], right[:, lanes:]
        if conj:
            real = left_r * right_r + left_i * right_i
            imag = left_r * right_i - left_i * right_r
        else:
            real = left_r * right_r - left_i * right_i
            imag = left_r * right_i + left_i * right_r
        return jnp.concatenate([real, imag], axis=1).astype(BF16)

    def inverse_two(operand, slots):
        def body(k, carry):
            out = jnp.dot(operand(k), two_inv_v[k], preferred_element_type=F32).astype(BF16)
            for slot in range(slots):
                for g in range(groups):
                    first = (slot * groups + g) * GROUP
                    for part in range(2):
                        qbuf[slot, part, k, :, pl.ds(g * lanes, lanes)] = out[
                            first : first + GROUP, part * lanes : (part + 1) * lanes
                        ]
            return carry

        lax.fori_loop(0, blocks, body, 0, unroll=4)

    def inverse_one(slot):
        out = jnp.dot(
            one_inv_v[...],
            qbuf[slot].reshape(2 * blocks * GROUP, groups * lanes),
            preferred_element_type=F32,
        )
        return out.reshape(blocks, GROUP, groups * lanes)

    tables[0].wait()
    tables[1].wait()
    await_bytes(hbuf, h_recv)
    for layer in range(sections):
        stage_one(
            lambda g: jnp.stack(
                [
                    hbuf[layer, pl.ds(g * GROUP, GROUP), pl.ds(a * lanes, lanes)]
                    for a in range(blocks)
                ]
            ),
            layer * rows,
        )
    stage_two(0, sections * rows, spec)

    await_bytes(tbuf, t_recv)
    for layer in range(sections):
        values = tbuf[layer]
        for n in range(3 * TAPS):
            tapb[layer, n] = jnp.broadcast_to(values[:, n : n + 1], (rows, lanes))

    lane = lax.broadcasted_iota(jnp.int32, (rows, lanes), 1)

    def features_of(layer):
        def body(a, before):
            window = xbuf[layer, a].astype(F32)
            sums = [None] * 3
            rolled = []
            for j in range(TAPS):
                if j == 0:
                    moved = window
                else:
                    turned = pltpu.roll(window, j, 1)
                    rolled.append(turned)
                    moved = jnp.where(lane < j, before[j - 1], turned)
                xs_ref[layer, j, a] = moved
                for i in range(3):
                    term = tapb[layer, i * TAPS + j] * moved
                    sums[i] = term if sums[i] is None else sums[i] + term
            rounded = [total.astype(BF16) for total in sums]
            for i in range(3):
                feat[layer, i, a] = rounded[i]
            sig[a] = (rounded[1].astype(F32) * rounded[2].astype(F32)).astype(BF16)
            return tuple(rolled)

        zero = jnp.zeros((rows, lanes), F32)
        lax.fori_loop(0, blocks, body, (zero,) * (TAPS - 1))

    mixed_row = sections * rows
    for layer in range(sections - 1, -1, -1):
        await_bytes(xbuf.at[layer], x_recv.at[layer])
        features_of(layer)
        stage_one(lambda g: sig[:, pl.ds(g * GROUP, GROUP), :], mixed_row + layer * rows)
    stage_two(mixed_row, sections * rows, spec)
    tables[2].wait()
    tables[3].wait()
    inverse_two(
        lambda k: product(
            spec[k, pl.ds(0, sections * rows)], spec[k, pl.ds(mixed_row, sections * rows)], False
        ),
        sections,
    )
    for layer in range(sections):
        out = inverse_one(layer)
        for g in range(groups):
            cbuf[layer, :, pl.ds(g * GROUP, GROUP), :] = out[:, :, g * lanes : (g + 1) * lanes]

    for layer in range(sections - 1, -1, -1):
        if layer == sections - 1:
            await_bytes(ogbuf, og_recv)
            carried = ogbuf
        else:
            carried = igbuf.at[layer + 1]

        sig[...] = (carried[...].astype(F32) * feat[layer, 0].astype(F32)).astype(BF16)
        stage_one(lambda g: sig[:, pl.ds(g * GROUP, GROUP), :], 0)
        stage_two(0, rows, dspec)

        def both(k):
            d_spec = dspec[k]
            with_h = product(spec[k, pl.ds(layer * rows, rows)], d_spec, True)
            with_w = product(spec[k, pl.ds(mixed_row + layer * rows, rows)], d_spec, True)
            return jnp.concatenate([with_h, with_w], axis=0)

        inverse_two(both, 2)
        out = inverse_one(0)
        for g in range(groups):
            gwbuf[:, pl.ds(g * GROUP, GROUP), :] = out[:, :, g * lanes : (g + 1) * lanes]

        def transposed_at(step, after):
            a = blocks - 1 - step
            grad_w = gwbuf[a]
            grads = (
                carried[a].astype(F32) * cbuf[layer, a],
                grad_w * feat[layer, 2, a].astype(F32),
                grad_w * feat[layer, 1, a].astype(F32),
            )
            for i in range(3):
                gbuf[i, a] = grads[i]
            total = None
            rolled = []
            for j in range(TAPS):
                part = tapb[layer, j] * grads[0]
                for i in range(1, 3):
                    part = part + tapb[layer, i * TAPS + j] * grads[i]
                if j == 0:
                    total = part
                else:
                    turned = pltpu.roll(part, lanes - j, 1)
                    rolled.append(turned)
                    total = total + jnp.where(lane < lanes - j, turned, after[j - 1])
            igbuf[layer, a] = total.astype(BF16)
            return tuple(rolled)

        zero = jnp.zeros((rows, lanes), F32)
        lax.fori_loop(0, blocks, transposed_at, (zero,) * (TAPS - 1))

        def send_ig(step, carry):
            to_ctx = lax.rem(ctx + step, blocks)
            src = igbuf.at[layer, to_ctx]
            dst = ig_out.at[row_block(sec, ctx)]
            local = (sec == layer) & (step == 0)

            @pl.when(local)
            def _():
                pltpu.make_async_copy(src, dst, ig_recv).start()

            @pl.when(jnp.logical_not(local))
            def _():
                remote(src, dst, ig_send, ig_recv, layer, to_ctx)

            return carry

        lax.fori_loop(0, blocks, send_ig, 0)

        out = inverse_one(1)
        for a in range(blocks):
            for g in range(groups):
                fgbuf[layer, pl.ds(g * GROUP, GROUP), pl.ds(a * lanes, lanes)] = out[
                    a, :, g * lanes : (g + 1) * lanes
                ]

        def send_home(src, dst, send_sem, recv_sem):
            @pl.when(sec == layer)
            def _():
                pltpu.make_async_copy(src, dst, recv_sem).start()

            @pl.when(sec != layer)
            def _():
                remote(src, dst, send_sem, recv_sem, layer, ctx)

        send_home(fgbuf.at[layer], fg_out.at[half(sec)], fg_send, fg_recv)

        for first in range(0, rows, 8):
            def add_taps(a, sums):
                grads = [gbuf[i, a, pl.ds(first, 8)] for i in range(3)]
                new = []
                for j in range(TAPS):
                    moved = xs_ref[layer, j, a, pl.ds(first, 8)]
                    for i in range(3):
                        new.append(sums[j * 3 + i] + grads[i] * moved)
                return tuple(new)

            zero_8 = jnp.zeros((8, lanes), F32)
            sums = lax.fori_loop(0, blocks, add_taps, (zero_8,) * (3 * TAPS))
            lane_8 = lax.broadcasted_iota(jnp.int32, (8, lanes), 1)
            packed = zero_8
            for j in range(TAPS):
                for i in range(3):
                    column = jnp.sum(sums[j * 3 + i], axis=1, keepdims=True)
                    packed = jnp.where(lane_8 == i * TAPS + j, column, packed)
            tgbuf[layer, pl.ds(first, 8)] = packed
        send_home(tgbuf.at[layer], tg_out.at[half(sec)], tg_send, tg_recv)

    others = sections * blocks - 1
    await_bytes(x_ref.at[pl.ds(0, others * rows)], x_send)
    await_bytes(og_ref.at[pl.ds(0, (blocks - 1) * rows)], og_send)
    await_bytes(filt_ref.at[pl.ds(0, rows)], h_send)
    await_bytes(tap_ref.at[pl.ds(0, rows)], t_send)
    await_bytes(ig_out.at[pl.ds(0, others * rows)], ig_send)
    await_bytes(fg_out.at[pl.ds(0, rows)], fg_send)
    await_bytes(tg_out.at[pl.ds(0, rows)], tg_send)
    await_bytes(ig_out, ig_recv)
    await_bytes(fg_out, fg_recv)
    await_bytes(tg_out, tg_recv)


def kernel_shards(inputs, out_grad, filters, conv_taps):
    sections = lax.axis_size("section")
    blocks = lax.axis_size("ctx")
    ctx_idx = lax.axis_index("ctx")
    _, depth, lanes = inputs.shape
    _, channels, length = filters.shape
    rows = channels // sections
    tables = right_angle_tables(blocks, lanes)
    own = lax.dynamic_slice_in_dim(conv_taps[0], ctx_idx * channels, channels, 2)
    own = own.reshape(3 * TAPS, channels).T
    own = jnp.pad(own, ((0, 0), (0, lanes - 3 * TAPS)))
    vmem = pltpu.VMEM
    dma = pltpu.SemaphoreType.DMA
    any_spec = pl.BlockSpec(memory_space=pl.ANY)
    spectrum_rows = 2 * sections * rows
    in_grad, filter_grad, tap_sums = pl.pallas_call(
        functools.partial(mixer_kernel, sections),
        out_shape=(
            jax.ShapeDtypeStruct((depth, lanes), BF16),
            jax.ShapeDtypeStruct((channels, length), F32),
            jax.ShapeDtypeStruct((channels, lanes), F32),
        ),
        in_specs=[any_spec] * 8,
        out_specs=(any_spec,) * 3,
        scratch_shapes=[
            vmem((sections, blocks, rows, lanes), BF16),
            vmem((blocks, rows, lanes), BF16),
            vmem((sections, rows, length), BF16),
            vmem((sections, rows, lanes), F32),
            vmem(tables[0].shape, BF16),
            vmem(tables[1].shape, BF16),
            vmem(tables[2].shape, BF16),
            vmem(tables[3].shape, BF16),
            vmem((sections, 3 * TAPS, rows, lanes), F32),
            vmem((sections, TAPS, blocks, rows, lanes), F32),
            vmem((sections, 3, blocks, rows, lanes), BF16),
            vmem((blocks, rows, lanes), BF16),
            vmem((blocks, spectrum_rows, 2 * lanes), BF16),
            vmem((blocks, spectrum_rows, 2 * lanes), F32),
            vmem((blocks, rows, 2 * lanes), F32),
            vmem((2, 2, blocks, GROUP, rows // GROUP * lanes), BF16),
            vmem((sections, blocks, rows, lanes), F32),
            vmem((blocks, rows, lanes), F32),
            vmem((3, blocks, rows, lanes), F32),
            vmem((sections, blocks, rows, lanes), BF16),
            vmem((sections, rows, length), F32),
            vmem((sections, rows, lanes), F32),
            dma(()),
            dma((sections,)),
            dma(()),
            dma(()),
            dma(()),
            dma(()),
            dma(()),
            dma(()),
            dma(()),
            dma(()),
            dma(()),
            dma(()),
            dma(()),
            dma(()),
            dma((4,)),
        ],
        compiler_params=pltpu.CompilerParams(
            collective_id=0, has_side_effects=True, vmem_limit_bytes=40 * 2**20
        ),
    )(inputs[0], out_grad, filters[0], own, *(jnp.asarray(table) for table in tables))
    tap_grad = tap_sums[:, : 3 * TAPS].T.reshape(3, TAPS, channels)
    return (in_grad[None], filter_grad[None], tap_grad[None])


def solution(mesh):
    placed = (
        P("section", None, "ctx"),
        P(None, "ctx"),
        P("section", "ctx", None),
        P("section", None, None, None),
    )

    def run(inputs, out_grad, filters, conv_taps):
        sections, blocks = mesh.shape["section"], mesh.shape["ctx"]
        rows = filters.shape[1] // (sections * blocks)
        lanes = inputs.shape[2] // blocks
        fits = sections == 2 and rows % GROUP == 0 and lanes == 128
        return jax.shard_map(
            kernel_shards if fits else shards,
            mesh=mesh,
            in_specs=placed,
            out_specs=(
                P("section", None, "ctx"),
                P("section", "ctx", None),
                P("section", None, None, "ctx"),
            ),
            check_vma=False,
        )(inputs, out_grad, filters, conv_taps)

    return run
```

```python
import functools
import math

import jax
import jax.numpy as jnp
import ml_dtypes
import numpy as np
from jax import lax
from jax.experimental import pallas as pl
from jax.experimental.pallas import tpu as pltpu
from jax.sharding import PartitionSpec as P

PRECISE = lax.Precision.HIGH


def shifted(block, axis, distance):
    devices = range(lax.axis_size(axis))
    route = [(i - distance, i) for i in devices if i - distance in devices]
    return lax.ppermute(block, axis, route)


def angle_table(row_count, col_count, modulus):
    row_ids = lax.broadcasted_iota(jnp.int32, (row_count, col_count), 0)
    col_ids = lax.broadcasted_iota(jnp.int32, (row_count, col_count), 1)
    product_mod = row_ids * col_ids % modulus
    angles = product_mod.astype(jnp.float32) * (2.0 * math.pi / modulus)
    return (jnp.cos(angles), jnp.sin(angles))


def make_tables(blocks_a, block_b):
    half_a = blocks_a // 2
    total_n = blocks_a * block_b
    return (
        angle_table(blocks_a, half_a, blocks_a),
        angle_table(half_a, blocks_a, blocks_a),
        angle_table(blocks_a, block_b, total_n),
        angle_table(block_b, block_b, block_b),
    )


def forward_spectrum(signal, tables):
    cos_one, sin_one = tables[0]
    cos_tw, sin_tw = tables[2]
    cos_two, sin_two = tables[3]
    channels = signal.shape[0]
    half_a = cos_one.shape[1]
    block_b = cos_two.shape[0]
    shaped = signal.reshape(channels, half_a, block_b)
    real_y = jnp.einsum("ka,cab->ckb", cos_one, shaped, precision=PRECISE)
    imag_y = -jnp.einsum("ka,cab->ckb", sin_one, shaped, precision=PRECISE)
    real_z = real_y * cos_tw + imag_y * sin_tw
    imag_z = imag_y * cos_tw - real_y * sin_tw
    real_x = jnp.einsum("ckb,mb->ckm", real_z, cos_two, precision=PRECISE) + jnp.einsum(
        "ckb,mb->ckm", imag_z, sin_two, precision=PRECISE
    )
    imag_x = jnp.einsum("ckb,mb->ckm", imag_z, cos_two, precision=PRECISE) - jnp.einsum(
        "ckb,mb->ckm", real_z, sin_two, precision=PRECISE
    )
    return (real_x, imag_x)


def inverse_signal(real_x, imag_x, tables):
    cos_one, sin_one = tables[1]
    cos_tw, sin_tw = tables[2]
    cos_two, sin_two = tables[3]
    channels = real_x.shape[0]
    half_a = cos_one.shape[0]
    block_b = cos_two.shape[0]
    total_n = cos_one.shape[1] * block_b
    real_p = jnp.einsum("ckm,mb->ckb", real_x, cos_two, precision=PRECISE) - jnp.einsum(
        "ckm,mb->ckb", imag_x, sin_two, precision=PRECISE
    )
    imag_p = jnp.einsum("ckm,mb->ckb", real_x, sin_two, precision=PRECISE) + jnp.einsum(
        "ckm,mb->ckb", imag_x, cos_two, precision=PRECISE
    )
    real_q = real_p * cos_tw - imag_p * sin_tw
    imag_q = real_p * sin_tw + imag_p * cos_tw
    summed = jnp.einsum("ak,ckb->cab", cos_one, real_q, precision=PRECISE) - jnp.einsum(
        "ak,ckb->cab", sin_one, imag_q, precision=PRECISE
    )
    return summed.reshape(channels, half_a * block_b) / total_n


def times_conj(real_a, imag_a, real_b, imag_b):
    return (real_a * real_b + imag_a * imag_b, real_a * imag_b - imag_a * real_b)


def features(padded, weights, length):
    summed = jnp.zeros((3, padded.shape[0], length), jnp.float32)
    for offset in range(7):
        window = padded[:, 6 - offset : 6 - offset + length].astype(jnp.float32)
        summed = summed + weights[:, offset, :, None] * window[None]
    return summed.astype(jnp.bfloat16)


def transposed(grad_all, weights):
    length = grad_all.shape[2]
    padded = jnp.pad(grad_all, ((0, 0), (0, 0), (0, 6)))
    summed = jnp.zeros(grad_all.shape[1:], jnp.float32)
    for offset in range(7):
        summed = summed + jnp.sum(
            weights[:, offset, :, None] * padded[:, :, offset : offset + length], axis=0
        )
    return summed


def tap_grads(padded, grad_all):
    length = grad_all.shape[2]
    per_offset = []
    for offset in range(7):
        window = padded[:, 6 - offset : 6 - offset + length].astype(jnp.float32)
        per_offset.append(jnp.sum(grad_all * window[None], axis=2))
    return jnp.stack(per_offset, axis=1)


def take_rows(array, first_ch, count, axis_num):
    return lax.dynamic_slice_in_dim(array, first_ch, count, axis_num)


def masked_write(array, update, first_ch, active, axis_num):
    previous = lax.dynamic_slice_in_dim(array, first_ch, update.shape[axis_num], axis_num)
    return lax.dynamic_update_slice_in_dim(
        array, jnp.where(active, update, previous), first_ch, axis_num
    )


def shards(inputs, out_grad, filters, conv_taps):
    x_rows = inputs[0]
    tok_dev = x_rows.shape[1]
    section_count = lax.axis_size("section")
    section_idx = lax.axis_index("section")
    ctx_idx = lax.axis_index("ctx")
    weights = conv_taps[0]
    channels = filters.shape[1]
    length = filters.shape[2]
    blocks_a = 2 * length // tok_dev
    own_taps = lax.dynamic_slice_in_dim(weights, ctx_idx * channels, channels, 2)
    prior_cols = shifted(x_rows[:, tok_dev - 6 :], "ctx", 1)
    featured_rows = features(jnp.concatenate([prior_cols, x_rows], axis=1), weights, tok_dev)
    x_chan, featured, grad_chan = (
        lax.all_to_all(x_rows[None], "ctx", split_axis=1, concat_axis=2, tiled=True),
        lax.all_to_all(featured_rows, "ctx", split_axis=1, concat_axis=2, tiled=True),
        lax.all_to_all(out_grad[None], "ctx", split_axis=1, concat_axis=2, tiled=True),
    )
    x_chan = x_chan[0]
    x_padded = jnp.pad(x_chan, ((0, 0), (6, 0)))
    grad_chan = grad_chan[0]
    tables = make_tables(blocks_a, tok_dev)
    key_full = featured[1].astype(jnp.float32)
    mixed_kv = key_full * featured[2].astype(jnp.float32)
    real_h, imag_h = forward_spectrum(filters[0].astype(jnp.float32), tables)
    real_w, imag_w = forward_spectrum(mixed_kv, tables)
    convolved = inverse_signal(
        real_h * real_w - imag_h * imag_w, real_h * imag_w + imag_h * real_w, tables
    )
    block_ch = 2
    block_count = channels // block_ch
    last_section = section_count - 1
    turns = block_count + section_count - 1
    dx_init = jnp.zeros((channels, length), jnp.bfloat16)

    def advance(turn_idx, carried):
        incoming, dz_all, dx_store, tap_acc = carried
        block_id = turn_idx - (last_section - section_idx)
        active = (block_id >= 0) & (block_id < block_count)
        first_ch = jnp.clip(block_id, 0, block_count - 1) * block_ch
        from_next = take_rows(grad_chan, first_ch, block_ch, 0)
        grad_in = jnp.where(section_idx == last_section, from_next, incoming).astype(jnp.float32)
        feat_blk = take_rows(featured, first_ch, block_ch, 1).astype(jnp.float32)
        grad_z = grad_in * feat_blk[0]
        grad_q = grad_in * take_rows(convolved, first_ch, block_ch, 0)
        real_d, imag_d = forward_spectrum(grad_z, tables)
        real_c, imag_c = times_conj(
            take_rows(real_h, first_ch, block_ch, 0),
            take_rows(imag_h, first_ch, block_ch, 0),
            real_d,
            imag_d,
        )
        grad_w = inverse_signal(real_c, imag_c, tables)
        grad_all = jnp.stack([grad_q, grad_w * feat_blk[2], grad_w * feat_blk[1]])
        in_blk = transposed(grad_all, take_rows(own_taps, first_ch, block_ch, 2)).astype(
            jnp.bfloat16
        )
        tap_new = tap_grads(take_rows(x_padded, first_ch, block_ch, 0), grad_all)
        tap_acc = masked_write(tap_acc, tap_new, first_ch, active, 2)
        dz_all = masked_write(dz_all, grad_z, first_ch, active, 0)
        outgoing = shifted(in_blk, "section", -1)
        dx_store = masked_write(dx_store, in_blk, first_ch, active, 0)
        return (outgoing, dz_all, dx_store, tap_acc)

    start_state = (
        jnp.zeros((block_ch, length), jnp.bfloat16),
        jnp.zeros((channels, length), jnp.float32),
        dx_init,
        jnp.zeros((3, 7, channels), jnp.float32),
    )
    final_state = lax.fori_loop(0, turns, advance, start_state)
    dz_all = final_state[1]
    dx_store = final_state[2]
    tap_acc = final_state[3]
    real_d, imag_d = forward_spectrum(dz_all, tables)
    real_c, imag_c = times_conj(real_w, imag_w, real_d, imag_d)
    filter_grad = inverse_signal(real_c, imag_c, tables)
    in_rows = lax.all_to_all(dx_store, "ctx", split_axis=1, concat_axis=0, tiled=True)
    return (in_rows[None], filter_grad[None], tap_acc[None])


TAPS = 7
GROUP = 16
MESH = pl.DeviceIdType.MESH
F32 = jnp.float32
BF16 = jnp.bfloat16


def right_angle_tables(blocks_a, block_b):
    total_n = blocks_a * block_b
    first_k = np.arange(blocks_a)
    phase_one = 2 * np.pi * np.outer(first_k + 0.25, np.arange(blocks_a)) / blocks_a
    one = np.stack([np.cos(phase_one), -np.sin(phase_one)])
    first = np.einsum("rka,cd->rkcad", one, np.eye(GROUP))
    first = first.reshape(2 * blocks_a * GROUP, blocks_a * GROUP)
    points = first_k[:, None, None] + 0.25 + blocks_a * np.arange(block_b)[None, None, :]
    phase_two = 2 * np.pi * np.arange(block_b)[None, :, None] * points / total_n
    real, imag = np.cos(phase_two), -np.sin(phase_two)
    second = np.concatenate(
        [np.concatenate([real, imag], axis=2), np.concatenate([-imag, real], axis=2)], axis=1
    )
    return tuple(
        array.astype(ml_dtypes.bfloat16)
        for array in (first, first.T / total_n, second, second.transpose(0, 2, 1))
    )


def mixer_kernel(
    sections,
    x_ref,
    og_ref,
    filt_ref,
    tap_ref,
    one_ref,
    one_inv_ref,
    two_ref,
    two_inv_ref,
    ig_out,
    fg_out,
    tg_out,
    xbuf,
    ogbuf,
    hbuf,
    tap_blk,
    tap_rows,
    tbuf,
    one_v,
    one_inv_v,
    two_v,
    two_inv_v,
    tapb,
    xs_ref,
    feat,
    sig,
    ybuf,
    spec,
    qbuf,
    cbuf,
    gwbuf,
    gbuf,
    igbuf,
    fgbuf,
    tgbuf,
    tgin,
    x_send,
    x_recv,
    og_send,
    og_recv,
    h_send,
    h_recv,
    t_send,
    t_recv,
    ig_send,
    ig_recv,
    fg_send,
    fg_recv,
    tg_send,
    tg_recv,
    table_sem,
    blk_sem,
):
    sec = lax.axis_index("section")
    ctx = lax.axis_index("ctx")
    blocks = xbuf.shape[1]
    rows = xbuf.shape[2]
    lanes = xbuf.shape[3]
    groups = rows // GROUP
    other = 1 - sec

    tables = [
        pltpu.make_async_copy(src, dst, table_sem.at[n])
        for n, (src, dst) in enumerate(
            ((one_ref, one_v), (two_ref, two_v), (one_inv_ref, one_inv_v), (two_inv_ref, two_inv_v))
        )
    ]

    channels = sections * rows
    tap_first = ctx * channels
    tap_lane = pl.multiple_of(tap_first // lanes * lanes, lanes)
    tap_load = pltpu.make_async_copy(tap_ref.at[:, :, pl.ds(tap_lane, lanes)], tap_blk, blk_sem)
    tap_load.start()

    barrier = pltpu.get_barrier_semaphore()

    def greet(step, carry):
        to_ctx = lax.rem(ctx + step, blocks)
        pl.semaphore_signal(barrier, inc=1, device_id=(other, to_ctx), device_id_type=MESH)

        @pl.when(step > 0)
        def _():
            pl.semaphore_signal(barrier, inc=1, device_id=(sec, to_ctx), device_id_type=MESH)

        return carry

    lax.fori_loop(0, blocks, greet, 0)
    for table in tables:
        table.start()
    pl.semaphore_wait(barrier, sections * blocks - 1)

    def row_block(to_sec, to_ctx):
        return pl.ds(pl.multiple_of((to_ctx * sections + to_sec) * rows, rows), rows)

    def half(which):
        return pl.ds(pl.multiple_of(which * rows, rows), rows)

    def remote(src, dst, send_sem, recv_sem, to_sec, to_ctx):
        pltpu.make_async_remote_copy(
            src_ref=src,
            dst_ref=dst,
            send_sem=send_sem,
            recv_sem=recv_sem,
            device_id=(to_sec, to_ctx),
            device_id_type=MESH,
        ).start()

    def await_bytes(ref, sem):
        pltpu.make_async_copy(ref, ref, sem).wait()

    remote(filt_ref.at[half(other)], hbuf.at[sec], h_send, h_recv, other, ctx)
    pltpu.make_async_copy(filt_ref.at[half(sec)], hbuf.at[sec], h_recv).start()

    def send_x(to_sec):
        def send(step, carry):
            to_ctx = lax.rem(ctx + step, blocks)
            src = x_ref.at[row_block(to_sec, to_ctx)]
            remote(src, xbuf.at[sec, ctx], x_send, x_recv.at[sec], to_sec, to_ctx)
            return carry

        return send

    pltpu.make_async_copy(
        x_ref.at[row_block(sec, ctx)], xbuf.at[sec, ctx], x_recv.at[sec]
    ).start()
    lax.fori_loop(1, blocks, send_x(sec), 0)
    lax.fori_loop(0, blocks, send_x(other), 0)

    def send_og(step, carry):
        to_ctx = lax.rem(ctx + step, blocks)
        remote(og_ref.at[row_block(sec, to_ctx)], ogbuf.at[ctx], og_send, og_recv, sec, to_ctx)
        return carry

    pltpu.make_async_copy(og_ref.at[row_block(sec, ctx)], ogbuf.at[ctx], og_recv).start()
    lax.fori_loop(1, blocks, send_og, 0)

    tap_load.wait()
    tap_rows[...] = jnp.zeros_like(tap_rows)
    tap_rows[pl.ds(0, 3 * TAPS)] = tap_blk[...].reshape(3 * TAPS, lanes)
    tap_rows[...] = tap_rows[...].T

    def tap_half(which):
        first = lax.rem(tap_first, lanes) + which * rows
        return tap_rows.at[pl.ds(pl.multiple_of(first, rows), rows)]

    remote(tap_half(other), tbuf.at[sec], t_send, t_recv, other, ctx)
    pltpu.make_async_copy(tap_half(sec), tbuf.at[sec], t_recv).start()

    def stage_one(blocks_of, first_row):
        cols = jnp.concatenate(
            [blocks_of(g).reshape(blocks * GROUP, lanes) for g in range(groups)], axis=1
        )
        out = jnp.dot(one_v[...], cols, preferred_element_type=F32).astype(BF16)
        out = out.reshape(2, blocks, GROUP, groups * lanes)
        for g in range(groups):
            for part in range(2):
                ybuf[:, pl.ds(first_row + g * GROUP, GROUP), pl.ds(part * lanes, lanes)] = out[
                    part, :, :, g * lanes : (g + 1) * lanes
                ]

    def stage_two(k, first_row, count):
        return jnp.dot(ybuf[k, pl.ds(first_row, count)], two_v[k], preferred_element_type=F32)

    def each_point(body):
        def step(k, carry):
            body(k)
            return carry

        lax.fori_loop(0, blocks, step, 0, unroll=True)

    def product(left, right, conj):
        left_r, left_i = left[:, :lanes], left[:, lanes:]
        right_r, right_i = right[:, :lanes], right[:, lanes:]
        if conj:
            real = left_r * right_r + left_i * right_i
            imag = left_r * right_i - left_i * right_r
        else:
            real = left_r * right_r - left_i * right_i
            imag = left_r * right_i + left_i * right_r
        return jnp.concatenate([real, imag], axis=1).astype(BF16)

    def inverse_two(k, operand, slots):
        out = jnp.dot(operand, two_inv_v[k], preferred_element_type=F32).astype(BF16)
        for slot in range(slots):
            for g in range(groups):
                first = (slot * groups + g) * GROUP
                for part in range(2):
                    qbuf[slot, part, k, :, pl.ds(g * lanes, lanes)] = out[
                        first : first + GROUP, part * lanes : (part + 1) * lanes
                    ]

    def inverse_one(slot):
        out = jnp.dot(
            one_inv_v[...],
            qbuf[slot].reshape(2 * blocks * GROUP, groups * lanes),
            preferred_element_type=F32,
        )
        return out.reshape(blocks, GROUP, groups * lanes)

    tables[0].wait()
    tables[1].wait()
    await_bytes(hbuf, h_recv)
    for layer in range(sections):
        stage_one(
            lambda g: jnp.stack(
                [
                    hbuf[layer, pl.ds(g * GROUP, GROUP), pl.ds(a * lanes, lanes)]
                    for a in range(blocks)
                ]
            ),
            layer * rows,
        )

    def filter_point(k):
        spec[k, pl.ds(0, channels)] = stage_two(k, 0, channels)

    each_point(filter_point)

    await_bytes(tbuf, t_recv)
    for layer in range(sections):
        values = tbuf[layer]
        for n in range(3 * TAPS):
            tapb[layer, n] = jnp.broadcast_to(values[:, n : n + 1], (rows, lanes))

    lane = lax.broadcasted_iota(jnp.int32, (rows, lanes), 1)

    def features_of(layer):
        def body(a, before):
            window = xbuf[layer, a].astype(F32)
            sums = [None] * 3
            rolled = []
            for j in range(TAPS):
                if j == 0:
                    moved = window
                else:
                    turned = pltpu.roll(window, j, 1)
                    rolled.append(turned)
                    moved = jnp.where(lane < j, before[j - 1], turned)
                xs_ref[layer, j, a] = moved
                for i in range(3):
                    term = tapb[layer, i * TAPS + j] * moved
                    sums[i] = term if sums[i] is None else sums[i] + term
            rounded = [total.astype(BF16) for total in sums]
            for i in range(3):
                feat[layer, i, a] = rounded[i]
            sig[a] = (rounded[1].astype(F32) * rounded[2].astype(F32)).astype(BF16)
            return tuple(rolled)

        zero = jnp.zeros((rows, lanes), F32)
        lax.fori_loop(0, blocks, body, (zero,) * (TAPS - 1), unroll=2)

    mixed_row = sections * rows
    for layer in range(sections - 1, -1, -1):
        await_bytes(xbuf.at[layer], x_recv.at[layer])
        features_of(layer)
        stage_one(lambda g: sig[:, pl.ds(g * GROUP, GROUP), :], mixed_row + layer * rows)
    tables[2].wait()
    tables[3].wait()

    def mixed_point(k):
        mixed = stage_two(k, mixed_row, channels)
        spec[k, pl.ds(mixed_row, channels)] = mixed
        inverse_two(k, product(spec[k, pl.ds(0, channels)], mixed, False), sections)

    each_point(mixed_point)
    for layer in range(sections):
        out = inverse_one(layer)
        for g in range(groups):
            cbuf[layer, :, pl.ds(g * GROUP, GROUP), :] = out[:, :, g * lanes : (g + 1) * lanes]

    def send_home(layer, src, dst, send_sem, recv_sem):
        @pl.when(sec == layer)
        def _():
            pltpu.make_async_copy(src, dst, recv_sem).start()

        @pl.when(sec != layer)
        def _():
            remote(src, dst, send_sem, recv_sem, layer, ctx)

    for layer in range(sections - 1, -1, -1):
        if layer == sections - 1:
            await_bytes(ogbuf, og_recv)
            carried = ogbuf
        else:
            carried = igbuf.at[layer + 1]

        sig[...] = (carried[...].astype(F32) * feat[layer, 0].astype(F32)).astype(BF16)
        stage_one(lambda g: sig[:, pl.ds(g * GROUP, GROUP), :], 0)

        def grad_point(k):
            d_spec = stage_two(k, 0, rows)
            with_h = product(spec[k, pl.ds(layer * rows, rows)], d_spec, True)
            with_w = product(spec[k, pl.ds(mixed_row + layer * rows, rows)], d_spec, True)
            inverse_two(k, jnp.concatenate([with_h, with_w], axis=0), 2)

        each_point(grad_point)
        out = inverse_one(0)
        for g in range(groups):
            gwbuf[:, pl.ds(g * GROUP, GROUP), :] = out[:, :, g * lanes : (g + 1) * lanes]

        def transposed_at(step, after):
            a = blocks - 1 - step
            grad_w = gwbuf[a]
            grads = (
                carried[a].astype(F32) * cbuf[layer, a],
                grad_w * feat[layer, 2, a].astype(F32),
                grad_w * feat[layer, 1, a].astype(F32),
            )
            for i in range(3):
                gbuf[layer, i, a] = grads[i]
            total = None
            rolled = []
            for j in range(TAPS):
                part = tapb[layer, j] * grads[0]
                for i in range(1, 3):
                    part = part + tapb[layer, i * TAPS + j] * grads[i]
                if j == 0:
                    total = part
                else:
                    turned = pltpu.roll(part, lanes - j, 1)
                    rolled.append(turned)
                    total = total + jnp.where(lane < lanes - j, turned, after[j - 1])
            igbuf[layer, a] = total.astype(BF16)
            return tuple(rolled)

        zero = jnp.zeros((rows, lanes), F32)
        lax.fori_loop(0, blocks, transposed_at, (zero,) * (TAPS - 1), unroll=2)

        def send_ig(step, carry):
            to_ctx = lax.rem(ctx + step, blocks)
            src = igbuf.at[layer, to_ctx]
            dst = ig_out.at[row_block(sec, ctx)]
            local = (sec == layer) & (step == 0)

            @pl.when(local)
            def _():
                pltpu.make_async_copy(src, dst, ig_recv).start()

            @pl.when(jnp.logical_not(local))
            def _():
                remote(src, dst, ig_send, ig_recv, layer, to_ctx)

            return carry

        lax.fori_loop(0, blocks, send_ig, 0)

        out = inverse_one(1)
        for a in range(blocks):
            for g in range(groups):
                fgbuf[layer, pl.ds(g * GROUP, GROUP), pl.ds(a * lanes, lanes)] = out[
                    a, :, g * lanes : (g + 1) * lanes
                ].astype(BF16)

        send_home(layer, fgbuf.at[layer], fg_out.at[half(sec)], fg_send, fg_recv)

    for layer in range(sections - 1, -1, -1):
        for first in range(0, rows, 8):
            def add_taps(a, sums):
                grads = [gbuf[layer, i, a, pl.ds(first, 8)] for i in range(3)]
                new = []
                for j in range(TAPS):
                    moved = xs_ref[layer, j, a, pl.ds(first, 8)]
                    for i in range(3):
                        new.append(sums[j * 3 + i] + grads[i] * moved)
                return tuple(new)

            zero_8 = jnp.zeros((8, lanes), F32)
            sums = lax.fori_loop(0, blocks, add_taps, (zero_8,) * (3 * TAPS), unroll=4)
            lane_8 = lax.broadcasted_iota(jnp.int32, (8, lanes), 1)
            packed = zero_8
            for j in range(TAPS):
                for i in range(3):
                    column = jnp.sum(sums[j * 3 + i], axis=1, keepdims=True)
                    packed = jnp.where(lane_8 == i * TAPS + j, column, packed)
            tgbuf[layer, pl.ds(first, 8)] = packed
        send_home(layer, tgbuf.at[layer], tgin.at[half(sec)], tg_send, tg_recv)

    others = sections * blocks - 1
    await_bytes(x_ref.at[pl.ds(0, others * rows)], x_send)
    await_bytes(og_ref.at[pl.ds(0, (blocks - 1) * rows)], og_send)
    await_bytes(filt_ref.at[pl.ds(0, rows)], h_send)
    await_bytes(tbuf.at[0], t_send)
    await_bytes(ig_out.at[pl.ds(0, others * rows)], ig_send)
    await_bytes(fg_out.at[pl.ds(0, rows)], fg_send)
    await_bytes(tgbuf.at[0], tg_send)
    await_bytes(tgin, tg_recv)
    tg_out[...] = tgin[...].T[: 3 * TAPS].reshape(3 * TAPS, 1, channels)
    await_bytes(fg_out, fg_recv)
    await_bytes(ig_out, ig_recv)


def kernel_shards(inputs, out_grad, filters, conv_taps):
    sections = lax.axis_size("section")
    blocks = lax.axis_size("ctx")
    _, depth, lanes = inputs.shape
    _, channels, length = filters.shape
    rows = channels // sections
    tables = right_angle_tables(blocks, lanes)
    taps = conv_taps.reshape(3 * TAPS, 1, depth)
    vmem = pltpu.VMEM
    dma = pltpu.SemaphoreType.DMA
    any_spec = pl.BlockSpec(memory_space=pl.ANY)
    hbm_spec = pl.BlockSpec(memory_space=pl.ANY)
    vmem_spec = pl.BlockSpec(memory_space=pltpu.VMEM)
    spectrum_rows = 2 * sections * rows
    in_grad, filter_grad, tap_sums = pl.pallas_call(
        functools.partial(mixer_kernel, sections),
        out_shape=(
            jax.ShapeDtypeStruct((depth, lanes), BF16),
            jax.ShapeDtypeStruct((channels, length), BF16),
            jax.ShapeDtypeStruct((3 * TAPS, 1, channels), F32),
        ),
        in_specs=[hbm_spec] * 8,
        out_specs=(any_spec, any_spec, vmem_spec),
        scratch_shapes=[
            vmem((sections, blocks, rows, lanes), BF16),
            vmem((blocks, rows, lanes), BF16),
            vmem((sections, rows, length), BF16),
            vmem((3 * TAPS, 1, lanes), F32),
            vmem((lanes, lanes), F32),
            vmem((sections, rows, lanes), F32),
            vmem(tables[0].shape, BF16),
            vmem(tables[1].shape, BF16),
            vmem(tables[2].shape, BF16),
            vmem(tables[3].shape, BF16),
            vmem((sections, 3 * TAPS, rows, lanes), F32),
            vmem((sections, TAPS, blocks, rows, lanes), F32),
            vmem((sections, 3, blocks, rows, lanes), BF16),
            vmem((blocks, rows, lanes), BF16),
            vmem((blocks, spectrum_rows, 2 * lanes), BF16),
            vmem((blocks, spectrum_rows, 2 * lanes), F32),
            vmem((2, 2, blocks, GROUP, rows // GROUP * lanes), BF16),
            vmem((sections, blocks, rows, lanes), F32),
            vmem((blocks, rows, lanes), F32),
            vmem((sections, 3, blocks, rows, lanes), F32),
            vmem((sections, blocks, rows, lanes), BF16),
            vmem((sections, rows, length), BF16),
            vmem((sections, rows, lanes), F32),
            vmem((channels, lanes), F32),
            dma(()),
            dma((sections,)),
            dma(()),
            dma(()),
            dma(()),
            dma(()),
            dma(()),
            dma(()),
            dma(()),
            dma(()),
            dma(()),
            dma(()),
            dma(()),
            dma(()),
            dma((4,)),
            dma(()),
        ],
        compiler_params=pltpu.CompilerParams(
            collective_id=0, has_side_effects=True, vmem_limit_bytes=58 * 2**20
        ),
    )(inputs[0], out_grad, filters[0], taps, *(jnp.asarray(table) for table in tables))
    tap_grad = tap_sums.reshape(1, 3, TAPS, channels)
    return (in_grad[None], filter_grad.astype(F32)[None], tap_grad)


def solution(mesh):
    placed = (
        P("section", None, "ctx"),
        P(None, "ctx"),
        P("section", "ctx", None),
        P("section", None, None, None),
    )

    def run(inputs, out_grad, filters, conv_taps):
        sections, blocks = mesh.shape["section"], mesh.shape["ctx"]
        rows = filters.shape[1] // (sections * blocks)
        lanes = inputs.shape[2] // blocks
        fits = sections == 2 and rows % GROUP == 0 and lanes == 128 and lanes % (sections * rows) == 0
        return jax.shard_map(
            kernel_shards if fits else shards,
            mesh=mesh,
            in_specs=placed,
            out_specs=(
                P("section", None, "ctx"),
                P("section", "ctx", None),
                P("section", None, None, "ctx"),
            ),
            check_vma=False,
        )(inputs, out_grad, filters, conv_taps)

    return run
```

```python
import functools
import math

import jax
import jax.numpy as jnp
import ml_dtypes
import numpy as np
from jax import lax
from jax.experimental import pallas as pl
from jax.experimental.pallas import tpu as pltpu
from jax.sharding import PartitionSpec as P

PRECISE = lax.Precision.HIGH


def shifted(block, axis, distance):
    devices = range(lax.axis_size(axis))
    route = [(i - distance, i) for i in devices if i - distance in devices]
    return lax.ppermute(block, axis, route)


def angle_table(row_count, col_count, modulus):
    row_ids = lax.broadcasted_iota(jnp.int32, (row_count, col_count), 0)
    col_ids = lax.broadcasted_iota(jnp.int32, (row_count, col_count), 1)
    product_mod = row_ids * col_ids % modulus
    angles = product_mod.astype(jnp.float32) * (2.0 * math.pi / modulus)
    return (jnp.cos(angles), jnp.sin(angles))


def make_tables(blocks_a, block_b):
    half_a = blocks_a // 2
    total_n = blocks_a * block_b
    return (
        angle_table(blocks_a, half_a, blocks_a),
        angle_table(half_a, blocks_a, blocks_a),
        angle_table(blocks_a, block_b, total_n),
        angle_table(block_b, block_b, block_b),
    )


def forward_spectrum(signal, tables):
    cos_one, sin_one = tables[0]
    cos_tw, sin_tw = tables[2]
    cos_two, sin_two = tables[3]
    channels = signal.shape[0]
    half_a = cos_one.shape[1]
    block_b = cos_two.shape[0]
    shaped = signal.reshape(channels, half_a, block_b)
    real_y = jnp.einsum("ka,cab->ckb", cos_one, shaped, precision=PRECISE)
    imag_y = -jnp.einsum("ka,cab->ckb", sin_one, shaped, precision=PRECISE)
    real_z = real_y * cos_tw + imag_y * sin_tw
    imag_z = imag_y * cos_tw - real_y * sin_tw
    real_x = jnp.einsum("ckb,mb->ckm", real_z, cos_two, precision=PRECISE) + jnp.einsum(
        "ckb,mb->ckm", imag_z, sin_two, precision=PRECISE
    )
    imag_x = jnp.einsum("ckb,mb->ckm", imag_z, cos_two, precision=PRECISE) - jnp.einsum(
        "ckb,mb->ckm", real_z, sin_two, precision=PRECISE
    )
    return (real_x, imag_x)


def inverse_signal(real_x, imag_x, tables):
    cos_one, sin_one = tables[1]
    cos_tw, sin_tw = tables[2]
    cos_two, sin_two = tables[3]
    channels = real_x.shape[0]
    half_a = cos_one.shape[0]
    block_b = cos_two.shape[0]
    total_n = cos_one.shape[1] * block_b
    real_p = jnp.einsum("ckm,mb->ckb", real_x, cos_two, precision=PRECISE) - jnp.einsum(
        "ckm,mb->ckb", imag_x, sin_two, precision=PRECISE
    )
    imag_p = jnp.einsum("ckm,mb->ckb", real_x, sin_two, precision=PRECISE) + jnp.einsum(
        "ckm,mb->ckb", imag_x, cos_two, precision=PRECISE
    )
    real_q = real_p * cos_tw - imag_p * sin_tw
    imag_q = real_p * sin_tw + imag_p * cos_tw
    summed = jnp.einsum("ak,ckb->cab", cos_one, real_q, precision=PRECISE) - jnp.einsum(
        "ak,ckb->cab", sin_one, imag_q, precision=PRECISE
    )
    return summed.reshape(channels, half_a * block_b) / total_n


def times_conj(real_a, imag_a, real_b, imag_b):
    return (real_a * real_b + imag_a * imag_b, real_a * imag_b - imag_a * real_b)


def features(padded, weights, length):
    summed = jnp.zeros((3, padded.shape[0], length), jnp.float32)
    for offset in range(7):
        window = padded[:, 6 - offset : 6 - offset + length].astype(jnp.float32)
        summed = summed + weights[:, offset, :, None] * window[None]
    return summed.astype(jnp.bfloat16)


def transposed(grad_all, weights):
    length = grad_all.shape[2]
    padded = jnp.pad(grad_all, ((0, 0), (0, 0), (0, 6)))
    summed = jnp.zeros(grad_all.shape[1:], jnp.float32)
    for offset in range(7):
        summed = summed + jnp.sum(
            weights[:, offset, :, None] * padded[:, :, offset : offset + length], axis=0
        )
    return summed


def tap_grads(padded, grad_all):
    length = grad_all.shape[2]
    per_offset = []
    for offset in range(7):
        window = padded[:, 6 - offset : 6 - offset + length].astype(jnp.float32)
        per_offset.append(jnp.sum(grad_all * window[None], axis=2))
    return jnp.stack(per_offset, axis=1)


def take_rows(array, first_ch, count, axis_num):
    return lax.dynamic_slice_in_dim(array, first_ch, count, axis_num)


def masked_write(array, update, first_ch, active, axis_num):
    previous = lax.dynamic_slice_in_dim(array, first_ch, update.shape[axis_num], axis_num)
    return lax.dynamic_update_slice_in_dim(
        array, jnp.where(active, update, previous), first_ch, axis_num
    )


def shards(inputs, out_grad, filters, conv_taps):
    x_rows = inputs[0]
    tok_dev = x_rows.shape[1]
    section_count = lax.axis_size("section")
    section_idx = lax.axis_index("section")
    ctx_idx = lax.axis_index("ctx")
    weights = conv_taps[0]
    channels = filters.shape[1]
    length = filters.shape[2]
    blocks_a = 2 * length // tok_dev
    own_taps = lax.dynamic_slice_in_dim(weights, ctx_idx * channels, channels, 2)
    prior_cols = shifted(x_rows[:, tok_dev - 6 :], "ctx", 1)
    featured_rows = features(jnp.concatenate([prior_cols, x_rows], axis=1), weights, tok_dev)
    x_chan, featured, grad_chan = (
        lax.all_to_all(x_rows[None], "ctx", split_axis=1, concat_axis=2, tiled=True),
        lax.all_to_all(featured_rows, "ctx", split_axis=1, concat_axis=2, tiled=True),
        lax.all_to_all(out_grad[None], "ctx", split_axis=1, concat_axis=2, tiled=True),
    )
    x_chan = x_chan[0]
    x_padded = jnp.pad(x_chan, ((0, 0), (6, 0)))
    grad_chan = grad_chan[0]
    tables = make_tables(blocks_a, tok_dev)
    key_full = featured[1].astype(jnp.float32)
    mixed_kv = key_full * featured[2].astype(jnp.float32)
    real_h, imag_h = forward_spectrum(filters[0].astype(jnp.float32), tables)
    real_w, imag_w = forward_spectrum(mixed_kv, tables)
    convolved = inverse_signal(
        real_h * real_w - imag_h * imag_w, real_h * imag_w + imag_h * real_w, tables
    )
    block_ch = 2
    block_count = channels // block_ch
    last_section = section_count - 1
    turns = block_count + section_count - 1
    dx_init = jnp.zeros((channels, length), jnp.bfloat16)

    def advance(turn_idx, carried):
        incoming, dz_all, dx_store, tap_acc = carried
        block_id = turn_idx - (last_section - section_idx)
        active = (block_id >= 0) & (block_id < block_count)
        first_ch = jnp.clip(block_id, 0, block_count - 1) * block_ch
        from_next = take_rows(grad_chan, first_ch, block_ch, 0)
        grad_in = jnp.where(section_idx == last_section, from_next, incoming).astype(jnp.float32)
        feat_blk = take_rows(featured, first_ch, block_ch, 1).astype(jnp.float32)
        grad_z = grad_in * feat_blk[0]
        grad_q = grad_in * take_rows(convolved, first_ch, block_ch, 0)
        real_d, imag_d = forward_spectrum(grad_z, tables)
        real_c, imag_c = times_conj(
            take_rows(real_h, first_ch, block_ch, 0),
            take_rows(imag_h, first_ch, block_ch, 0),
            real_d,
            imag_d,
        )
        grad_w = inverse_signal(real_c, imag_c, tables)
        grad_all = jnp.stack([grad_q, grad_w * feat_blk[2], grad_w * feat_blk[1]])
        in_blk = transposed(grad_all, take_rows(own_taps, first_ch, block_ch, 2)).astype(
            jnp.bfloat16
        )
        tap_new = tap_grads(take_rows(x_padded, first_ch, block_ch, 0), grad_all)
        tap_acc = masked_write(tap_acc, tap_new, first_ch, active, 2)
        dz_all = masked_write(dz_all, grad_z, first_ch, active, 0)
        outgoing = shifted(in_blk, "section", -1)
        dx_store = masked_write(dx_store, in_blk, first_ch, active, 0)
        return (outgoing, dz_all, dx_store, tap_acc)

    start_state = (
        jnp.zeros((block_ch, length), jnp.bfloat16),
        jnp.zeros((channels, length), jnp.float32),
        dx_init,
        jnp.zeros((3, 7, channels), jnp.float32),
    )
    final_state = lax.fori_loop(0, turns, advance, start_state)
    dz_all = final_state[1]
    dx_store = final_state[2]
    tap_acc = final_state[3]
    real_d, imag_d = forward_spectrum(dz_all, tables)
    real_c, imag_c = times_conj(real_w, imag_w, real_d, imag_d)
    filter_grad = inverse_signal(real_c, imag_c, tables)
    in_rows = lax.all_to_all(dx_store, "ctx", split_axis=1, concat_axis=0, tiled=True)
    return (in_rows[None], filter_grad[None], tap_acc[None])


TAPS = 7
GROUP = 16
MESH = pl.DeviceIdType.MESH
F32 = jnp.float32
BF16 = jnp.bfloat16


def right_angle_tables(blocks_a, block_b):
    total_n = blocks_a * block_b
    first_k = np.arange(blocks_a)
    phase_one = 2 * np.pi * np.outer(first_k + 0.25, np.arange(blocks_a)) / blocks_a
    one = np.stack([np.cos(phase_one), -np.sin(phase_one)])
    first = np.einsum("rka,cd->rkcad", one, np.eye(GROUP))
    first = first.reshape(2 * blocks_a * GROUP, blocks_a * GROUP)
    points = first_k[:, None, None] + 0.25 + blocks_a * np.arange(block_b)[None, None, :]
    phase_two = 2 * np.pi * np.arange(block_b)[None, :, None] * points / total_n
    real, imag = np.cos(phase_two), -np.sin(phase_two)
    second = np.concatenate(
        [np.concatenate([real, imag], axis=2), np.concatenate([-imag, real], axis=2)], axis=1
    )
    return tuple(
        array.astype(ml_dtypes.bfloat16)
        for array in (first, first.T / total_n, second, second.transpose(0, 2, 1))
    )


def mixer_kernel(
    sections,
    x_ref,
    og_ref,
    filt_ref,
    tap_ref,
    one_ref,
    one_inv_ref,
    two_ref,
    two_inv_ref,
    ig_out,
    fg_out,
    tg_out,
    xbuf,
    ogbuf,
    hbuf,
    tap_blk,
    tap_rows,
    tbuf,
    one_v,
    one_inv_v,
    two_v,
    two_inv_v,
    tapb,
    xs_ref,
    feat,
    sig,
    ybuf,
    spec,
    qbuf,
    cbuf,
    gwbuf,
    gbuf,
    igbuf,
    fgbuf,
    tgbuf,
    tgin,
    x_send,
    x_recv,
    og_send,
    og_recv,
    h_send,
    h_recv,
    t_send,
    t_recv,
    ig_send,
    ig_recv,
    fg_send,
    fg_recv,
    tg_send,
    tg_recv,
    table_sem,
    blk_sem,
):
    sec = lax.axis_index("section")
    ctx = lax.axis_index("ctx")
    blocks = xbuf.shape[1]
    rows = xbuf.shape[2]
    lanes = xbuf.shape[3]
    groups = rows // GROUP
    other = 1 - sec

    tables = [
        pltpu.make_async_copy(src, dst, table_sem.at[n])
        for n, (src, dst) in enumerate(
            ((one_ref, one_v), (two_ref, two_v), (one_inv_ref, one_inv_v), (two_inv_ref, two_inv_v))
        )
    ]

    channels = sections * rows
    tap_first = ctx * channels
    tap_lane = pl.multiple_of(tap_first // lanes * lanes, lanes)
    tap_load = pltpu.make_async_copy(tap_ref.at[:, :, pl.ds(tap_lane, lanes)], tap_blk, blk_sem)
    tap_load.start()

    barrier = pltpu.get_barrier_semaphore()

    def greet(step, carry):
        to_ctx = lax.rem(ctx + step, blocks)
        pl.semaphore_signal(barrier, inc=1, device_id=(other, to_ctx), device_id_type=MESH)

        @pl.when(step > 0)
        def _():
            pl.semaphore_signal(barrier, inc=1, device_id=(sec, to_ctx), device_id_type=MESH)

        return carry

    lax.fori_loop(0, blocks, greet, 0, unroll=True)
    for table in tables:
        table.start()
    pl.semaphore_wait(barrier, sections * blocks - 1)

    def row_block(to_sec, to_ctx):
        return pl.ds(pl.multiple_of((to_ctx * sections + to_sec) * rows, rows), rows)

    def half(which):
        return pl.ds(pl.multiple_of(which * rows, rows), rows)

    def remote(src, dst, send_sem, recv_sem, to_sec, to_ctx):
        pltpu.make_async_remote_copy(
            src_ref=src,
            dst_ref=dst,
            send_sem=send_sem,
            recv_sem=recv_sem,
            device_id=(to_sec, to_ctx),
            device_id_type=MESH,
        ).start()

    def await_bytes(ref, sem):
        pltpu.make_async_copy(ref, ref, sem).wait()

    remote(filt_ref.at[half(other)], hbuf.at[sec], h_send, h_recv, other, ctx)
    pltpu.make_async_copy(filt_ref.at[half(sec)], hbuf.at[sec], h_recv).start()

    def send_x(to_sec):
        def send(step, carry):
            to_ctx = lax.rem(ctx + step, blocks)
            src = x_ref.at[row_block(to_sec, to_ctx)]
            remote(src, xbuf.at[sec, ctx], x_send, x_recv.at[sec], to_sec, to_ctx)
            return carry

        return send

    pltpu.make_async_copy(
        x_ref.at[row_block(sec, ctx)], xbuf.at[sec, ctx], x_recv.at[sec]
    ).start()
    lax.fori_loop(1, blocks, send_x(sec), 0, unroll=True)
    lax.fori_loop(0, blocks, send_x(other), 0, unroll=True)

    def send_og(step, carry):
        to_ctx = lax.rem(ctx + step, blocks)
        remote(og_ref.at[row_block(sec, to_ctx)], ogbuf.at[ctx], og_send, og_recv, sec, to_ctx)
        return carry

    pltpu.make_async_copy(og_ref.at[row_block(sec, ctx)], ogbuf.at[ctx], og_recv).start()
    lax.fori_loop(1, blocks, send_og, 0, unroll=True)

    tap_load.wait()
    tap_rows[...] = jnp.zeros_like(tap_rows)
    tap_rows[pl.ds(0, 3 * TAPS)] = tap_blk[...].reshape(3 * TAPS, lanes)
    tap_rows[...] = tap_rows[...].T

    def tap_half(which):
        first = lax.rem(tap_first, lanes) + which * rows
        return tap_rows.at[pl.ds(pl.multiple_of(first, rows), rows)]

    remote(tap_half(other), tbuf.at[sec], t_send, t_recv, other, ctx)
    pltpu.make_async_copy(tap_half(sec), tbuf.at[sec], t_recv).start()

    def rows_at(first):
        return pl.ds(first if isinstance(first, int) else pl.multiple_of(first, GROUP), GROUP)

    def stage_one(blocks_of, first_row):
        cols = jnp.concatenate(
            [blocks_of(g).reshape(blocks * GROUP, lanes) for g in range(groups)], axis=1
        )
        out = jnp.dot(one_v[...], cols, preferred_element_type=F32).astype(BF16)
        out = out.reshape(2, blocks, GROUP, groups * lanes)
        for g in range(groups):
            for part in range(2):
                ybuf[:, rows_at(first_row + g * GROUP), pl.ds(part * lanes, lanes)] = out[
                    part, :, :, g * lanes : (g + 1) * lanes
                ]

    def stage_two(k, first_row, count):
        return jnp.dot(ybuf[k, pl.ds(first_row, count)], two_v[k], preferred_element_type=F32)

    def each_point(body):
        def step(k, carry):
            body(k)
            return carry

        lax.fori_loop(0, blocks, step, 0, unroll=True)

    def product(left, right, conj):
        left_r, left_i = left[:, :lanes], left[:, lanes:]
        right_r, right_i = right[:, :lanes], right[:, lanes:]
        if conj:
            real = left_r * right_r + left_i * right_i
            imag = left_r * right_i - left_i * right_r
        else:
            real = left_r * right_r - left_i * right_i
            imag = left_r * right_i + left_i * right_r
        return jnp.concatenate([real, imag], axis=1).astype(BF16)

    def inverse_two(k, operand, slots):
        out = jnp.dot(operand, two_inv_v[k], preferred_element_type=F32).astype(BF16)
        for position, slot in enumerate(slots):
            for g in range(groups):
                first = (position * groups + g) * GROUP
                for part in range(2):
                    qbuf[slot, part, k, :, pl.ds(g * lanes, lanes)] = out[
                        first : first + GROUP, part * lanes : (part + 1) * lanes
                    ]

    def inverse_one(slot):
        out = jnp.dot(
            one_inv_v[...],
            qbuf[slot].reshape(2 * blocks * GROUP, groups * lanes),
            preferred_element_type=F32,
        )
        return out.reshape(blocks, GROUP, groups * lanes)

    tables[0].wait()
    tables[1].wait()
    await_bytes(hbuf, h_recv)
    for layer in range(sections):
        stage_one(
            lambda g: jnp.stack(
                [
                    hbuf[layer, pl.ds(g * GROUP, GROUP), pl.ds(a * lanes, lanes)]
                    for a in range(blocks)
                ]
            ),
            layer * rows,
        )

    def filter_point(k):
        spec[k, pl.ds(0, channels)] = stage_two(k, 0, channels)

    each_point(filter_point)

    await_bytes(tbuf, t_recv)
    for layer in range(sections):
        values = tbuf[layer]
        for n in range(3 * TAPS):
            tapb[layer, n] = jnp.broadcast_to(values[:, n : n + 1], (rows, lanes))

    lane = lax.broadcasted_iota(jnp.int32, (rows, lanes), 1)

    def features_of(layer):
        def body(a, before):
            window = xbuf[layer, a].astype(F32)
            sums = [None] * 3
            rolled = []
            for j in range(TAPS):
                if j == 0:
                    moved = window
                else:
                    turned = pltpu.roll(window, j, 1)
                    rolled.append(turned)
                    moved = jnp.where(lane < j, before[j - 1], turned)
                xs_ref[layer, j, a] = moved
                for i in range(3):
                    term = tapb[layer, i * TAPS + j] * moved
                    sums[i] = term if sums[i] is None else sums[i] + term
            rounded = [total.astype(BF16) for total in sums]
            for i in range(3):
                feat[layer, i, a] = rounded[i]
            sig[a] = (rounded[1].astype(F32) * rounded[2].astype(F32)).astype(BF16)
            return tuple(rolled)

        zero = jnp.zeros((rows, lanes), F32)
        lax.fori_loop(0, blocks, body, (zero,) * (TAPS - 1), unroll=2)

    mixed_row = sections * rows
    for layer in (sec, other):
        await_bytes(xbuf.at[layer], x_recv.at[layer])
        features_of(layer)
        first_row = pl.multiple_of(mixed_row + layer * rows, rows)
        stage_one(lambda g: sig[:, pl.ds(g * GROUP, GROUP), :], first_row)
    tables[2].wait()
    tables[3].wait()

    def mixed_point(k):
        mixed = stage_two(k, mixed_row, channels)
        spec[k, pl.ds(mixed_row, channels)] = mixed
        inverse_two(k, product(spec[k, pl.ds(0, channels)], mixed, False), range(sections))

    each_point(mixed_point)
    for layer in range(sections):
        out = inverse_one(layer)
        for g in range(groups):
            cbuf[layer, :, pl.ds(g * GROUP, GROUP), :] = out[:, :, g * lanes : (g + 1) * lanes]

    def send_home(layer, src, dst, send_sem, recv_sem):
        @pl.when(sec == layer)
        def _():
            pltpu.make_async_copy(src, dst, recv_sem).start()

        @pl.when(sec != layer)
        def _():
            remote(src, dst, send_sem, recv_sem, layer, ctx)

    def filter_grad_of(layer):
        out = inverse_one(1 + layer)
        for a in range(blocks):
            for g in range(groups):
                fgbuf[layer, pl.ds(g * GROUP, GROUP), pl.ds(a * lanes, lanes)] = out[
                    a, :, g * lanes : (g + 1) * lanes
                ].astype(BF16)
        send_home(layer, fgbuf.at[layer], fg_out.at[half(sec)], fg_send, fg_recv)

    for layer in range(sections - 1, -1, -1):
        if layer == sections - 1:
            await_bytes(ogbuf, og_recv)
            carried = ogbuf
        else:
            carried = igbuf.at[layer + 1]

        sig[...] = (carried[...].astype(F32) * feat[layer, 0].astype(F32)).astype(BF16)
        stage_one(lambda g: sig[:, pl.ds(g * GROUP, GROUP), :], 0)

        def grad_point(k):
            d_spec = stage_two(k, 0, rows)
            with_h = product(spec[k, pl.ds(layer * rows, rows)], d_spec, True)
            with_w = product(spec[k, pl.ds(mixed_row + layer * rows, rows)], d_spec, True)
            inverse_two(k, jnp.concatenate([with_h, with_w], axis=0), (0, 1 + layer))

        each_point(grad_point)
        if layer == 0:
            filter_grad_of(layer)
        out = inverse_one(0)
        for g in range(groups):
            gwbuf[:, pl.ds(g * GROUP, GROUP), :] = out[:, :, g * lanes : (g + 1) * lanes]

        def transposed_at(step, after):
            a = blocks - 1 - step
            grad_w = gwbuf[a]
            grads = (
                carried[a].astype(F32) * cbuf[layer, a],
                grad_w * feat[layer, 2, a].astype(F32),
                grad_w * feat[layer, 1, a].astype(F32),
            )
            for i in range(3):
                gbuf[layer, i, a] = grads[i]
            total = None
            rolled = []
            for j in range(TAPS):
                part = tapb[layer, j] * grads[0]
                for i in range(1, 3):
                    part = part + tapb[layer, i * TAPS + j] * grads[i]
                if j == 0:
                    total = part
                else:
                    turned = pltpu.roll(part, lanes - j, 1)
                    rolled.append(turned)
                    total = total + jnp.where(lane < lanes - j, turned, after[j - 1])
            igbuf[layer, a] = total.astype(BF16)
            return tuple(rolled)

        zero = jnp.zeros((rows, lanes), F32)
        lax.fori_loop(0, blocks, transposed_at, (zero,) * (TAPS - 1), unroll=2)

        def send_ig(step, carry):
            to_ctx = lax.rem(ctx + step, blocks)
            src = igbuf.at[layer, to_ctx]
            dst = ig_out.at[row_block(sec, ctx)]
            local = (sec == layer) & (step == 0)

            @pl.when(local)
            def _():
                pltpu.make_async_copy(src, dst, ig_recv).start()

            @pl.when(jnp.logical_not(local))
            def _():
                remote(src, dst, ig_send, ig_recv, layer, to_ctx)

            return carry

        lax.fori_loop(0, blocks, send_ig, 0, unroll=4)

        if layer == 0:
            for later in range(1, sections):
                filter_grad_of(later)

    for layer in range(sections - 1, -1, -1):
        for first in range(0, rows, 8):
            def add_taps(a, sums):
                grads = [gbuf[layer, i, a, pl.ds(first, 8)] for i in range(3)]
                new = []
                for j in range(TAPS):
                    moved = xs_ref[layer, j, a, pl.ds(first, 8)]
                    for i in range(3):
                        new.append(sums[j * 3 + i] + grads[i] * moved)
                return tuple(new)

            zero_8 = jnp.zeros((8, lanes), F32)
            sums = lax.fori_loop(0, blocks, add_taps, (zero_8,) * (3 * TAPS), unroll=4)
            lane_8 = lax.broadcasted_iota(jnp.int32, (8, lanes), 1)
            packed = zero_8
            for j in range(TAPS):
                for i in range(3):
                    column = jnp.sum(sums[j * 3 + i], axis=1, keepdims=True)
                    packed = jnp.where(lane_8 == i * TAPS + j, column, packed)
            tgbuf[layer, pl.ds(first, 8)] = packed
        send_home(layer, tgbuf.at[layer], tgin.at[half(sec)], tg_send, tg_recv)

    others = sections * blocks - 1
    await_bytes(x_ref.at[pl.ds(0, others * rows)], x_send)
    await_bytes(og_ref.at[pl.ds(0, (blocks - 1) * rows)], og_send)
    await_bytes(filt_ref.at[pl.ds(0, rows)], h_send)
    await_bytes(tbuf.at[0], t_send)
    await_bytes(ig_out.at[pl.ds(0, others * rows)], ig_send)
    await_bytes(fg_out.at[pl.ds(0, rows)], fg_send)
    await_bytes(tgbuf.at[0], tg_send)
    await_bytes(tgin, tg_recv)
    tg_out[...] = tgin[...].T[: 3 * TAPS].reshape(3 * TAPS, 1, channels)
    await_bytes(fg_out, fg_recv)
    await_bytes(ig_out, ig_recv)


def write_kernel(ig_ref, fg_ref, tg_ref, ig_out, fg_out, tg_out):
    ig_out[...] = ig_ref[...]
    fg_out[...] = fg_ref[...].astype(F32)
    tg_out[...] = tg_ref[...]


def kernel_shards(inputs, out_grad, filters, conv_taps):
    sections = lax.axis_size("section")
    blocks = lax.axis_size("ctx")
    _, depth, lanes = inputs.shape
    _, channels, length = filters.shape
    rows = channels // sections
    tables = right_angle_tables(blocks, lanes)
    taps = conv_taps.reshape(3 * TAPS, 1, depth)
    vmem = pltpu.VMEM
    dma = pltpu.SemaphoreType.DMA
    any_spec = pl.BlockSpec(memory_space=pl.ANY)
    hbm_spec = pl.BlockSpec(memory_space=pl.ANY)
    vmem_spec = pl.BlockSpec(memory_space=pltpu.VMEM)
    spectrum_rows = 2 * sections * rows
    in_grad, filter_grad, tap_sums = pl.pallas_call(
        functools.partial(mixer_kernel, sections),
        out_shape=(
            jax.ShapeDtypeStruct((depth, lanes), BF16),
            jax.ShapeDtypeStruct((channels, length), BF16),
            jax.ShapeDtypeStruct((3 * TAPS, 1, channels), F32),
        ),
        in_specs=[hbm_spec] * 8,
        out_specs=(any_spec, any_spec, vmem_spec),
        scratch_shapes=[
            vmem((sections, blocks, rows, lanes), BF16),
            vmem((blocks, rows, lanes), BF16),
            vmem((sections, rows, length), BF16),
            vmem((3 * TAPS, 1, lanes), F32),
            vmem((lanes, lanes), F32),
            vmem((sections, rows, lanes), F32),
            vmem(tables[0].shape, BF16),
            vmem(tables[1].shape, BF16),
            vmem(tables[2].shape, BF16),
            vmem(tables[3].shape, BF16),
            vmem((sections, 3 * TAPS, rows, lanes), F32),
            vmem((sections, TAPS, blocks, rows, lanes), F32),
            vmem((sections, 3, blocks, rows, lanes), BF16),
            vmem((blocks, rows, lanes), BF16),
            vmem((blocks, spectrum_rows, 2 * lanes), BF16),
            vmem((blocks, spectrum_rows, 2 * lanes), F32),
            vmem((1 + sections, 2, blocks, GROUP, rows // GROUP * lanes), BF16),
            vmem((sections, blocks, rows, lanes), F32),
            vmem((blocks, rows, lanes), F32),
            vmem((sections, 3, blocks, rows, lanes), F32),
            vmem((sections, blocks, rows, lanes), BF16),
            vmem((sections, rows, length), BF16),
            vmem((sections, rows, lanes), F32),
            vmem((channels, lanes), F32),
            dma(()),
            dma((sections,)),
            dma(()),
            dma(()),
            dma(()),
            dma(()),
            dma(()),
            dma(()),
            dma(()),
            dma(()),
            dma(()),
            dma(()),
            dma(()),
            dma(()),
            dma((4,)),
            dma(()),
        ],
        compiler_params=pltpu.CompilerParams(
            collective_id=0, has_side_effects=True, vmem_limit_bytes=58 * 2**20
        ),
    )(inputs[0], out_grad, filters[0], taps, *(jnp.asarray(table) for table in tables))
    in_grad, filter_grad, tap_grad = pl.pallas_call(
        write_kernel,
        out_shape=(
            jax.ShapeDtypeStruct(in_grad.shape, BF16),
            jax.ShapeDtypeStruct(filter_grad.shape, F32),
            jax.ShapeDtypeStruct(tap_sums.shape, F32),
        ),
        in_specs=[vmem_spec] * 3,
        out_specs=(vmem_spec,) * 3,
        compiler_params=pltpu.CompilerParams(vmem_limit_bytes=58 * 2**20),
    )(in_grad, filter_grad, tap_sums)
    return (in_grad[None], filter_grad[None], tap_grad.reshape(1, 3, TAPS, channels))


def solution(mesh):
    placed = (
        P("section", None, "ctx"),
        P(None, "ctx"),
        P("section", "ctx", None),
        P("section", None, None, None),
    )

    def run(inputs, out_grad, filters, conv_taps):
        sections, blocks = mesh.shape["section"], mesh.shape["ctx"]
        rows = filters.shape[1] // (sections * blocks)
        lanes = inputs.shape[2] // blocks
        fits = sections == 2 and rows % GROUP == 0 and lanes == 128 and lanes % (sections * rows) == 0
        return jax.shard_map(
            kernel_shards if fits else shards,
            mesh=mesh,
            in_specs=placed,
            out_specs=(
                P("section", None, "ctx"),
                P("section", "ctx", None),
                P("section", None, None, "ctx"),
            ),
            check_vma=False,
        )(inputs, out_grad, filters, conv_taps)

    return run
```

```python
import functools
import math

import jax
import jax.numpy as jnp
import ml_dtypes
import numpy as np
from jax import lax
from jax.experimental import pallas as pl
from jax.experimental.pallas import tpu as pltpu
from jax.sharding import PartitionSpec as P

PRECISE = lax.Precision.HIGH


def shifted(block, axis, distance):
    devices = range(lax.axis_size(axis))
    route = [(i - distance, i) for i in devices if i - distance in devices]
    return lax.ppermute(block, axis, route)


def angle_table(row_count, col_count, modulus):
    row_ids = lax.broadcasted_iota(jnp.int32, (row_count, col_count), 0)
    col_ids = lax.broadcasted_iota(jnp.int32, (row_count, col_count), 1)
    product_mod = row_ids * col_ids % modulus
    angles = product_mod.astype(jnp.float32) * (2.0 * math.pi / modulus)
    return (jnp.cos(angles), jnp.sin(angles))


def make_tables(blocks_a, block_b):
    half_a = blocks_a // 2
    total_n = blocks_a * block_b
    return (
        angle_table(blocks_a, half_a, blocks_a),
        angle_table(half_a, blocks_a, blocks_a),
        angle_table(blocks_a, block_b, total_n),
        angle_table(block_b, block_b, block_b),
    )


def forward_spectrum(signal, tables):
    cos_one, sin_one = tables[0]
    cos_tw, sin_tw = tables[2]
    cos_two, sin_two = tables[3]
    channels = signal.shape[0]
    half_a = cos_one.shape[1]
    block_b = cos_two.shape[0]
    shaped = signal.reshape(channels, half_a, block_b)
    real_y = jnp.einsum("ka,cab->ckb", cos_one, shaped, precision=PRECISE)
    imag_y = -jnp.einsum("ka,cab->ckb", sin_one, shaped, precision=PRECISE)
    real_z = real_y * cos_tw + imag_y * sin_tw
    imag_z = imag_y * cos_tw - real_y * sin_tw
    real_x = jnp.einsum("ckb,mb->ckm", real_z, cos_two, precision=PRECISE) + jnp.einsum(
        "ckb,mb->ckm", imag_z, sin_two, precision=PRECISE
    )
    imag_x = jnp.einsum("ckb,mb->ckm", imag_z, cos_two, precision=PRECISE) - jnp.einsum(
        "ckb,mb->ckm", real_z, sin_two, precision=PRECISE
    )
    return (real_x, imag_x)


def inverse_signal(real_x, imag_x, tables):
    cos_one, sin_one = tables[1]
    cos_tw, sin_tw = tables[2]
    cos_two, sin_two = tables[3]
    channels = real_x.shape[0]
    half_a = cos_one.shape[0]
    block_b = cos_two.shape[0]
    total_n = cos_one.shape[1] * block_b
    real_p = jnp.einsum("ckm,mb->ckb", real_x, cos_two, precision=PRECISE) - jnp.einsum(
        "ckm,mb->ckb", imag_x, sin_two, precision=PRECISE
    )
    imag_p = jnp.einsum("ckm,mb->ckb", real_x, sin_two, precision=PRECISE) + jnp.einsum(
        "ckm,mb->ckb", imag_x, cos_two, precision=PRECISE
    )
    real_q = real_p * cos_tw - imag_p * sin_tw
    imag_q = real_p * sin_tw + imag_p * cos_tw
    summed = jnp.einsum("ak,ckb->cab", cos_one, real_q, precision=PRECISE) - jnp.einsum(
        "ak,ckb->cab", sin_one, imag_q, precision=PRECISE
    )
    return summed.reshape(channels, half_a * block_b) / total_n


def times_conj(real_a, imag_a, real_b, imag_b):
    return (real_a * real_b + imag_a * imag_b, real_a * imag_b - imag_a * real_b)


def features(padded, weights, length):
    summed = jnp.zeros((3, padded.shape[0], length), jnp.float32)
    for offset in range(7):
        window = padded[:, 6 - offset : 6 - offset + length].astype(jnp.float32)
        summed = summed + weights[:, offset, :, None] * window[None]
    return summed.astype(jnp.bfloat16)


def transposed(grad_all, weights):
    length = grad_all.shape[2]
    padded = jnp.pad(grad_all, ((0, 0), (0, 0), (0, 6)))
    summed = jnp.zeros(grad_all.shape[1:], jnp.float32)
    for offset in range(7):
        summed = summed + jnp.sum(
            weights[:, offset, :, None] * padded[:, :, offset : offset + length], axis=0
        )
    return summed


def tap_grads(padded, grad_all):
    length = grad_all.shape[2]
    per_offset = []
    for offset in range(7):
        window = padded[:, 6 - offset : 6 - offset + length].astype(jnp.float32)
        per_offset.append(jnp.sum(grad_all * window[None], axis=2))
    return jnp.stack(per_offset, axis=1)


def take_rows(array, first_ch, count, axis_num):
    return lax.dynamic_slice_in_dim(array, first_ch, count, axis_num)


def masked_write(array, update, first_ch, active, axis_num):
    previous = lax.dynamic_slice_in_dim(array, first_ch, update.shape[axis_num], axis_num)
    return lax.dynamic_update_slice_in_dim(
        array, jnp.where(active, update, previous), first_ch, axis_num
    )


def shards(inputs, out_grad, filters, conv_taps):
    x_rows = inputs[0]
    tok_dev = x_rows.shape[1]
    section_count = lax.axis_size("section")
    section_idx = lax.axis_index("section")
    ctx_idx = lax.axis_index("ctx")
    weights = conv_taps[0]
    channels = filters.shape[1]
    length = filters.shape[2]
    blocks_a = 2 * length // tok_dev
    own_taps = lax.dynamic_slice_in_dim(weights, ctx_idx * channels, channels, 2)
    prior_cols = shifted(x_rows[:, tok_dev - 6 :], "ctx", 1)
    featured_rows = features(jnp.concatenate([prior_cols, x_rows], axis=1), weights, tok_dev)
    x_chan, featured, grad_chan = (
        lax.all_to_all(x_rows[None], "ctx", split_axis=1, concat_axis=2, tiled=True),
        lax.all_to_all(featured_rows, "ctx", split_axis=1, concat_axis=2, tiled=True),
        lax.all_to_all(out_grad[None], "ctx", split_axis=1, concat_axis=2, tiled=True),
    )
    x_chan = x_chan[0]
    x_padded = jnp.pad(x_chan, ((0, 0), (6, 0)))
    grad_chan = grad_chan[0]
    tables = make_tables(blocks_a, tok_dev)
    key_full = featured[1].astype(jnp.float32)
    mixed_kv = key_full * featured[2].astype(jnp.float32)
    real_h, imag_h = forward_spectrum(filters[0].astype(jnp.float32), tables)
    real_w, imag_w = forward_spectrum(mixed_kv, tables)
    convolved = inverse_signal(
        real_h * real_w - imag_h * imag_w, real_h * imag_w + imag_h * real_w, tables
    )
    block_ch = 2
    block_count = channels // block_ch
    last_section = section_count - 1
    turns = block_count + section_count - 1
    dx_init = jnp.zeros((channels, length), jnp.bfloat16)

    def advance(turn_idx, carried):
        incoming, dz_all, dx_store, tap_acc = carried
        block_id = turn_idx - (last_section - section_idx)
        active = (block_id >= 0) & (block_id < block_count)
        first_ch = jnp.clip(block_id, 0, block_count - 1) * block_ch
        from_next = take_rows(grad_chan, first_ch, block_ch, 0)
        grad_in = jnp.where(section_idx == last_section, from_next, incoming).astype(jnp.float32)
        feat_blk = take_rows(featured, first_ch, block_ch, 1).astype(jnp.float32)
        grad_z = grad_in * feat_blk[0]
        grad_q = grad_in * take_rows(convolved, first_ch, block_ch, 0)
        real_d, imag_d = forward_spectrum(grad_z, tables)
        real_c, imag_c = times_conj(
            take_rows(real_h, first_ch, block_ch, 0),
            take_rows(imag_h, first_ch, block_ch, 0),
            real_d,
            imag_d,
        )
        grad_w = inverse_signal(real_c, imag_c, tables)
        grad_all = jnp.stack([grad_q, grad_w * feat_blk[2], grad_w * feat_blk[1]])
        in_blk = transposed(grad_all, take_rows(own_taps, first_ch, block_ch, 2)).astype(
            jnp.bfloat16
        )
        tap_new = tap_grads(take_rows(x_padded, first_ch, block_ch, 0), grad_all)
        tap_acc = masked_write(tap_acc, tap_new, first_ch, active, 2)
        dz_all = masked_write(dz_all, grad_z, first_ch, active, 0)
        outgoing = shifted(in_blk, "section", -1)
        dx_store = masked_write(dx_store, in_blk, first_ch, active, 0)
        return (outgoing, dz_all, dx_store, tap_acc)

    start_state = (
        jnp.zeros((block_ch, length), jnp.bfloat16),
        jnp.zeros((channels, length), jnp.float32),
        dx_init,
        jnp.zeros((3, 7, channels), jnp.float32),
    )
    final_state = lax.fori_loop(0, turns, advance, start_state)
    dz_all = final_state[1]
    dx_store = final_state[2]
    tap_acc = final_state[3]
    real_d, imag_d = forward_spectrum(dz_all, tables)
    real_c, imag_c = times_conj(real_w, imag_w, real_d, imag_d)
    filter_grad = inverse_signal(real_c, imag_c, tables)
    in_rows = lax.all_to_all(dx_store, "ctx", split_axis=1, concat_axis=0, tiled=True)
    return (in_rows[None], filter_grad[None], tap_acc[None])


TAPS = 7
GROUP = 16
MESH = pl.DeviceIdType.MESH
F32 = jnp.float32
BF16 = jnp.bfloat16


def right_angle_tables(blocks_a, block_b):
    total_n = blocks_a * block_b
    first_k = np.arange(blocks_a)
    phase_one = 2 * np.pi * np.outer(first_k + 0.25, np.arange(blocks_a)) / blocks_a
    one = np.stack([np.cos(phase_one), -np.sin(phase_one)])
    first = np.einsum("rka,cd->rkcad", one, np.eye(GROUP))
    first = first.reshape(2 * blocks_a * GROUP, blocks_a * GROUP)
    points = first_k[:, None, None] + 0.25 + blocks_a * np.arange(block_b)[None, None, :]
    phase_two = 2 * np.pi * np.arange(block_b)[None, :, None] * points / total_n
    real, imag = np.cos(phase_two), -np.sin(phase_two)
    second = np.concatenate(
        [np.concatenate([real, imag], axis=2), np.concatenate([-imag, real], axis=2)], axis=1
    )
    return tuple(
        array.astype(ml_dtypes.bfloat16)
        for array in (first, first.T / total_n, second, second.transpose(0, 2, 1))
    )


def mixer_kernel(
    sections,
    x_ref,
    og_ref,
    filt_ref,
    tap_ref,
    one_ref,
    one_inv_ref,
    two_ref,
    two_inv_ref,
    ig_out,
    fg_out,
    tg_out,
    xbuf,
    ogbuf,
    hbuf,
    tap_blk,
    tap_rows,
    tbuf,
    one_v,
    one_inv_v,
    two_v,
    two_inv_v,
    tapb,
    xs_ref,
    feat,
    sig,
    ybuf,
    spec,
    qbuf,
    cbuf,
    gwbuf,
    gbuf,
    igbuf,
    fgbuf,
    tgbuf,
    tgin,
    x_send,
    x_recv,
    og_send,
    og_recv,
    h_send,
    h_recv,
    t_send,
    t_recv,
    ig_send,
    ig_recv,
    fg_send,
    fg_recv,
    tg_send,
    tg_recv,
    table_sem,
    blk_sem,
):
    sec = lax.axis_index("section")
    ctx = lax.axis_index("ctx")
    blocks = xbuf.shape[1]
    rows = xbuf.shape[2]
    lanes = xbuf.shape[3]
    groups = rows // GROUP
    other = 1 - sec

    tables = [
        pltpu.make_async_copy(src, dst, table_sem.at[n])
        for n, (src, dst) in enumerate(
            ((one_ref, one_v), (two_ref, two_v), (one_inv_ref, one_inv_v), (two_inv_ref, two_inv_v))
        )
    ]

    channels = sections * rows
    tap_first = ctx * channels
    tap_lane = pl.multiple_of(tap_first // lanes * lanes, lanes)
    tap_load = pltpu.make_async_copy(tap_ref.at[:, :, pl.ds(tap_lane, lanes)], tap_blk, blk_sem)
    tap_load.start()

    barrier = pltpu.get_barrier_semaphore()

    def greet(step, carry):
        to_ctx = lax.rem(ctx + step, blocks)
        pl.semaphore_signal(barrier, inc=1, device_id=(other, to_ctx), device_id_type=MESH)

        @pl.when(step > 0)
        def _():
            pl.semaphore_signal(barrier, inc=1, device_id=(sec, to_ctx), device_id_type=MESH)

        return carry

    lax.fori_loop(0, blocks, greet, 0, unroll=True)
    for table in tables:
        table.start()
    pl.semaphore_wait(barrier, sections * blocks - 1)

    def row_block(to_sec, to_ctx):
        return pl.ds(pl.multiple_of((to_ctx * sections + to_sec) * rows, rows), rows)

    def half(which):
        return pl.ds(pl.multiple_of(which * rows, rows), rows)

    def remote(src, dst, send_sem, recv_sem, to_sec, to_ctx):
        pltpu.make_async_remote_copy(
            src_ref=src,
            dst_ref=dst,
            send_sem=send_sem,
            recv_sem=recv_sem,
            device_id=(to_sec, to_ctx),
            device_id_type=MESH,
        ).start()

    def await_bytes(ref, sem):
        pltpu.make_async_copy(ref, ref, sem).wait()

    remote(filt_ref.at[half(other)], hbuf.at[sec], h_send, h_recv.at[1], other, ctx)
    pltpu.make_async_copy(filt_ref.at[half(sec)], hbuf.at[sec], h_recv.at[0]).start()

    def send_x(to_sec):
        def send(step, carry):
            to_ctx = lax.rem(ctx + step, blocks)
            src = x_ref.at[row_block(to_sec, to_ctx)]
            remote(src, xbuf.at[sec, ctx], x_send, x_recv.at[sec], to_sec, to_ctx)
            return carry

        return send

    pltpu.make_async_copy(
        x_ref.at[row_block(sec, ctx)], xbuf.at[sec, ctx], x_recv.at[sec]
    ).start()
    lax.fori_loop(1, blocks, send_x(sec), 0, unroll=True)
    lax.fori_loop(0, blocks, send_x(other), 0, unroll=True)

    def send_og(step, carry):
        to_ctx = lax.rem(ctx + step, blocks)
        remote(og_ref.at[row_block(sec, to_ctx)], ogbuf.at[ctx], og_send, og_recv, sec, to_ctx)
        return carry

    pltpu.make_async_copy(og_ref.at[row_block(sec, ctx)], ogbuf.at[ctx], og_recv).start()
    lax.fori_loop(1, blocks, send_og, 0, unroll=True)

    tap_load.wait()
    tap_rows[...] = jnp.zeros_like(tap_rows)
    tap_rows[pl.ds(0, 3 * TAPS)] = tap_blk[...].reshape(3 * TAPS, lanes)
    tap_rows[...] = tap_rows[...].T

    def tap_half(which):
        first = lax.rem(tap_first, lanes) + which * rows
        return tap_rows.at[pl.ds(pl.multiple_of(first, rows), rows)]

    remote(tap_half(other), tbuf.at[sec], t_send, t_recv.at[1], other, ctx)
    pltpu.make_async_copy(tap_half(sec), tbuf.at[sec], t_recv.at[0]).start()

    def rows_at(first):
        return pl.ds(first if isinstance(first, int) else pl.multiple_of(first, GROUP), GROUP)

    def stage_one(blocks_of, first_row):
        cols = jnp.concatenate(
            [blocks_of(g).reshape(blocks * GROUP, lanes) for g in range(groups)], axis=1
        )
        out = jnp.dot(one_v[...], cols, preferred_element_type=F32).astype(BF16)
        out = out.reshape(2, blocks, GROUP, groups * lanes)
        for g in range(groups):
            for part in range(2):
                ybuf[:, rows_at(first_row + g * GROUP), pl.ds(part * lanes, lanes)] = out[
                    part, :, :, g * lanes : (g + 1) * lanes
                ]

    def stage_two(k, first_row, count):
        return jnp.dot(ybuf[k, pl.ds(first_row, count)], two_v[k], preferred_element_type=F32)

    def each_point(body):
        def step(k, carry):
            body(k)
            return carry

        lax.fori_loop(0, blocks, step, 0, unroll=True)

    def product(left, right, conj):
        left_r, left_i = left[:, :lanes], left[:, lanes:]
        right_r, right_i = right[:, :lanes], right[:, lanes:]
        if conj:
            real = left_r * right_r + left_i * right_i
            imag = left_r * right_i - left_i * right_r
        else:
            real = left_r * right_r - left_i * right_i
            imag = left_r * right_i + left_i * right_r
        return jnp.concatenate([real, imag], axis=1).astype(BF16)

    def inverse_two(k, operand, slots):
        out = jnp.dot(operand, two_inv_v[k], preferred_element_type=F32).astype(BF16)
        for position, slot in enumerate(slots):
            for g in range(groups):
                first = (position * groups + g) * GROUP
                for part in range(2):
                    qbuf[slot, part, k, :, pl.ds(g * lanes, lanes)] = out[
                        first : first + GROUP, part * lanes : (part + 1) * lanes
                    ]

    def inverse_one(slot):
        out = jnp.dot(
            one_inv_v[...],
            qbuf[slot].reshape(2 * blocks * GROUP, groups * lanes),
            preferred_element_type=F32,
        )
        return out.reshape(blocks, GROUP, groups * lanes)

    lane = lax.broadcasted_iota(jnp.int32, (rows, lanes), 1)

    def features_of(layer):
        def body(a, before):
            window = xbuf[layer, a].astype(F32)
            sums = [None] * 3
            rolled = []
            for j in range(TAPS):
                if j == 0:
                    moved = window
                else:
                    turned = pltpu.roll(window, j, 1)
                    rolled.append(turned)
                    moved = jnp.where(lane < j, before[j - 1], turned)
                xs_ref[layer, j, a] = moved
                for i in range(3):
                    term = tapb[layer, i * TAPS + j] * moved
                    sums[i] = term if sums[i] is None else sums[i] + term
            rounded = [total.astype(BF16) for total in sums]
            for i in range(3):
                feat[layer, i, a] = rounded[i]
            sig[a] = (rounded[1].astype(F32) * rounded[2].astype(F32)).astype(BF16)
            return tuple(rolled)

        zero = jnp.zeros((rows, lanes), F32)
        lax.fori_loop(0, blocks, body, (zero,) * (TAPS - 1), unroll=2)

    pair = 2 * rows
    for place, layer in enumerate((sec, other)):
        first_row = pl.multiple_of(layer * pair, pair)
        if place == 0:
            tables[0].wait()
        await_bytes(hbuf.at[layer], h_recv.at[place])
        stage_one(
            lambda g: jnp.stack(
                [
                    hbuf[layer, pl.ds(g * GROUP, GROUP), pl.ds(a * lanes, lanes)]
                    for a in range(blocks)
                ]
            ),
            first_row,
        )
        await_bytes(tbuf.at[layer], t_recv.at[place])
        values = tbuf[layer]
        for n in range(3 * TAPS):
            tapb[layer, n] = jnp.broadcast_to(values[:, n : n + 1], (rows, lanes))
        await_bytes(xbuf.at[layer], x_recv.at[layer])
        features_of(layer)
        stage_one(lambda g: sig[:, pl.ds(g * GROUP, GROUP), :], first_row + rows)
        if place == 0:
            tables[1].wait()
            tables[2].wait()
            tables[3].wait()

        def mixed_point(k):
            both = stage_two(k, first_row, pair)
            spec[k, pl.ds(first_row, pair)] = both
            inverse_two(k, product(both[:rows], both[rows:], False), (0,))

        each_point(mixed_point)
        out = inverse_one(0)
        for g in range(groups):
            cbuf[layer, :, pl.ds(g * GROUP, GROUP), :] = out[:, :, g * lanes : (g + 1) * lanes]

    def send_home(layer, src, dst, send_sem, recv_sem):
        @pl.when(sec == layer)
        def _():
            pltpu.make_async_copy(src, dst, recv_sem).start()

        @pl.when(sec != layer)
        def _():
            remote(src, dst, send_sem, recv_sem, layer, ctx)

    def filter_grad_of(layer):
        out = inverse_one(1 + layer)
        for a in range(blocks):
            for g in range(groups):
                fgbuf[layer, pl.ds(g * GROUP, GROUP), pl.ds(a * lanes, lanes)] = out[
                    a, :, g * lanes : (g + 1) * lanes
                ].astype(BF16)
        send_home(layer, fgbuf.at[layer], fg_out.at[half(sec)], fg_send, fg_recv)

    for layer in range(sections - 1, -1, -1):
        if layer == sections - 1:
            await_bytes(ogbuf, og_recv)
            carried = ogbuf
        else:
            carried = igbuf.at[layer + 1]

        sig[...] = (carried[...].astype(F32) * feat[layer, 0].astype(F32)).astype(BF16)
        stage_one(lambda g: sig[:, pl.ds(g * GROUP, GROUP), :], 0)

        def grad_point(k):
            d_spec = stage_two(k, 0, rows)
            with_h = product(spec[k, pl.ds(layer * pair, rows)], d_spec, True)
            with_w = product(spec[k, pl.ds(layer * pair + rows, rows)], d_spec, True)
            inverse_two(k, jnp.concatenate([with_h, with_w], axis=0), (0, 1 + layer))

        each_point(grad_point)
        if layer == 0:
            filter_grad_of(layer)
        out = inverse_one(0)
        for g in range(groups):
            gwbuf[:, pl.ds(g * GROUP, GROUP), :] = out[:, :, g * lanes : (g + 1) * lanes]

        def transposed_at(step, after):
            a = blocks - 1 - step
            grad_w = gwbuf[a]
            grads = (
                carried[a].astype(F32) * cbuf[layer, a],
                grad_w * feat[layer, 2, a].astype(F32),
                grad_w * feat[layer, 1, a].astype(F32),
            )
            for i in range(3):
                gbuf[layer, i, a] = grads[i]
            total = None
            rolled = []
            for j in range(TAPS):
                part = tapb[layer, j] * grads[0]
                for i in range(1, 3):
                    part = part + tapb[layer, i * TAPS + j] * grads[i]
                if j == 0:
                    total = part
                else:
                    turned = pltpu.roll(part, lanes - j, 1)
                    rolled.append(turned)
                    total = total + jnp.where(lane < lanes - j, turned, after[j - 1])
            igbuf[layer, a] = total.astype(BF16)
            return tuple(rolled)

        zero = jnp.zeros((rows, lanes), F32)
        lax.fori_loop(0, blocks, transposed_at, (zero,) * (TAPS - 1), unroll=2)

        def send_ig(step, carry):
            to_ctx = lax.rem(ctx + step, blocks)
            dst = ig_out.at[row_block(sec, ctx)]
            remote(igbuf.at[layer, to_ctx], dst, ig_send, ig_recv, layer, to_ctx)
            return carry

        lax.fori_loop(1, blocks, send_ig, 0, unroll=True)
        send_home(layer, igbuf.at[layer, ctx], ig_out.at[row_block(sec, ctx)], ig_send, ig_recv)

        if layer == 0:
            for later in range(1, sections):
                filter_grad_of(later)

    for layer in range(sections - 1, -1, -1):
        for first in range(0, rows, 8):
            def add_taps(a, sums):
                grads = [gbuf[layer, i, a, pl.ds(first, 8)] for i in range(3)]
                new = []
                for j in range(TAPS):
                    moved = xs_ref[layer, j, a, pl.ds(first, 8)]
                    for i in range(3):
                        new.append(sums[j * 3 + i] + grads[i] * moved)
                return tuple(new)

            zero_8 = jnp.zeros((8, lanes), F32)
            sums = lax.fori_loop(0, blocks, add_taps, (zero_8,) * (3 * TAPS), unroll=4)
            lane_8 = lax.broadcasted_iota(jnp.int32, (8, lanes), 1)
            packed = zero_8
            for j in range(TAPS):
                for i in range(3):
                    column = jnp.sum(sums[j * 3 + i], axis=1, keepdims=True)
                    packed = jnp.where(lane_8 == i * TAPS + j, column, packed)
            tgbuf[layer, pl.ds(first, 8)] = packed
        send_home(layer, tgbuf.at[layer], tgin.at[half(sec)], tg_send, tg_recv)

    others = sections * blocks - 1
    await_bytes(x_ref.at[pl.ds(0, others * rows)], x_send)
    await_bytes(og_ref.at[pl.ds(0, (blocks - 1) * rows)], og_send)
    await_bytes(filt_ref.at[pl.ds(0, rows)], h_send)
    await_bytes(tbuf.at[0], t_send)
    await_bytes(ig_out.at[pl.ds(0, others * rows)], ig_send)
    await_bytes(fg_out.at[pl.ds(0, rows)], fg_send)
    await_bytes(tgbuf.at[0], tg_send)
    await_bytes(tgin, tg_recv)
    tg_out[...] = tgin[...].T[: 3 * TAPS].reshape(3 * TAPS, 1, channels)
    await_bytes(fg_out, fg_recv)
    await_bytes(ig_out, ig_recv)


def write_kernel(ig_ref, fg_ref, tg_ref, ig_out, fg_out, tg_out, narrow, wide, sems, load, store):
    whole = [
        pltpu.make_async_copy(ig_ref, ig_out, sems.at[0]),
        pltpu.make_async_copy(tg_ref, tg_out, sems.at[1]),
    ]
    parts = [pl.ds(first, GROUP) for first in range(0, fg_ref.shape[0], GROUP)]
    loads = [
        pltpu.make_async_copy(fg_ref.at[part], narrow.at[part], load.at[n])
        for n, part in enumerate(parts)
    ]
    stores = [
        pltpu.make_async_copy(wide.at[part], fg_out.at[part], store.at[n])
        for n, part in enumerate(parts)
    ]
    for copy in loads + whole:
        copy.start()
    for n, part in enumerate(parts):
        loads[n].wait()
        wide[part] = narrow[part].astype(F32)
        stores[n].start()
    for copy in stores + whole:
        copy.wait()


def kernel_shards(inputs, out_grad, filters, conv_taps):
    sections = lax.axis_size("section")
    blocks = lax.axis_size("ctx")
    _, depth, lanes = inputs.shape
    _, channels, length = filters.shape
    rows = channels // sections
    tables = right_angle_tables(blocks, lanes)
    taps = conv_taps.reshape(3 * TAPS, 1, depth)
    vmem = pltpu.VMEM
    dma = pltpu.SemaphoreType.DMA
    any_spec = pl.BlockSpec(memory_space=pl.ANY)
    hbm_spec = pl.BlockSpec(memory_space=pl.ANY)
    vmem_spec = pl.BlockSpec(memory_space=pltpu.VMEM)
    spectrum_rows = 2 * sections * rows
    in_grad, filter_grad, tap_sums = pl.pallas_call(
        functools.partial(mixer_kernel, sections),
        out_shape=(
            jax.ShapeDtypeStruct((depth, lanes), BF16),
            jax.ShapeDtypeStruct((channels, length), BF16),
            jax.ShapeDtypeStruct((3 * TAPS, 1, channels), F32),
        ),
        in_specs=[hbm_spec] * 8,
        out_specs=(any_spec, any_spec, vmem_spec),
        scratch_shapes=[
            vmem((sections, blocks, rows, lanes), BF16),
            vmem((blocks, rows, lanes), BF16),
            vmem((sections, rows, length), BF16),
            vmem((3 * TAPS, 1, lanes), F32),
            vmem((lanes, lanes), F32),
            vmem((sections, rows, lanes), F32),
            vmem(tables[0].shape, BF16),
            vmem(tables[1].shape, BF16),
            vmem(tables[2].shape, BF16),
            vmem(tables[3].shape, BF16),
            vmem((sections, 3 * TAPS, rows, lanes), F32),
            vmem((sections, TAPS, blocks, rows, lanes), F32),
            vmem((sections, 3, blocks, rows, lanes), BF16),
            vmem((blocks, rows, lanes), BF16),
            vmem((blocks, spectrum_rows, 2 * lanes), BF16),
            vmem((blocks, spectrum_rows, 2 * lanes), F32),
            vmem((1 + sections, 2, blocks, GROUP, rows // GROUP * lanes), BF16),
            vmem((sections, blocks, rows, lanes), F32),
            vmem((blocks, rows, lanes), F32),
            vmem((sections, 3, blocks, rows, lanes), F32),
            vmem((sections, blocks, rows, lanes), BF16),
            vmem((sections, rows, length), BF16),
            vmem((sections, rows, lanes), F32),
            vmem((channels, lanes), F32),
            dma(()),
            dma((sections,)),
            dma(()),
            dma(()),
            dma(()),
            dma((2,)),
            dma(()),
            dma((2,)),
            dma(()),
            dma(()),
            dma(()),
            dma(()),
            dma(()),
            dma(()),
            dma((4,)),
            dma(()),
        ],
        compiler_params=pltpu.CompilerParams(
            collective_id=0, has_side_effects=True, vmem_limit_bytes=58 * 2**20
        ),
    )(inputs[0], out_grad, filters[0], taps, *(jnp.asarray(table) for table in tables))
    in_grad, filter_grad, tap_grad = pl.pallas_call(
        write_kernel,
        out_shape=(
            jax.ShapeDtypeStruct(in_grad.shape, BF16),
            jax.ShapeDtypeStruct(filter_grad.shape, F32),
            jax.ShapeDtypeStruct(tap_sums.shape, F32),
        ),
        in_specs=[any_spec] * 3,
        out_specs=(any_spec,) * 3,
        scratch_shapes=[
            vmem(filter_grad.shape, BF16),
            vmem(filter_grad.shape, F32),
            dma((2,)),
            dma((channels // GROUP,)),
            dma((channels // GROUP,)),
        ],
        compiler_params=pltpu.CompilerParams(vmem_limit_bytes=58 * 2**20),
    )(in_grad, filter_grad, tap_sums)
    return (in_grad[None], filter_grad[None], tap_grad.reshape(1, 3, TAPS, channels))


def solution(mesh):
    placed = (
        P("section", None, "ctx"),
        P(None, "ctx"),
        P("section", "ctx", None),
        P("section", None, None, None),
    )

    def run(inputs, out_grad, filters, conv_taps):
        sections, blocks = mesh.shape["section"], mesh.shape["ctx"]
        rows = filters.shape[1] // (sections * blocks)
        lanes = inputs.shape[2] // blocks
        fits = sections == 2 and rows % GROUP == 0 and lanes == 128 and lanes % (sections * rows) == 0
        return jax.shard_map(
            kernel_shards if fits else shards,
            mesh=mesh,
            in_specs=placed,
            out_specs=(
                P("section", None, "ctx"),
                P("section", "ctx", None),
                P("section", None, None, "ctx"),
            ),
            check_vma=False,
        )(inputs, out_grad, filters, conv_taps)

    return run
```

```python
import functools
import math

import jax
import jax.numpy as jnp
import ml_dtypes
import numpy as np
from jax import lax
from jax.experimental import pallas as pl
from jax.experimental.pallas import tpu as pltpu
from jax.sharding import PartitionSpec as P

PRECISE = lax.Precision.HIGH


def shifted(block, axis, distance):
    devices = range(lax.axis_size(axis))
    route = [(i - distance, i) for i in devices if i - distance in devices]
    return lax.ppermute(block, axis, route)


def angle_table(row_count, col_count, modulus):
    row_ids = lax.broadcasted_iota(jnp.int32, (row_count, col_count), 0)
    col_ids = lax.broadcasted_iota(jnp.int32, (row_count, col_count), 1)
    product_mod = row_ids * col_ids % modulus
    angles = product_mod.astype(jnp.float32) * (2.0 * math.pi / modulus)
    return (jnp.cos(angles), jnp.sin(angles))


def make_tables(blocks_a, block_b):
    half_a = blocks_a // 2
    total_n = blocks_a * block_b
    return (
        angle_table(blocks_a, half_a, blocks_a),
        angle_table(half_a, blocks_a, blocks_a),
        angle_table(blocks_a, block_b, total_n),
        angle_table(block_b, block_b, block_b),
    )


def forward_spectrum(signal, tables):
    cos_one, sin_one = tables[0]
    cos_tw, sin_tw = tables[2]
    cos_two, sin_two = tables[3]
    channels = signal.shape[0]
    half_a = cos_one.shape[1]
    block_b = cos_two.shape[0]
    shaped = signal.reshape(channels, half_a, block_b)
    real_y = jnp.einsum("ka,cab->ckb", cos_one, shaped, precision=PRECISE)
    imag_y = -jnp.einsum("ka,cab->ckb", sin_one, shaped, precision=PRECISE)
    real_z = real_y * cos_tw + imag_y * sin_tw
    imag_z = imag_y * cos_tw - real_y * sin_tw
    real_x = jnp.einsum("ckb,mb->ckm", real_z, cos_two, precision=PRECISE) + jnp.einsum(
        "ckb,mb->ckm", imag_z, sin_two, precision=PRECISE
    )
    imag_x = jnp.einsum("ckb,mb->ckm", imag_z, cos_two, precision=PRECISE) - jnp.einsum(
        "ckb,mb->ckm", real_z, sin_two, precision=PRECISE
    )
    return (real_x, imag_x)


def inverse_signal(real_x, imag_x, tables):
    cos_one, sin_one = tables[1]
    cos_tw, sin_tw = tables[2]
    cos_two, sin_two = tables[3]
    channels = real_x.shape[0]
    half_a = cos_one.shape[0]
    block_b = cos_two.shape[0]
    total_n = cos_one.shape[1] * block_b
    real_p = jnp.einsum("ckm,mb->ckb", real_x, cos_two, precision=PRECISE) - jnp.einsum(
        "ckm,mb->ckb", imag_x, sin_two, precision=PRECISE
    )
    imag_p = jnp.einsum("ckm,mb->ckb", real_x, sin_two, precision=PRECISE) + jnp.einsum(
        "ckm,mb->ckb", imag_x, cos_two, precision=PRECISE
    )
    real_q = real_p * cos_tw - imag_p * sin_tw
    imag_q = real_p * sin_tw + imag_p * cos_tw
    summed = jnp.einsum("ak,ckb->cab", cos_one, real_q, precision=PRECISE) - jnp.einsum(
        "ak,ckb->cab", sin_one, imag_q, precision=PRECISE
    )
    return summed.reshape(channels, half_a * block_b) / total_n


def times_conj(real_a, imag_a, real_b, imag_b):
    return (real_a * real_b + imag_a * imag_b, real_a * imag_b - imag_a * real_b)


def features(padded, weights, length):
    summed = jnp.zeros((3, padded.shape[0], length), jnp.float32)
    for offset in range(7):
        window = padded[:, 6 - offset : 6 - offset + length].astype(jnp.float32)
        summed = summed + weights[:, offset, :, None] * window[None]
    return summed.astype(jnp.bfloat16)


def transposed(grad_all, weights):
    length = grad_all.shape[2]
    padded = jnp.pad(grad_all, ((0, 0), (0, 0), (0, 6)))
    summed = jnp.zeros(grad_all.shape[1:], jnp.float32)
    for offset in range(7):
        summed = summed + jnp.sum(
            weights[:, offset, :, None] * padded[:, :, offset : offset + length], axis=0
        )
    return summed


def tap_grads(padded, grad_all):
    length = grad_all.shape[2]
    per_offset = []
    for offset in range(7):
        window = padded[:, 6 - offset : 6 - offset + length].astype(jnp.float32)
        per_offset.append(jnp.sum(grad_all * window[None], axis=2))
    return jnp.stack(per_offset, axis=1)


def take_rows(array, first_ch, count, axis_num):
    return lax.dynamic_slice_in_dim(array, first_ch, count, axis_num)


def masked_write(array, update, first_ch, active, axis_num):
    previous = lax.dynamic_slice_in_dim(array, first_ch, update.shape[axis_num], axis_num)
    return lax.dynamic_update_slice_in_dim(
        array, jnp.where(active, update, previous), first_ch, axis_num
    )


def shards(inputs, out_grad, filters, conv_taps):
    x_rows = inputs[0]
    tok_dev = x_rows.shape[1]
    section_count = lax.axis_size("section")
    section_idx = lax.axis_index("section")
    ctx_idx = lax.axis_index("ctx")
    weights = conv_taps[0]
    channels = filters.shape[1]
    length = filters.shape[2]
    blocks_a = 2 * length // tok_dev
    own_taps = lax.dynamic_slice_in_dim(weights, ctx_idx * channels, channels, 2)
    prior_cols = shifted(x_rows[:, tok_dev - 6 :], "ctx", 1)
    featured_rows = features(jnp.concatenate([prior_cols, x_rows], axis=1), weights, tok_dev)
    x_chan, featured, grad_chan = (
        lax.all_to_all(x_rows[None], "ctx", split_axis=1, concat_axis=2, tiled=True),
        lax.all_to_all(featured_rows, "ctx", split_axis=1, concat_axis=2, tiled=True),
        lax.all_to_all(out_grad[None], "ctx", split_axis=1, concat_axis=2, tiled=True),
    )
    x_chan = x_chan[0]
    x_padded = jnp.pad(x_chan, ((0, 0), (6, 0)))
    grad_chan = grad_chan[0]
    tables = make_tables(blocks_a, tok_dev)
    key_full = featured[1].astype(jnp.float32)
    mixed_kv = key_full * featured[2].astype(jnp.float32)
    real_h, imag_h = forward_spectrum(filters[0].astype(jnp.float32), tables)
    real_w, imag_w = forward_spectrum(mixed_kv, tables)
    convolved = inverse_signal(
        real_h * real_w - imag_h * imag_w, real_h * imag_w + imag_h * real_w, tables
    )
    block_ch = 2
    block_count = channels // block_ch
    last_section = section_count - 1
    turns = block_count + section_count - 1
    dx_init = jnp.zeros((channels, length), jnp.bfloat16)

    def advance(turn_idx, carried):
        incoming, dz_all, dx_store, tap_acc = carried
        block_id = turn_idx - (last_section - section_idx)
        active = (block_id >= 0) & (block_id < block_count)
        first_ch = jnp.clip(block_id, 0, block_count - 1) * block_ch
        from_next = take_rows(grad_chan, first_ch, block_ch, 0)
        grad_in = jnp.where(section_idx == last_section, from_next, incoming).astype(jnp.float32)
        feat_blk = take_rows(featured, first_ch, block_ch, 1).astype(jnp.float32)
        grad_z = grad_in * feat_blk[0]
        grad_q = grad_in * take_rows(convolved, first_ch, block_ch, 0)
        real_d, imag_d = forward_spectrum(grad_z, tables)
        real_c, imag_c = times_conj(
            take_rows(real_h, first_ch, block_ch, 0),
            take_rows(imag_h, first_ch, block_ch, 0),
            real_d,
            imag_d,
        )
        grad_w = inverse_signal(real_c, imag_c, tables)
        grad_all = jnp.stack([grad_q, grad_w * feat_blk[2], grad_w * feat_blk[1]])
        in_blk = transposed(grad_all, take_rows(own_taps, first_ch, block_ch, 2)).astype(
            jnp.bfloat16
        )
        tap_new = tap_grads(take_rows(x_padded, first_ch, block_ch, 0), grad_all)
        tap_acc = masked_write(tap_acc, tap_new, first_ch, active, 2)
        dz_all = masked_write(dz_all, grad_z, first_ch, active, 0)
        outgoing = shifted(in_blk, "section", -1)
        dx_store = masked_write(dx_store, in_blk, first_ch, active, 0)
        return (outgoing, dz_all, dx_store, tap_acc)

    start_state = (
        jnp.zeros((block_ch, length), jnp.bfloat16),
        jnp.zeros((channels, length), jnp.float32),
        dx_init,
        jnp.zeros((3, 7, channels), jnp.float32),
    )
    final_state = lax.fori_loop(0, turns, advance, start_state)
    dz_all = final_state[1]
    dx_store = final_state[2]
    tap_acc = final_state[3]
    real_d, imag_d = forward_spectrum(dz_all, tables)
    real_c, imag_c = times_conj(real_w, imag_w, real_d, imag_d)
    filter_grad = inverse_signal(real_c, imag_c, tables)
    in_rows = lax.all_to_all(dx_store, "ctx", split_axis=1, concat_axis=0, tiled=True)
    return (in_rows[None], filter_grad[None], tap_acc[None])


TAPS = 7
GROUP = 16
MESH = pl.DeviceIdType.MESH
F32 = jnp.float32
BF16 = jnp.bfloat16


def right_angle_tables(blocks_a, block_b):
    total_n = blocks_a * block_b
    first_k = np.arange(blocks_a)
    phase_one = 2 * np.pi * np.outer(first_k + 0.25, np.arange(blocks_a)) / blocks_a
    one = np.stack([np.cos(phase_one), -np.sin(phase_one)])
    first = np.einsum("rka,cd->rkcad", one, np.eye(GROUP))
    first = first.reshape(2 * blocks_a * GROUP, blocks_a * GROUP)
    points = first_k[:, None, None] + 0.25 + blocks_a * np.arange(block_b)[None, None, :]
    phase_two = 2 * np.pi * np.arange(block_b)[None, :, None] * points / total_n
    real, imag = np.cos(phase_two), -np.sin(phase_two)
    second = np.concatenate(
        [np.concatenate([real, imag], axis=2), np.concatenate([-imag, real], axis=2)], axis=1
    )
    return tuple(
        array.astype(ml_dtypes.bfloat16)
        for array in (first, first.T / total_n, second, second.transpose(0, 2, 1))
    )


def mixer_kernel(
    sections,
    x_hbm,
    og_hbm,
    filt_hbm,
    tap_ref,
    one_ref,
    one_inv_ref,
    two_ref,
    two_inv_ref,
    ig_out,
    fg_out,
    tg_out,
    x_ref,
    og_ref,
    filt_ref,
    xbuf,
    ogbuf,
    hbuf,
    tap_blk,
    tap_rows,
    tbuf,
    one_v,
    one_inv_v,
    two_v,
    two_inv_v,
    tapb,
    xs_ref,
    feat,
    sig,
    ybuf,
    spec,
    qbuf,
    cbuf,
    gwbuf,
    gbuf,
    igbuf,
    fgbuf,
    tgbuf,
    tgin,
    x_send,
    x_recv,
    og_send,
    og_recv,
    h_send,
    h_recv,
    t_send,
    t_recv,
    ig_send,
    ig_recv,
    fg_send,
    fg_recv,
    tg_send,
    tg_recv,
    table_sem,
    blk_sem,
    load_sem,
):
    sec = lax.axis_index("section")
    ctx = lax.axis_index("ctx")
    blocks = xbuf.shape[1]
    rows = xbuf.shape[2]
    lanes = xbuf.shape[3]
    groups = rows // GROUP
    other = 1 - sec

    tables = [
        pltpu.make_async_copy(src, dst, table_sem.at[n])
        for n, (src, dst) in enumerate(
            ((one_ref, one_v), (two_ref, two_v), (one_inv_ref, one_inv_v), (two_inv_ref, two_inv_v))
        )
    ]

    channels = sections * rows
    tap_first = ctx * channels
    tap_lane = pl.multiple_of(tap_first // lanes * lanes, lanes)
    tap_load = pltpu.make_async_copy(tap_ref.at[:, :, pl.ds(tap_lane, lanes)], tap_blk, blk_sem)
    tap_load.start()

    loads = [
        pltpu.make_async_copy(src, dst, load_sem.at[n])
        for n, (src, dst) in enumerate(((filt_hbm, filt_ref), (x_hbm, x_ref), (og_hbm, og_ref)))
    ]
    for load in loads:
        load.start()

    barrier = pltpu.get_barrier_semaphore()

    def greet(step, carry):
        to_ctx = lax.rem(ctx + step, blocks)
        pl.semaphore_signal(barrier, inc=1, device_id=(other, to_ctx), device_id_type=MESH)

        @pl.when(step > 0)
        def _():
            pl.semaphore_signal(barrier, inc=1, device_id=(sec, to_ctx), device_id_type=MESH)

        return carry

    lax.fori_loop(0, blocks, greet, 0, unroll=True)
    for table in tables:
        table.start()
    pl.semaphore_wait(barrier, sections * blocks - 1)

    def row_block(to_sec, to_ctx):
        return pl.ds(pl.multiple_of((to_ctx * sections + to_sec) * rows, rows), rows)

    def half(which):
        return pl.ds(pl.multiple_of(which * rows, rows), rows)

    def remote(src, dst, send_sem, recv_sem, to_sec, to_ctx):
        pltpu.make_async_remote_copy(
            src_ref=src,
            dst_ref=dst,
            send_sem=send_sem,
            recv_sem=recv_sem,
            device_id=(to_sec, to_ctx),
            device_id_type=MESH,
        ).start()

    def await_bytes(ref, sem):
        pltpu.make_async_copy(ref, ref, sem).wait()

    loads[0].wait()
    remote(filt_ref.at[half(other)], hbuf.at[sec], h_send, h_recv.at[1], other, ctx)
    pltpu.make_async_copy(filt_ref.at[half(sec)], hbuf.at[sec], h_recv.at[0]).start()

    def send_x(to_sec):
        def send(step, carry):
            to_ctx = lax.rem(ctx + step, blocks)
            src = x_ref.at[row_block(to_sec, to_ctx)]
            remote(src, xbuf.at[sec, ctx], x_send, x_recv.at[sec], to_sec, to_ctx)
            return carry

        return send

    loads[1].wait()
    pltpu.make_async_copy(
        x_ref.at[row_block(sec, ctx)], xbuf.at[sec, ctx], x_recv.at[sec]
    ).start()
    lax.fori_loop(1, blocks, send_x(sec), 0, unroll=True)
    lax.fori_loop(0, blocks, send_x(other), 0, unroll=True)

    def send_og(step, carry):
        to_ctx = lax.rem(ctx + step, blocks)
        remote(og_ref.at[row_block(sec, to_ctx)], ogbuf.at[ctx], og_send, og_recv, sec, to_ctx)
        return carry

    loads[2].wait()
    pltpu.make_async_copy(og_ref.at[row_block(sec, ctx)], ogbuf.at[ctx], og_recv).start()
    lax.fori_loop(1, blocks, send_og, 0, unroll=True)

    tap_load.wait()
    tap_rows[...] = jnp.zeros_like(tap_rows)
    tap_rows[pl.ds(0, 3 * TAPS)] = tap_blk[...].reshape(3 * TAPS, lanes)
    tap_rows[...] = tap_rows[...].T

    def tap_half(which):
        first = lax.rem(tap_first, lanes) + which * rows
        return tap_rows.at[pl.ds(pl.multiple_of(first, rows), rows)]

    remote(tap_half(other), tbuf.at[sec], t_send, t_recv.at[1], other, ctx)
    pltpu.make_async_copy(tap_half(sec), tbuf.at[sec], t_recv.at[0]).start()

    def rows_at(first):
        return pl.ds(first if isinstance(first, int) else pl.multiple_of(first, GROUP), GROUP)

    def stage_one(blocks_of, first_row):
        cols = jnp.concatenate(
            [blocks_of(g).reshape(blocks * GROUP, lanes) for g in range(groups)], axis=1
        )
        out = jnp.dot(one_v[...], cols, preferred_element_type=F32).astype(BF16)
        out = out.reshape(2, blocks, GROUP, groups * lanes)
        for g in range(groups):
            for part in range(2):
                ybuf[:, rows_at(first_row + g * GROUP), pl.ds(part * lanes, lanes)] = out[
                    part, :, :, g * lanes : (g + 1) * lanes
                ]

    def stage_two(k, first_row, count):
        return jnp.dot(ybuf[k, pl.ds(first_row, count)], two_v[k], preferred_element_type=F32)

    def each_point(body):
        def step(k, carry):
            body(k)
            return carry

        lax.fori_loop(0, blocks, step, 0, unroll=True)

    def product(left, right, conj):
        left_r, left_i = left[:, :lanes], left[:, lanes:]
        right_r, right_i = right[:, :lanes], right[:, lanes:]
        if conj:
            real = left_r * right_r + left_i * right_i
            imag = left_r * right_i - left_i * right_r
        else:
            real = left_r * right_r - left_i * right_i
            imag = left_r * right_i + left_i * right_r
        return jnp.concatenate([real, imag], axis=1).astype(BF16)

    def inverse_two(k, operand, slots):
        out = jnp.dot(operand, two_inv_v[k], preferred_element_type=F32).astype(BF16)
        for position, slot in enumerate(slots):
            for g in range(groups):
                first = (position * groups + g) * GROUP
                for part in range(2):
                    qbuf[slot, part, k, :, pl.ds(g * lanes, lanes)] = out[
                        first : first + GROUP, part * lanes : (part + 1) * lanes
                    ]

    def inverse_one(slot):
        out = jnp.dot(
            one_inv_v[...],
            qbuf[slot].reshape(2 * blocks * GROUP, groups * lanes),
            preferred_element_type=F32,
        )
        return out.reshape(blocks, GROUP, groups * lanes)

    lane = lax.broadcasted_iota(jnp.int32, (rows, lanes), 1)

    def features_of(layer):
        def body(a, before):
            window = xbuf[layer, a].astype(F32)
            sums = [None] * 3
            rolled = []
            for j in range(TAPS):
                if j == 0:
                    moved = window
                else:
                    turned = pltpu.roll(window, j, 1)
                    rolled.append(turned)
                    moved = jnp.where(lane < j, before[j - 1], turned)
                xs_ref[layer, j, a] = moved
                for i in range(3):
                    term = tapb[layer, i * TAPS + j] * moved
                    sums[i] = term if sums[i] is None else sums[i] + term
            rounded = [total.astype(BF16) for total in sums]
            for i in range(3):
                feat[layer, i, a] = rounded[i]
            sig[a] = (rounded[1].astype(F32) * rounded[2].astype(F32)).astype(BF16)
            return tuple(rolled)

        zero = jnp.zeros((rows, lanes), F32)
        lax.fori_loop(0, blocks, body, (zero,) * (TAPS - 1), unroll=2)

    pair = 2 * rows
    for place, layer in enumerate((sec, other)):
        first_row = pl.multiple_of(layer * pair, pair)
        if place == 0:
            tables[0].wait()
        await_bytes(hbuf.at[layer], h_recv.at[place])
        stage_one(
            lambda g: jnp.stack(
                [
                    hbuf[layer, pl.ds(g * GROUP, GROUP), pl.ds(a * lanes, lanes)]
                    for a in range(blocks)
                ]
            ),
            first_row,
        )
        await_bytes(tbuf.at[layer], t_recv.at[place])
        values = tbuf[layer]
        for n in range(3 * TAPS):
            tapb[layer, n] = jnp.broadcast_to(values[:, n : n + 1], (rows, lanes))
        await_bytes(xbuf.at[layer], x_recv.at[layer])
        features_of(layer)
        stage_one(lambda g: sig[:, pl.ds(g * GROUP, GROUP), :], first_row + rows)
        if place == 0:
            tables[1].wait()
            tables[2].wait()
            tables[3].wait()

        def mixed_point(k):
            both = stage_two(k, first_row, pair)
            spec[k, pl.ds(first_row, pair)] = both
            inverse_two(k, product(both[:rows], both[rows:], False), (0,))

        each_point(mixed_point)
        out = inverse_one(0)
        for g in range(groups):
            cbuf[layer, :, pl.ds(g * GROUP, GROUP), :] = out[:, :, g * lanes : (g + 1) * lanes]

    def send_home(layer, src, dst, send_sem, recv_sem):
        @pl.when(sec == layer)
        def _():
            pltpu.make_async_copy(src, dst, recv_sem).start()

        @pl.when(sec != layer)
        def _():
            remote(src, dst, send_sem, recv_sem, layer, ctx)

    def filter_grad_of(layer):
        out = inverse_one(1 + layer)
        for a in range(blocks):
            for g in range(groups):
                fgbuf[layer, pl.ds(g * GROUP, GROUP), pl.ds(a * lanes, lanes)] = out[
                    a, :, g * lanes : (g + 1) * lanes
                ].astype(BF16)
        send_home(layer, fgbuf.at[layer], fg_out.at[half(sec)], fg_send, fg_recv)

    for layer in range(sections - 1, -1, -1):
        if layer == sections - 1:
            await_bytes(ogbuf, og_recv)
            carried = ogbuf
        else:
            carried = igbuf.at[layer + 1]

        sig[...] = (carried[...].astype(F32) * feat[layer, 0].astype(F32)).astype(BF16)
        stage_one(lambda g: sig[:, pl.ds(g * GROUP, GROUP), :], 0)

        def grad_point(k):
            d_spec = stage_two(k, 0, rows)
            with_h = product(spec[k, pl.ds(layer * pair, rows)], d_spec, True)
            with_w = product(spec[k, pl.ds(layer * pair + rows, rows)], d_spec, True)
            inverse_two(k, jnp.concatenate([with_h, with_w], axis=0), (0, 1 + layer))

        each_point(grad_point)
        if layer == 0:
            filter_grad_of(layer)
        out = inverse_one(0)
        for g in range(groups):
            gwbuf[:, pl.ds(g * GROUP, GROUP), :] = out[:, :, g * lanes : (g + 1) * lanes]

        def transposed_at(step, after):
            a = blocks - 1 - step
            grad_w = gwbuf[a]
            grads = (
                carried[a].astype(F32) * cbuf[layer, a],
                grad_w * feat[layer, 2, a].astype(F32),
                grad_w * feat[layer, 1, a].astype(F32),
            )
            for i in range(3):
                gbuf[layer, i, a] = grads[i]
            total = None
            rolled = []
            for j in range(TAPS):
                part = tapb[layer, j] * grads[0]
                for i in range(1, 3):
                    part = part + tapb[layer, i * TAPS + j] * grads[i]
                if j == 0:
                    total = part
                else:
                    turned = pltpu.roll(part, lanes - j, 1)
                    rolled.append(turned)
                    total = total + jnp.where(lane < lanes - j, turned, after[j - 1])
            igbuf[layer, a] = total.astype(BF16)
            return tuple(rolled)

        zero = jnp.zeros((rows, lanes), F32)
        lax.fori_loop(0, blocks, transposed_at, (zero,) * (TAPS - 1), unroll=2)

        def send_ig(step, carry):
            to_ctx = lax.rem(ctx + step, blocks)
            dst = ig_out.at[row_block(sec, ctx)]
            remote(igbuf.at[layer, to_ctx], dst, ig_send, ig_recv, layer, to_ctx)
            return carry

        lax.fori_loop(1, blocks, send_ig, 0, unroll=True)
        send_home(layer, igbuf.at[layer, ctx], ig_out.at[row_block(sec, ctx)], ig_send, ig_recv)

        if layer == 0:
            for later in range(1, sections):
                filter_grad_of(later)

    for layer in range(sections - 1, -1, -1):
        for first in range(0, rows, 8):
            def add_taps(a, sums):
                grads = [gbuf[layer, i, a, pl.ds(first, 8)] for i in range(3)]
                new = []
                for j in range(TAPS):
                    moved = xs_ref[layer, j, a, pl.ds(first, 8)]
                    for i in range(3):
                        new.append(sums[j * 3 + i] + grads[i] * moved)
                return tuple(new)

            zero_8 = jnp.zeros((8, lanes), F32)
            sums = lax.fori_loop(0, blocks, add_taps, (zero_8,) * (3 * TAPS), unroll=4)
            lane_8 = lax.broadcasted_iota(jnp.int32, (8, lanes), 1)
            packed = zero_8
            for j in range(TAPS):
                for i in range(3):
                    column = jnp.sum(sums[j * 3 + i], axis=1, keepdims=True)
                    packed = jnp.where(lane_8 == i * TAPS + j, column, packed)
            tgbuf[layer, pl.ds(first, 8)] = packed
        send_home(layer, tgbuf.at[layer], tgin.at[half(sec)], tg_send, tg_recv)

    others = sections * blocks - 1
    await_bytes(x_ref.at[pl.ds(0, others * rows)], x_send)
    await_bytes(og_ref.at[pl.ds(0, (blocks - 1) * rows)], og_send)
    await_bytes(filt_ref.at[pl.ds(0, rows)], h_send)
    await_bytes(tbuf.at[0], t_send)
    await_bytes(ig_out.at[pl.ds(0, others * rows)], ig_send)
    await_bytes(fg_out.at[pl.ds(0, rows)], fg_send)
    await_bytes(tgbuf.at[0], tg_send)
    await_bytes(tgin, tg_recv)
    tg_out[...] = tgin[...].T[: 3 * TAPS].reshape(3 * TAPS, 1, channels)
    await_bytes(fg_out, fg_recv)
    await_bytes(ig_out, ig_recv)


def write_kernel(ig_ref, fg_ref, tg_ref, ig_out, fg_out, tg_out):
    ig_out[...] = ig_ref[...]
    fg_out[...] = fg_ref[...].astype(F32)
    tg_out[...] = tg_ref[...]


def kernel_shards(inputs, out_grad, filters, conv_taps):
    sections = lax.axis_size("section")
    blocks = lax.axis_size("ctx")
    _, depth, lanes = inputs.shape
    _, channels, length = filters.shape
    rows = channels // sections
    tables = right_angle_tables(blocks, lanes)
    taps = conv_taps.reshape(3 * TAPS, 1, depth)
    vmem = pltpu.VMEM
    dma = pltpu.SemaphoreType.DMA
    any_spec = pl.BlockSpec(memory_space=pl.ANY)
    hbm_spec = pl.BlockSpec(memory_space=pl.ANY)
    vmem_spec = pl.BlockSpec(memory_space=pltpu.VMEM)
    spectrum_rows = 2 * sections * rows
    in_grad, filter_grad, tap_sums = pl.pallas_call(
        functools.partial(mixer_kernel, sections),
        out_shape=(
            jax.ShapeDtypeStruct((depth, lanes), BF16),
            jax.ShapeDtypeStruct((channels, length), BF16),
            jax.ShapeDtypeStruct((3 * TAPS, 1, channels), F32),
        ),
        in_specs=[hbm_spec] * 8,
        out_specs=(any_spec, any_spec, vmem_spec),
        scratch_shapes=[
            vmem((depth, lanes), BF16),
            vmem((depth, lanes), BF16),
            vmem((channels, length), BF16),
            vmem((sections, blocks, rows, lanes), BF16),
            vmem((blocks, rows, lanes), BF16),
            vmem((sections, rows, length), BF16),
            vmem((3 * TAPS, 1, lanes), F32),
            vmem((lanes, lanes), F32),
            vmem((sections, rows, lanes), F32),
            vmem(tables[0].shape, BF16),
            vmem(tables[1].shape, BF16),
            vmem(tables[2].shape, BF16),
            vmem(tables[3].shape, BF16),
            vmem((sections, 3 * TAPS, rows, lanes), F32),
            vmem((sections, TAPS, blocks, rows, lanes), F32),
            vmem((sections, 3, blocks, rows, lanes), BF16),
            vmem((blocks, rows, lanes), BF16),
            vmem((blocks, spectrum_rows, 2 * lanes), BF16),
            vmem((blocks, spectrum_rows, 2 * lanes), F32),
            vmem((1 + sections, 2, blocks, GROUP, rows // GROUP * lanes), BF16),
            vmem((sections, blocks, rows, lanes), F32),
            vmem((blocks, rows, lanes), F32),
            vmem((sections, 3, blocks, rows, lanes), F32),
            vmem((sections, blocks, rows, lanes), BF16),
            vmem((sections, rows, length), BF16),
            vmem((sections, rows, lanes), F32),
            vmem((channels, lanes), F32),
            dma(()),
            dma((sections,)),
            dma(()),
            dma(()),
            dma(()),
            dma((2,)),
            dma(()),
            dma((2,)),
            dma(()),
            dma(()),
            dma(()),
            dma(()),
            dma(()),
            dma(()),
            dma((4,)),
            dma(()),
            dma((3,)),
        ],
        compiler_params=pltpu.CompilerParams(
            collective_id=0, has_side_effects=True, vmem_limit_bytes=58 * 2**20
        ),
    )(inputs[0], out_grad, filters[0], taps, *(jnp.asarray(table) for table in tables))
    in_grad, filter_grad, tap_grad = pl.pallas_call(
        write_kernel,
        out_shape=(
            jax.ShapeDtypeStruct(in_grad.shape, BF16),
            jax.ShapeDtypeStruct(filter_grad.shape, F32),
            jax.ShapeDtypeStruct(tap_sums.shape, F32),
        ),
        in_specs=[vmem_spec] * 3,
        out_specs=(vmem_spec,) * 3,
        compiler_params=pltpu.CompilerParams(vmem_limit_bytes=58 * 2**20),
    )(in_grad, filter_grad, tap_sums)
    return (in_grad[None], filter_grad[None], tap_grad.reshape(1, 3, TAPS, channels))


def solution(mesh):
    placed = (
        P("section", None, "ctx"),
        P(None, "ctx"),
        P("section", "ctx", None),
        P("section", None, None, None),
    )

    def run(inputs, out_grad, filters, conv_taps):
        sections, blocks = mesh.shape["section"], mesh.shape["ctx"]
        rows = filters.shape[1] // (sections * blocks)
        lanes = inputs.shape[2] // blocks
        fits = sections == 2 and rows % GROUP == 0 and lanes == 128 and lanes % (sections * rows) == 0
        return jax.shard_map(
            kernel_shards if fits else shards,
            mesh=mesh,
            in_specs=placed,
            out_specs=(
                P("section", None, "ctx"),
                P("section", "ctx", None),
                P("section", None, None, "ctx"),
            ),
            check_vma=False,
        )(inputs, out_grad, filters, conv_taps)

    return run
```

```python
import functools
import math

import jax
import jax.numpy as jnp
import ml_dtypes
import numpy as np
from jax import lax
from jax.experimental import pallas as pl
from jax.experimental.pallas import tpu as pltpu
from jax.sharding import PartitionSpec as P

PRECISE = lax.Precision.HIGH


def shifted(block, axis, distance):
    devices = range(lax.axis_size(axis))
    route = [(i - distance, i) for i in devices if i - distance in devices]
    return lax.ppermute(block, axis, route)


def angle_table(row_count, col_count, modulus):
    row_ids = lax.broadcasted_iota(jnp.int32, (row_count, col_count), 0)
    col_ids = lax.broadcasted_iota(jnp.int32, (row_count, col_count), 1)
    product_mod = row_ids * col_ids % modulus
    angles = product_mod.astype(jnp.float32) * (2.0 * math.pi / modulus)
    return (jnp.cos(angles), jnp.sin(angles))


def make_tables(blocks_a, block_b):
    half_a = blocks_a // 2
    total_n = blocks_a * block_b
    return (
        angle_table(blocks_a, half_a, blocks_a),
        angle_table(half_a, blocks_a, blocks_a),
        angle_table(blocks_a, block_b, total_n),
        angle_table(block_b, block_b, block_b),
    )


def forward_spectrum(signal, tables):
    cos_one, sin_one = tables[0]
    cos_tw, sin_tw = tables[2]
    cos_two, sin_two = tables[3]
    channels = signal.shape[0]
    half_a = cos_one.shape[1]
    block_b = cos_two.shape[0]
    shaped = signal.reshape(channels, half_a, block_b)
    real_y = jnp.einsum("ka,cab->ckb", cos_one, shaped, precision=PRECISE)
    imag_y = -jnp.einsum("ka,cab->ckb", sin_one, shaped, precision=PRECISE)
    real_z = real_y * cos_tw + imag_y * sin_tw
    imag_z = imag_y * cos_tw - real_y * sin_tw
    real_x = jnp.einsum("ckb,mb->ckm", real_z, cos_two, precision=PRECISE) + jnp.einsum(
        "ckb,mb->ckm", imag_z, sin_two, precision=PRECISE
    )
    imag_x = jnp.einsum("ckb,mb->ckm", imag_z, cos_two, precision=PRECISE) - jnp.einsum(
        "ckb,mb->ckm", real_z, sin_two, precision=PRECISE
    )
    return (real_x, imag_x)


def inverse_signal(real_x, imag_x, tables):
    cos_one, sin_one = tables[1]
    cos_tw, sin_tw = tables[2]
    cos_two, sin_two = tables[3]
    channels = real_x.shape[0]
    half_a = cos_one.shape[0]
    block_b = cos_two.shape[0]
    total_n = cos_one.shape[1] * block_b
    real_p = jnp.einsum("ckm,mb->ckb", real_x, cos_two, precision=PRECISE) - jnp.einsum(
        "ckm,mb->ckb", imag_x, sin_two, precision=PRECISE
    )
    imag_p = jnp.einsum("ckm,mb->ckb", real_x, sin_two, precision=PRECISE) + jnp.einsum(
        "ckm,mb->ckb", imag_x, cos_two, precision=PRECISE
    )
    real_q = real_p * cos_tw - imag_p * sin_tw
    imag_q = real_p * sin_tw + imag_p * cos_tw
    summed = jnp.einsum("ak,ckb->cab", cos_one, real_q, precision=PRECISE) - jnp.einsum(
        "ak,ckb->cab", sin_one, imag_q, precision=PRECISE
    )
    return summed.reshape(channels, half_a * block_b) / total_n


def times_conj(real_a, imag_a, real_b, imag_b):
    return (real_a * real_b + imag_a * imag_b, real_a * imag_b - imag_a * real_b)


def features(padded, weights, length):
    summed = jnp.zeros((3, padded.shape[0], length), jnp.float32)
    for offset in range(7):
        window = padded[:, 6 - offset : 6 - offset + length].astype(jnp.float32)
        summed = summed + weights[:, offset, :, None] * window[None]
    return summed.astype(jnp.bfloat16)


def transposed(grad_all, weights):
    length = grad_all.shape[2]
    padded = jnp.pad(grad_all, ((0, 0), (0, 0), (0, 6)))
    summed = jnp.zeros(grad_all.shape[1:], jnp.float32)
    for offset in range(7):
        summed = summed + jnp.sum(
            weights[:, offset, :, None] * padded[:, :, offset : offset + length], axis=0
        )
    return summed


def tap_grads(padded, grad_all):
    length = grad_all.shape[2]
    per_offset = []
    for offset in range(7):
        window = padded[:, 6 - offset : 6 - offset + length].astype(jnp.float32)
        per_offset.append(jnp.sum(grad_all * window[None], axis=2))
    return jnp.stack(per_offset, axis=1)


def take_rows(array, first_ch, count, axis_num):
    return lax.dynamic_slice_in_dim(array, first_ch, count, axis_num)


def masked_write(array, update, first_ch, active, axis_num):
    previous = lax.dynamic_slice_in_dim(array, first_ch, update.shape[axis_num], axis_num)
    return lax.dynamic_update_slice_in_dim(
        array, jnp.where(active, update, previous), first_ch, axis_num
    )


def shards(inputs, out_grad, filters, conv_taps):
    x_rows = inputs[0]
    tok_dev = x_rows.shape[1]
    section_count = lax.axis_size("section")
    section_idx = lax.axis_index("section")
    ctx_idx = lax.axis_index("ctx")
    weights = conv_taps[0]
    channels = filters.shape[1]
    length = filters.shape[2]
    blocks_a = 2 * length // tok_dev
    own_taps = lax.dynamic_slice_in_dim(weights, ctx_idx * channels, channels, 2)
    prior_cols = shifted(x_rows[:, tok_dev - 6 :], "ctx", 1)
    featured_rows = features(jnp.concatenate([prior_cols, x_rows], axis=1), weights, tok_dev)
    x_chan, featured, grad_chan = (
        lax.all_to_all(x_rows[None], "ctx", split_axis=1, concat_axis=2, tiled=True),
        lax.all_to_all(featured_rows, "ctx", split_axis=1, concat_axis=2, tiled=True),
        lax.all_to_all(out_grad[None], "ctx", split_axis=1, concat_axis=2, tiled=True),
    )
    x_chan = x_chan[0]
    x_padded = jnp.pad(x_chan, ((0, 0), (6, 0)))
    grad_chan = grad_chan[0]
    tables = make_tables(blocks_a, tok_dev)
    key_full = featured[1].astype(jnp.float32)
    mixed_kv = key_full * featured[2].astype(jnp.float32)
    real_h, imag_h = forward_spectrum(filters[0].astype(jnp.float32), tables)
    real_w, imag_w = forward_spectrum(mixed_kv, tables)
    convolved = inverse_signal(
        real_h * real_w - imag_h * imag_w, real_h * imag_w + imag_h * real_w, tables
    )
    block_ch = 2
    block_count = channels // block_ch
    last_section = section_count - 1
    turns = block_count + section_count - 1
    dx_init = jnp.zeros((channels, length), jnp.bfloat16)

    def advance(turn_idx, carried):
        incoming, dz_all, dx_store, tap_acc = carried
        block_id = turn_idx - (last_section - section_idx)
        active = (block_id >= 0) & (block_id < block_count)
        first_ch = jnp.clip(block_id, 0, block_count - 1) * block_ch
        from_next = take_rows(grad_chan, first_ch, block_ch, 0)
        grad_in = jnp.where(section_idx == last_section, from_next, incoming).astype(jnp.float32)
        feat_blk = take_rows(featured, first_ch, block_ch, 1).astype(jnp.float32)
        grad_z = grad_in * feat_blk[0]
        grad_q = grad_in * take_rows(convolved, first_ch, block_ch, 0)
        real_d, imag_d = forward_spectrum(grad_z, tables)
        real_c, imag_c = times_conj(
            take_rows(real_h, first_ch, block_ch, 0),
            take_rows(imag_h, first_ch, block_ch, 0),
            real_d,
            imag_d,
        )
        grad_w = inverse_signal(real_c, imag_c, tables)
        grad_all = jnp.stack([grad_q, grad_w * feat_blk[2], grad_w * feat_blk[1]])
        in_blk = transposed(grad_all, take_rows(own_taps, first_ch, block_ch, 2)).astype(
            jnp.bfloat16
        )
        tap_new = tap_grads(take_rows(x_padded, first_ch, block_ch, 0), grad_all)
        tap_acc = masked_write(tap_acc, tap_new, first_ch, active, 2)
        dz_all = masked_write(dz_all, grad_z, first_ch, active, 0)
        outgoing = shifted(in_blk, "section", -1)
        dx_store = masked_write(dx_store, in_blk, first_ch, active, 0)
        return (outgoing, dz_all, dx_store, tap_acc)

    start_state = (
        jnp.zeros((block_ch, length), jnp.bfloat16),
        jnp.zeros((channels, length), jnp.float32),
        dx_init,
        jnp.zeros((3, 7, channels), jnp.float32),
    )
    final_state = lax.fori_loop(0, turns, advance, start_state)
    dz_all = final_state[1]
    dx_store = final_state[2]
    tap_acc = final_state[3]
    real_d, imag_d = forward_spectrum(dz_all, tables)
    real_c, imag_c = times_conj(real_w, imag_w, real_d, imag_d)
    filter_grad = inverse_signal(real_c, imag_c, tables)
    in_rows = lax.all_to_all(dx_store, "ctx", split_axis=1, concat_axis=0, tiled=True)
    return (in_rows[None], filter_grad[None], tap_acc[None])


TAPS = 7
GROUP = 16
CHUNK = 4
MESH = pl.DeviceIdType.MESH
F32 = jnp.float32
BF16 = jnp.bfloat16


def right_angle_tables(blocks_a, block_b):
    total_n = blocks_a * block_b
    first_k = np.arange(blocks_a)
    phase_one = 2 * np.pi * np.outer(first_k + 0.25, np.arange(blocks_a)) / blocks_a
    one = np.stack([np.cos(phase_one), -np.sin(phase_one)])
    first = np.einsum("rka,cd->krcad", one, np.eye(GROUP))
    first = first.reshape(2 * blocks_a * GROUP, blocks_a * GROUP)
    phase_turn = 2 * np.pi * np.outer(first_k + 0.25, np.arange(block_b)) / total_n
    turn = np.stack([np.cos(phase_turn), -np.sin(phase_turn)])
    turn = np.repeat(turn[:, :, None, :], GROUP, axis=2).astype(np.float32)
    phase_two = 2 * np.pi * np.outer(np.arange(block_b), np.arange(block_b)) / block_b
    real, imag = np.cos(phase_two), -np.sin(phase_two)
    second = np.concatenate(
        [np.concatenate([real, imag], axis=1), np.concatenate([-imag, real], axis=1)], axis=0
    )
    rounded = [
        array.astype(ml_dtypes.bfloat16) for array in (first, first.T / total_n, second, second.T)
    ]
    return (*rounded, turn)


def mixer_kernel(
    sections,
    x_hbm,
    og_hbm,
    filt_hbm,
    tap_ref,
    one_ref,
    one_inv_ref,
    two_ref,
    two_inv_ref,
    turn_ref,
    ig_out,
    fg_out,
    tg_out,
    x_ref,
    og_ref,
    filt_ref,
    xbuf,
    ogbuf,
    hbuf,
    tap_blk,
    tap_rows,
    tbuf,
    one_v,
    one_inv_v,
    two_v,
    two_inv_v,
    turn_v,
    tapb,
    xs_ref,
    feat,
    sig,
    ybuf,
    spec,
    qbuf,
    cbuf,
    gwbuf,
    gbuf,
    igbuf,
    fgbuf,
    tgbuf,
    tgin,
    x_send,
    x_recv,
    og_send,
    og_recv,
    h_send,
    h_recv,
    t_send,
    t_recv,
    ig_send,
    ig_recv,
    fg_send,
    fg_recv,
    tg_send,
    tg_recv,
    table_sem,
    blk_sem,
    load_sem,
):
    sec = lax.axis_index("section")
    ctx = lax.axis_index("ctx")
    blocks = xbuf.shape[1]
    rows = xbuf.shape[2]
    lanes = xbuf.shape[3]
    groups = rows // GROUP
    other = 1 - sec

    tables = [
        pltpu.make_async_copy(src, dst, table_sem.at[n])
        for n, (src, dst) in enumerate(
            ((one_ref, one_v), (two_ref, two_v), (one_inv_ref, one_inv_v), (two_inv_ref, two_inv_v), (turn_ref, turn_v))
        )
    ]

    channels = sections * rows
    tap_first = ctx * channels
    tap_lane = pl.multiple_of(tap_first // lanes * lanes, lanes)
    tap_load = pltpu.make_async_copy(tap_ref.at[:, :, pl.ds(tap_lane, lanes)], tap_blk, blk_sem)
    tap_load.start()

    loads = [
        pltpu.make_async_copy(src, dst, load_sem.at[n])
        for n, (src, dst) in enumerate(((filt_hbm, filt_ref), (x_hbm, x_ref), (og_hbm, og_ref)))
    ]
    for load in loads:
        load.start()

    barrier = pltpu.get_barrier_semaphore()

    def greet(step, carry):
        to_ctx = lax.rem(ctx + step, blocks)
        pl.semaphore_signal(barrier, inc=1, device_id=(other, to_ctx), device_id_type=MESH)

        @pl.when(step > 0)
        def _():
            pl.semaphore_signal(barrier, inc=1, device_id=(sec, to_ctx), device_id_type=MESH)

        return carry

    lax.fori_loop(0, blocks, greet, 0, unroll=True)
    for table in tables:
        table.start()
    pl.semaphore_wait(barrier, sections * blocks - 1)

    def row_block(to_sec, to_ctx):
        return pl.ds(pl.multiple_of((to_ctx * sections + to_sec) * rows, rows), rows)

    def half(which):
        return pl.ds(pl.multiple_of(which * rows, rows), rows)

    def remote(src, dst, send_sem, recv_sem, to_sec, to_ctx):
        pltpu.make_async_remote_copy(
            src_ref=src,
            dst_ref=dst,
            send_sem=send_sem,
            recv_sem=recv_sem,
            device_id=(to_sec, to_ctx),
            device_id_type=MESH,
        ).start()

    def await_bytes(ref, sem):
        pltpu.make_async_copy(ref, ref, sem).wait()

    loads[0].wait()
    remote(filt_ref.at[half(other)], hbuf.at[sec], h_send, h_recv.at[1], other, ctx)
    pltpu.make_async_copy(filt_ref.at[half(sec)], hbuf.at[sec], h_recv.at[0]).start()

    def send_x(to_sec):
        def send(step, carry):
            to_ctx = lax.rem(ctx + step, blocks)
            src = x_ref.at[row_block(to_sec, to_ctx)]
            remote(src, xbuf.at[sec, ctx], x_send, x_recv.at[sec], to_sec, to_ctx)
            return carry

        return send

    loads[1].wait()
    pltpu.make_async_copy(
        x_ref.at[row_block(sec, ctx)], xbuf.at[sec, ctx], x_recv.at[sec]
    ).start()
    lax.fori_loop(1, blocks, send_x(sec), 0, unroll=True)
    lax.fori_loop(0, blocks, send_x(other), 0, unroll=True)

    def send_og(step, carry):
        to_ctx = lax.rem(ctx + step, blocks)
        remote(og_ref.at[row_block(sec, to_ctx)], ogbuf.at[ctx], og_send, og_recv, sec, to_ctx)
        return carry

    loads[2].wait()
    pltpu.make_async_copy(og_ref.at[row_block(sec, ctx)], ogbuf.at[ctx], og_recv).start()
    lax.fori_loop(1, blocks, send_og, 0, unroll=True)

    tap_load.wait()
    tap_rows[...] = jnp.zeros_like(tap_rows)
    tap_rows[pl.ds(0, 3 * TAPS)] = tap_blk[...].reshape(3 * TAPS, lanes)
    tap_rows[...] = tap_rows[...].T

    def tap_half(which):
        first = lax.rem(tap_first, lanes) + which * rows
        return tap_rows.at[pl.ds(pl.multiple_of(first, rows), rows)]

    remote(tap_half(other), tbuf.at[sec], t_send, t_recv.at[1], other, ctx)
    pltpu.make_async_copy(tap_half(sec), tbuf.at[sec], t_recv.at[0]).start()

    def rows_at(first):
        return pl.ds(first if isinstance(first, int) else pl.multiple_of(first, GROUP), GROUP)

    chunk_size = min(CHUNK, blocks)

    def each_chunk(body):
        def step(n, carry):
            body(pl.ds(n * chunk_size, chunk_size))
            return carry

        lax.fori_loop(0, blocks // chunk_size, step, 0, unroll=True)

    def stage_one(blocks_of, first_row):
        cols = jnp.concatenate(
            [blocks_of(g).reshape(blocks * GROUP, lanes) for g in range(groups)], axis=1
        )

        def chunk(ks):
            out = jnp.dot(
                one_v[pl.ds(ks.start * 2 * GROUP, ks.size * 2 * GROUP)],
                cols,
                preferred_element_type=F32,
            ).reshape(ks.size, 2, GROUP, groups * lanes)
            turn_r, turn_i = turn_v[0, ks], turn_v[1, ks]
            for g in range(groups):
                real = out[:, 0, :, g * lanes : (g + 1) * lanes]
                imag = out[:, 1, :, g * lanes : (g + 1) * lanes]
                where = rows_at(first_row + g * GROUP)
                ybuf[ks, where, pl.ds(0, lanes)] = (real * turn_r - imag * turn_i).astype(BF16)
                ybuf[ks, where, pl.ds(lanes, lanes)] = (real * turn_i + imag * turn_r).astype(BF16)

        each_chunk(chunk)

    def stage_two(ks, first_row, count):
        operand = ybuf[ks, pl.ds(first_row, count)].reshape(ks.size * count, 2 * lanes)
        out = jnp.dot(operand, two_v[...], preferred_element_type=F32)
        return out.reshape(ks.size, count, 2 * lanes)

    def product(left, right, conj):
        left_r, left_i = left[..., :lanes], left[..., lanes:]
        right_r, right_i = right[..., :lanes], right[..., lanes:]
        if conj:
            real = left_r * right_r + left_i * right_i
            imag = left_r * right_i - left_i * right_r
        else:
            real = left_r * right_r - left_i * right_i
            imag = left_r * right_i + left_i * right_r
        return jnp.concatenate([real, imag], axis=2).astype(BF16)

    def inverse_two(ks, operand, slot):
        count = operand.shape[1]
        out = jnp.dot(
            operand.reshape(ks.size * count, 2 * lanes), two_inv_v[...], preferred_element_type=F32
        ).reshape(ks.size, count, 2 * lanes)
        turn_r, turn_i = turn_v[0, ks], turn_v[1, ks]
        for g in range(groups):
            real = out[:, g * GROUP : (g + 1) * GROUP, :lanes]
            imag = out[:, g * GROUP : (g + 1) * GROUP, lanes:]
            where = pl.ds(g * lanes, lanes)
            qbuf[slot, ks, 0, :, where] = (real * turn_r + imag * turn_i).astype(BF16)
            qbuf[slot, ks, 1, :, where] = (imag * turn_r - real * turn_i).astype(BF16)

    def inverse_one(slot):
        out = jnp.dot(
            one_inv_v[...],
            qbuf[slot].reshape(2 * blocks * GROUP, groups * lanes),
            preferred_element_type=F32,
        )
        return out.reshape(blocks, GROUP, groups * lanes)

    lane = lax.broadcasted_iota(jnp.int32, (rows, lanes), 1)

    def features_of(layer):
        def body(a, before):
            window = xbuf[layer, a].astype(F32)
            sums = [None] * 3
            rolled = []
            for j in range(TAPS):
                if j == 0:
                    moved = window
                else:
                    turned = pltpu.roll(window, j, 1)
                    rolled.append(turned)
                    moved = jnp.where(lane < j, before[j - 1], turned)
                xs_ref[layer, j, a] = moved
                for i in range(3):
                    term = tapb[layer, i * TAPS + j] * moved
                    sums[i] = term if sums[i] is None else sums[i] + term
            rounded = [total.astype(BF16) for total in sums]
            for i in range(3):
                feat[layer, i, a] = rounded[i]
            sig[a] = (rounded[1].astype(F32) * rounded[2].astype(F32)).astype(BF16)
            return tuple(rolled)

        zero = jnp.zeros((rows, lanes), F32)
        lax.fori_loop(0, blocks, body, (zero,) * (TAPS - 1), unroll=2)

    pair = 2 * rows
    for place, layer in enumerate((sec, other)):
        first_row = pl.multiple_of(layer * pair, pair)
        if place == 0:
            tables[0].wait()
            tables[4].wait()
        await_bytes(hbuf.at[layer], h_recv.at[place])
        stage_one(
            lambda g: jnp.stack(
                [
                    hbuf[layer, pl.ds(g * GROUP, GROUP), pl.ds(a * lanes, lanes)]
                    for a in range(blocks)
                ]
            ),
            first_row,
        )
        await_bytes(tbuf.at[layer], t_recv.at[place])
        values = tbuf[layer]
        for n in range(3 * TAPS):
            tapb[layer, n] = jnp.broadcast_to(values[:, n : n + 1], (rows, lanes))
        await_bytes(xbuf.at[layer], x_recv.at[layer])
        features_of(layer)
        stage_one(lambda g: sig[:, pl.ds(g * GROUP, GROUP), :], first_row + rows)
        if place == 0:
            tables[1].wait()
            tables[2].wait()
            tables[3].wait()

        def mixed_points(ks):
            both = stage_two(ks, first_row, pair)
            spec[ks, pl.ds(first_row, pair)] = both
            inverse_two(ks, product(both[:, :rows], both[:, rows:], False), 0)

        each_chunk(mixed_points)
        out = inverse_one(0)
        for g in range(groups):
            cbuf[layer, :, pl.ds(g * GROUP, GROUP), :] = out[:, :, g * lanes : (g + 1) * lanes]

    def send_home(layer, src, dst, send_sem, recv_sem):
        @pl.when(sec == layer)
        def _():
            pltpu.make_async_copy(src, dst, recv_sem).start()

        @pl.when(sec != layer)
        def _():
            remote(src, dst, send_sem, recv_sem, layer, ctx)

    def filter_grad_of(layer):
        out = inverse_one(1 + layer)
        for a in range(blocks):
            for g in range(groups):
                fgbuf[layer, pl.ds(g * GROUP, GROUP), pl.ds(a * lanes, lanes)] = out[
                    a, :, g * lanes : (g + 1) * lanes
                ].astype(BF16)
        send_home(layer, fgbuf.at[layer], fg_out.at[half(sec)], fg_send, fg_recv)

    for layer in range(sections - 1, -1, -1):
        if layer == sections - 1:
            await_bytes(ogbuf, og_recv)
            carried = ogbuf
        else:
            carried = igbuf.at[layer + 1]

        sig[...] = (carried[...].astype(F32) * feat[layer, 0].astype(F32)).astype(BF16)
        stage_one(lambda g: sig[:, pl.ds(g * GROUP, GROUP), :], 0)

        def grad_points(ks):
            d_spec = stage_two(ks, 0, rows)
            with_h = product(spec[ks, pl.ds(layer * pair, rows)], d_spec, True)
            with_w = product(spec[ks, pl.ds(layer * pair + rows, rows)], d_spec, True)
            inverse_two(ks, with_h, 0)
            inverse_two(ks, with_w, 1 + layer)

        each_chunk(grad_points)
        if layer == 0:
            filter_grad_of(layer)
        out = inverse_one(0)
        for g in range(groups):
            gwbuf[:, pl.ds(g * GROUP, GROUP), :] = out[:, :, g * lanes : (g + 1) * lanes]

        def transposed_at(step, after):
            a = blocks - 1 - step
            grad_w = gwbuf[a]
            grads = (
                carried[a].astype(F32) * cbuf[layer, a],
                grad_w * feat[layer, 2, a].astype(F32),
                grad_w * feat[layer, 1, a].astype(F32),
            )
            for i in range(3):
                gbuf[layer, i, a] = grads[i]
            total = None
            rolled = []
            for j in range(TAPS):
                part = tapb[layer, j] * grads[0]
                for i in range(1, 3):
                    part = part + tapb[layer, i * TAPS + j] * grads[i]
                if j == 0:
                    total = part
                else:
                    turned = pltpu.roll(part, lanes - j, 1)
                    rolled.append(turned)
                    total = total + jnp.where(lane < lanes - j, turned, after[j - 1])
            igbuf[layer, a] = total.astype(BF16)
            return tuple(rolled)

        zero = jnp.zeros((rows, lanes), F32)
        lax.fori_loop(0, blocks, transposed_at, (zero,) * (TAPS - 1), unroll=2)

        def send_ig(step, carry):
            to_ctx = lax.rem(ctx + step, blocks)
            dst = ig_out.at[row_block(sec, ctx)]
            remote(igbuf.at[layer, to_ctx], dst, ig_send, ig_recv, layer, to_ctx)
            return carry

        lax.fori_loop(1, blocks, send_ig, 0, unroll=True)
        send_home(layer, igbuf.at[layer, ctx], ig_out.at[row_block(sec, ctx)], ig_send, ig_recv)

        if layer == 0:
            for later in range(1, sections):
                filter_grad_of(later)

    for layer in range(sections - 1, -1, -1):
        for first in range(0, rows, 8):
            def add_taps(a, sums):
                grads = [gbuf[layer, i, a, pl.ds(first, 8)] for i in range(3)]
                new = []
                for j in range(TAPS):
                    moved = xs_ref[layer, j, a, pl.ds(first, 8)]
                    for i in range(3):
                        new.append(sums[j * 3 + i] + grads[i] * moved)
                return tuple(new)

            zero_8 = jnp.zeros((8, lanes), F32)
            sums = lax.fori_loop(0, blocks, add_taps, (zero_8,) * (3 * TAPS), unroll=4)
            lane_8 = lax.broadcasted_iota(jnp.int32, (8, lanes), 1)
            packed = zero_8
            for j in range(TAPS):
                for i in range(3):
                    column = jnp.sum(sums[j * 3 + i], axis=1, keepdims=True)
                    packed = jnp.where(lane_8 == i * TAPS + j, column, packed)
            tgbuf[layer, pl.ds(first, 8)] = packed
        send_home(layer, tgbuf.at[layer], tgin.at[half(sec)], tg_send, tg_recv)

    others = sections * blocks - 1
    await_bytes(x_ref.at[pl.ds(0, others * rows)], x_send)
    await_bytes(og_ref.at[pl.ds(0, (blocks - 1) * rows)], og_send)
    await_bytes(filt_ref.at[pl.ds(0, rows)], h_send)
    await_bytes(tbuf.at[0], t_send)
    await_bytes(ig_out.at[pl.ds(0, others * rows)], ig_send)
    await_bytes(fg_out.at[pl.ds(0, rows)], fg_send)
    await_bytes(tgbuf.at[0], tg_send)
    await_bytes(tgin, tg_recv)
    tg_out[...] = tgin[...].T[: 3 * TAPS].reshape(3 * TAPS, 1, channels)
    await_bytes(fg_out, fg_recv)
    await_bytes(ig_out, ig_recv)


def write_kernel(ig_ref, fg_ref, tg_ref, ig_out, fg_out, tg_out):
    ig_out[...] = ig_ref[...]
    fg_out[...] = fg_ref[...].astype(F32)
    tg_out[...] = tg_ref[...]


def kernel_shards(inputs, out_grad, filters, conv_taps):
    sections = lax.axis_size("section")
    blocks = lax.axis_size("ctx")
    _, depth, lanes = inputs.shape
    _, channels, length = filters.shape
    rows = channels // sections
    tables = right_angle_tables(blocks, lanes)
    taps = conv_taps.reshape(3 * TAPS, 1, depth)
    vmem = pltpu.VMEM
    dma = pltpu.SemaphoreType.DMA
    any_spec = pl.BlockSpec(memory_space=pl.ANY)
    hbm_spec = pl.BlockSpec(memory_space=pl.ANY)
    vmem_spec = pl.BlockSpec(memory_space=pltpu.VMEM)
    spectrum_rows = 2 * sections * rows
    in_grad, filter_grad, tap_sums = pl.pallas_call(
        functools.partial(mixer_kernel, sections),
        out_shape=(
            jax.ShapeDtypeStruct((depth, lanes), BF16),
            jax.ShapeDtypeStruct((channels, length), BF16),
            jax.ShapeDtypeStruct((3 * TAPS, 1, channels), F32),
        ),
        in_specs=[hbm_spec] * 9,
        out_specs=(any_spec, any_spec, vmem_spec),
        scratch_shapes=[
            vmem((depth, lanes), BF16),
            vmem((depth, lanes), BF16),
            vmem((channels, length), BF16),
            vmem((sections, blocks, rows, lanes), BF16),
            vmem((blocks, rows, lanes), BF16),
            vmem((sections, rows, length), BF16),
            vmem((3 * TAPS, 1, lanes), F32),
            vmem((lanes, lanes), F32),
            vmem((sections, rows, lanes), F32),
            vmem(tables[0].shape, BF16),
            vmem(tables[1].shape, BF16),
            vmem(tables[2].shape, BF16),
            vmem(tables[3].shape, BF16),
            vmem(tables[4].shape, F32),
            vmem((sections, 3 * TAPS, rows, lanes), F32),
            vmem((sections, TAPS, blocks, rows, lanes), F32),
            vmem((sections, 3, blocks, rows, lanes), BF16),
            vmem((blocks, rows, lanes), BF16),
            vmem((blocks, spectrum_rows, 2 * lanes), BF16),
            vmem((blocks, spectrum_rows, 2 * lanes), F32),
            vmem((1 + sections, blocks, 2, GROUP, rows // GROUP * lanes), BF16),
            vmem((sections, blocks, rows, lanes), F32),
            vmem((blocks, rows, lanes), F32),
            vmem((sections, 3, blocks, rows, lanes), F32),
            vmem((sections, blocks, rows, lanes), BF16),
            vmem((sections, rows, length), BF16),
            vmem((sections, rows, lanes), F32),
            vmem((channels, lanes), F32),
            dma(()),
            dma((sections,)),
            dma(()),
            dma(()),
            dma(()),
            dma((2,)),
            dma(()),
            dma((2,)),
            dma(()),
            dma(()),
            dma(()),
            dma(()),
            dma(()),
            dma(()),
            dma((5,)),
            dma(()),
            dma((3,)),
        ],
        compiler_params=pltpu.CompilerParams(
            collective_id=0, has_side_effects=True, vmem_limit_bytes=58 * 2**20
        ),
    )(inputs[0], out_grad, filters[0], taps, *(jnp.asarray(table) for table in tables))
    in_grad, filter_grad, tap_grad = pl.pallas_call(
        write_kernel,
        out_shape=(
            jax.ShapeDtypeStruct(in_grad.shape, BF16),
            jax.ShapeDtypeStruct(filter_grad.shape, F32),
            jax.ShapeDtypeStruct(tap_sums.shape, F32),
        ),
        in_specs=[vmem_spec] * 3,
        out_specs=(vmem_spec,) * 3,
        compiler_params=pltpu.CompilerParams(vmem_limit_bytes=58 * 2**20),
    )(in_grad, filter_grad, tap_sums)
    return (in_grad[None], filter_grad[None], tap_grad.reshape(1, 3, TAPS, channels))


def solution(mesh):
    placed = (
        P("section", None, "ctx"),
        P(None, "ctx"),
        P("section", "ctx", None),
        P("section", None, None, None),
    )

    def run(inputs, out_grad, filters, conv_taps):
        sections, blocks = mesh.shape["section"], mesh.shape["ctx"]
        rows = filters.shape[1] // (sections * blocks)
        lanes = inputs.shape[2] // blocks
        fits = sections == 2 and rows % GROUP == 0 and lanes == 128 and lanes % (sections * rows) == 0
        return jax.shard_map(
            kernel_shards if fits else shards,
            mesh=mesh,
            in_specs=placed,
            out_specs=(
                P("section", None, "ctx"),
                P("section", "ctx", None),
                P("section", None, None, "ctx"),
            ),
            check_vma=False,
        )(inputs, out_grad, filters, conv_taps)

    return run
```

```python
import functools
import math

import jax
import jax.numpy as jnp
import ml_dtypes
import numpy as np
from jax import lax
from jax.experimental import pallas as pl
from jax.experimental.pallas import tpu as pltpu
from jax.sharding import PartitionSpec as P

PRECISE = lax.Precision.HIGH


def shifted(block, axis, distance):
    devices = range(lax.axis_size(axis))
    route = [(i - distance, i) for i in devices if i - distance in devices]
    return lax.ppermute(block, axis, route)


def angle_table(row_count, col_count, modulus):
    row_ids = lax.broadcasted_iota(jnp.int32, (row_count, col_count), 0)
    col_ids = lax.broadcasted_iota(jnp.int32, (row_count, col_count), 1)
    product_mod = row_ids * col_ids % modulus
    angles = product_mod.astype(jnp.float32) * (2.0 * math.pi / modulus)
    return (jnp.cos(angles), jnp.sin(angles))


def make_tables(blocks_a, block_b):
    half_a = blocks_a // 2
    total_n = blocks_a * block_b
    return (
        angle_table(blocks_a, half_a, blocks_a),
        angle_table(half_a, blocks_a, blocks_a),
        angle_table(blocks_a, block_b, total_n),
        angle_table(block_b, block_b, block_b),
    )


def forward_spectrum(signal, tables):
    cos_one, sin_one = tables[0]
    cos_tw, sin_tw = tables[2]
    cos_two, sin_two = tables[3]
    channels = signal.shape[0]
    half_a = cos_one.shape[1]
    block_b = cos_two.shape[0]
    shaped = signal.reshape(channels, half_a, block_b)
    real_y = jnp.einsum("ka,cab->ckb", cos_one, shaped, precision=PRECISE)
    imag_y = -jnp.einsum("ka,cab->ckb", sin_one, shaped, precision=PRECISE)
    real_z = real_y * cos_tw + imag_y * sin_tw
    imag_z = imag_y * cos_tw - real_y * sin_tw
    real_x = jnp.einsum("ckb,mb->ckm", real_z, cos_two, precision=PRECISE) + jnp.einsum(
        "ckb,mb->ckm", imag_z, sin_two, precision=PRECISE
    )
    imag_x = jnp.einsum("ckb,mb->ckm", imag_z, cos_two, precision=PRECISE) - jnp.einsum(
        "ckb,mb->ckm", real_z, sin_two, precision=PRECISE
    )
    return (real_x, imag_x)


def inverse_signal(real_x, imag_x, tables):
    cos_one, sin_one = tables[1]
    cos_tw, sin_tw = tables[2]
    cos_two, sin_two = tables[3]
    channels = real_x.shape[0]
    half_a = cos_one.shape[0]
    block_b = cos_two.shape[0]
    total_n = cos_one.shape[1] * block_b
    real_p = jnp.einsum("ckm,mb->ckb", real_x, cos_two, precision=PRECISE) - jnp.einsum(
        "ckm,mb->ckb", imag_x, sin_two, precision=PRECISE
    )
    imag_p = jnp.einsum("ckm,mb->ckb", real_x, sin_two, precision=PRECISE) + jnp.einsum(
        "ckm,mb->ckb", imag_x, cos_two, precision=PRECISE
    )
    real_q = real_p * cos_tw - imag_p * sin_tw
    imag_q = real_p * sin_tw + imag_p * cos_tw
    summed = jnp.einsum("ak,ckb->cab", cos_one, real_q, precision=PRECISE) - jnp.einsum(
        "ak,ckb->cab", sin_one, imag_q, precision=PRECISE
    )
    return summed.reshape(channels, half_a * block_b) / total_n


def times_conj(real_a, imag_a, real_b, imag_b):
    return (real_a * real_b + imag_a * imag_b, real_a * imag_b - imag_a * real_b)


def features(padded, weights, length):
    summed = jnp.zeros((3, padded.shape[0], length), jnp.float32)
    for offset in range(7):
        window = padded[:, 6 - offset : 6 - offset + length].astype(jnp.float32)
        summed = summed + weights[:, offset, :, None] * window[None]
    return summed.astype(jnp.bfloat16)


def transposed(grad_all, weights):
    length = grad_all.shape[2]
    padded = jnp.pad(grad_all, ((0, 0), (0, 0), (0, 6)))
    summed = jnp.zeros(grad_all.shape[1:], jnp.float32)
    for offset in range(7):
        summed = summed + jnp.sum(
            weights[:, offset, :, None] * padded[:, :, offset : offset + length], axis=0
        )
    return summed


def tap_grads(padded, grad_all):
    length = grad_all.shape[2]
    per_offset = []
    for offset in range(7):
        window = padded[:, 6 - offset : 6 - offset + length].astype(jnp.float32)
        per_offset.append(jnp.sum(grad_all * window[None], axis=2))
    return jnp.stack(per_offset, axis=1)


def take_rows(array, first_ch, count, axis_num):
    return lax.dynamic_slice_in_dim(array, first_ch, count, axis_num)


def masked_write(array, update, first_ch, active, axis_num):
    previous = lax.dynamic_slice_in_dim(array, first_ch, update.shape[axis_num], axis_num)
    return lax.dynamic_update_slice_in_dim(
        array, jnp.where(active, update, previous), first_ch, axis_num
    )


def shards(inputs, out_grad, filters, conv_taps):
    x_rows = inputs[0]
    tok_dev = x_rows.shape[1]
    section_count = lax.axis_size("section")
    section_idx = lax.axis_index("section")
    ctx_idx = lax.axis_index("ctx")
    weights = conv_taps[0]
    channels = filters.shape[1]
    length = filters.shape[2]
    blocks_a = 2 * length // tok_dev
    own_taps = lax.dynamic_slice_in_dim(weights, ctx_idx * channels, channels, 2)
    prior_cols = shifted(x_rows[:, tok_dev - 6 :], "ctx", 1)
    featured_rows = features(jnp.concatenate([prior_cols, x_rows], axis=1), weights, tok_dev)
    x_chan, featured, grad_chan = (
        lax.all_to_all(x_rows[None], "ctx", split_axis=1, concat_axis=2, tiled=True),
        lax.all_to_all(featured_rows, "ctx", split_axis=1, concat_axis=2, tiled=True),
        lax.all_to_all(out_grad[None], "ctx", split_axis=1, concat_axis=2, tiled=True),
    )
    x_chan = x_chan[0]
    x_padded = jnp.pad(x_chan, ((0, 0), (6, 0)))
    grad_chan = grad_chan[0]
    tables = make_tables(blocks_a, tok_dev)
    key_full = featured[1].astype(jnp.float32)
    mixed_kv = key_full * featured[2].astype(jnp.float32)
    real_h, imag_h = forward_spectrum(filters[0].astype(jnp.float32), tables)
    real_w, imag_w = forward_spectrum(mixed_kv, tables)
    convolved = inverse_signal(
        real_h * real_w - imag_h * imag_w, real_h * imag_w + imag_h * real_w, tables
    )
    block_ch = 2
    block_count = channels // block_ch
    last_section = section_count - 1
    turns = block_count + section_count - 1
    dx_init = jnp.zeros((channels, length), jnp.bfloat16)

    def advance(turn_idx, carried):
        incoming, dz_all, dx_store, tap_acc = carried
        block_id = turn_idx - (last_section - section_idx)
        active = (block_id >= 0) & (block_id < block_count)
        first_ch = jnp.clip(block_id, 0, block_count - 1) * block_ch
        from_next = take_rows(grad_chan, first_ch, block_ch, 0)
        grad_in = jnp.where(section_idx == last_section, from_next, incoming).astype(jnp.float32)
        feat_blk = take_rows(featured, first_ch, block_ch, 1).astype(jnp.float32)
        grad_z = grad_in * feat_blk[0]
        grad_q = grad_in * take_rows(convolved, first_ch, block_ch, 0)
        real_d, imag_d = forward_spectrum(grad_z, tables)
        real_c, imag_c = times_conj(
            take_rows(real_h, first_ch, block_ch, 0),
            take_rows(imag_h, first_ch, block_ch, 0),
            real_d,
            imag_d,
        )
        grad_w = inverse_signal(real_c, imag_c, tables)
        grad_all = jnp.stack([grad_q, grad_w * feat_blk[2], grad_w * feat_blk[1]])
        in_blk = transposed(grad_all, take_rows(own_taps, first_ch, block_ch, 2)).astype(
            jnp.bfloat16
        )
        tap_new = tap_grads(take_rows(x_padded, first_ch, block_ch, 0), grad_all)
        tap_acc = masked_write(tap_acc, tap_new, first_ch, active, 2)
        dz_all = masked_write(dz_all, grad_z, first_ch, active, 0)
        outgoing = shifted(in_blk, "section", -1)
        dx_store = masked_write(dx_store, in_blk, first_ch, active, 0)
        return (outgoing, dz_all, dx_store, tap_acc)

    start_state = (
        jnp.zeros((block_ch, length), jnp.bfloat16),
        jnp.zeros((channels, length), jnp.float32),
        dx_init,
        jnp.zeros((3, 7, channels), jnp.float32),
    )
    final_state = lax.fori_loop(0, turns, advance, start_state)
    dz_all = final_state[1]
    dx_store = final_state[2]
    tap_acc = final_state[3]
    real_d, imag_d = forward_spectrum(dz_all, tables)
    real_c, imag_c = times_conj(real_w, imag_w, real_d, imag_d)
    filter_grad = inverse_signal(real_c, imag_c, tables)
    in_rows = lax.all_to_all(dx_store, "ctx", split_axis=1, concat_axis=0, tiled=True)
    return (in_rows[None], filter_grad[None], tap_acc[None])


TAPS = 7
GROUP = 16
CHUNK = 4
MESH = pl.DeviceIdType.MESH
F32 = jnp.float32
BF16 = jnp.bfloat16


def right_angle_tables(blocks_a, block_b):
    total_n = blocks_a * block_b
    first_k = np.arange(blocks_a)
    phase_one = 2 * np.pi * np.outer(first_k + 0.25, np.arange(blocks_a)) / blocks_a
    one = np.stack([np.cos(phase_one), -np.sin(phase_one)])
    first = np.einsum("rka,cd->krcad", one, np.eye(GROUP))
    first = first.reshape(2 * blocks_a * GROUP, blocks_a * GROUP)
    phase_turn = 2 * np.pi * np.outer(first_k + 0.25, np.arange(block_b)) / total_n
    turn = np.stack([np.cos(phase_turn), -np.sin(phase_turn)])
    turn = np.repeat(turn[:, :, None, :], GROUP, axis=2).astype(np.float32)
    phase_two = 2 * np.pi * np.outer(np.arange(block_b), np.arange(block_b)) / block_b
    real, imag = np.cos(phase_two), -np.sin(phase_two)
    second = np.concatenate(
        [np.concatenate([real, imag], axis=1), np.concatenate([-imag, real], axis=1)], axis=0
    )
    rounded = [
        array.astype(ml_dtypes.bfloat16) for array in (first, first.T / total_n, second, second.T)
    ]
    return (*rounded, turn)


def mixer_kernel(
    sections,
    x_hbm,
    og_hbm,
    filt_hbm,
    tap_ref,
    one_ref,
    one_inv_ref,
    two_ref,
    two_inv_ref,
    turn_ref,
    ig_out,
    fg_out,
    tg_out,
    x_ref,
    og_ref,
    filt_ref,
    xbuf,
    ogbuf,
    hbuf,
    tap_blk,
    tap_rows,
    tbuf,
    one_v,
    one_inv_v,
    two_v,
    two_inv_v,
    turn_v,
    tapb,
    xs_ref,
    feat,
    sig,
    ybuf,
    spec,
    qbuf,
    cbuf,
    gwbuf,
    gbuf,
    igbuf,
    fgbuf,
    tgbuf,
    tgin,
    x_send,
    x_recv,
    og_send,
    og_recv,
    h_send,
    h_recv,
    t_send,
    t_recv,
    ig_send,
    ig_recv,
    fg_send,
    fg_recv,
    tg_send,
    tg_recv,
    table_sem,
    blk_sem,
    load_sem,
):
    sec = lax.axis_index("section")
    ctx = lax.axis_index("ctx")
    blocks = xbuf.shape[1]
    rows = xbuf.shape[2]
    lanes = xbuf.shape[3]
    groups = rows // GROUP
    other = 1 - sec

    tables = [
        pltpu.make_async_copy(src, dst, table_sem.at[n])
        for n, (src, dst) in enumerate(
            ((one_ref, one_v), (two_ref, two_v), (one_inv_ref, one_inv_v), (two_inv_ref, two_inv_v), (turn_ref, turn_v))
        )
    ]

    channels = sections * rows
    tap_first = ctx * channels
    tap_lane = pl.multiple_of(tap_first // lanes * lanes, lanes)
    tap_load = pltpu.make_async_copy(tap_ref.at[:, :, pl.ds(tap_lane, lanes)], tap_blk, blk_sem)
    tap_load.start()

    loads = [
        pltpu.make_async_copy(src, dst, load_sem.at[n])
        for n, (src, dst) in enumerate(((filt_hbm, filt_ref), (x_hbm, x_ref), (og_hbm, og_ref)))
    ]
    for load in loads:
        load.start()

    barrier = pltpu.get_barrier_semaphore()

    def greet(step, carry):
        to_ctx = lax.rem(ctx + step, blocks)
        pl.semaphore_signal(barrier, inc=1, device_id=(other, to_ctx), device_id_type=MESH)

        @pl.when(step > 0)
        def _():
            pl.semaphore_signal(barrier, inc=1, device_id=(sec, to_ctx), device_id_type=MESH)

        return carry

    lax.fori_loop(0, blocks, greet, 0, unroll=True)
    for table in tables:
        table.start()
    pl.semaphore_wait(barrier, sections * blocks - 1)

    def row_block(to_sec, to_ctx):
        return pl.ds(pl.multiple_of((to_ctx * sections + to_sec) * rows, rows), rows)

    def half(which):
        return pl.ds(pl.multiple_of(which * rows, rows), rows)

    def remote(src, dst, send_sem, recv_sem, to_sec, to_ctx):
        pltpu.make_async_remote_copy(
            src_ref=src,
            dst_ref=dst,
            send_sem=send_sem,
            recv_sem=recv_sem,
            device_id=(to_sec, to_ctx),
            device_id_type=MESH,
        ).start()

    def await_bytes(ref, sem):
        pltpu.make_async_copy(ref, ref, sem).wait()

    loads[0].wait()
    remote(filt_ref.at[half(other)], hbuf.at[sec], h_send, h_recv.at[1], other, ctx)
    pltpu.make_async_copy(filt_ref.at[half(sec)], hbuf.at[sec], h_recv.at[0]).start()

    def partner(step):
        return lax.rem(ctx + 1 + lax.rem(ctx * max(1, blocks // 4) + step, blocks - 1), blocks)

    def send_x(to_sec):
        def send(step, carry):
            to_ctx = partner(step)
            src = x_ref.at[row_block(to_sec, to_ctx)]
            remote(src, xbuf.at[sec, ctx], x_send, x_recv.at[sec], to_sec, to_ctx)
            return carry

        return send

    loads[1].wait()
    pltpu.make_async_copy(
        x_ref.at[row_block(sec, ctx)], xbuf.at[sec, ctx], x_recv.at[sec]
    ).start()
    lax.fori_loop(0, blocks - 1, send_x(sec), 0, unroll=True)
    lax.fori_loop(0, blocks - 1, send_x(other), 0, unroll=True)
    remote(
        x_ref.at[row_block(other, ctx)], xbuf.at[sec, ctx], x_send, x_recv.at[sec], other, ctx
    )

    def send_og(step, carry):
        to_ctx = partner(step)
        remote(og_ref.at[row_block(sec, to_ctx)], ogbuf.at[ctx], og_send, og_recv, sec, to_ctx)
        return carry

    loads[2].wait()
    pltpu.make_async_copy(og_ref.at[row_block(sec, ctx)], ogbuf.at[ctx], og_recv).start()
    lax.fori_loop(0, blocks - 1, send_og, 0, unroll=True)

    tap_load.wait()
    tap_rows[...] = jnp.zeros_like(tap_rows)
    tap_rows[pl.ds(0, 3 * TAPS)] = tap_blk[...].reshape(3 * TAPS, lanes)
    tap_rows[...] = tap_rows[...].T

    def tap_half(which):
        first = lax.rem(tap_first, lanes) + which * rows
        return tap_rows.at[pl.ds(pl.multiple_of(first, rows), rows)]

    remote(tap_half(other), tbuf.at[sec], t_send, t_recv.at[1], other, ctx)
    pltpu.make_async_copy(tap_half(sec), tbuf.at[sec], t_recv.at[0]).start()

    def rows_at(first):
        return pl.ds(first if isinstance(first, int) else pl.multiple_of(first, GROUP), GROUP)

    chunk_size = min(CHUNK, blocks)

    def each_chunk(body):
        def step(n, carry):
            body(pl.ds(n * chunk_size, chunk_size))
            return carry

        lax.fori_loop(0, blocks // chunk_size, step, 0, unroll=True)

    def stage_one(blocks_of, first_row):
        cols = jnp.concatenate(
            [blocks_of(g).reshape(blocks * GROUP, lanes) for g in range(groups)], axis=1
        )

        def chunk(ks):
            out = jnp.dot(
                one_v[pl.ds(ks.start * 2 * GROUP, ks.size * 2 * GROUP)],
                cols,
                preferred_element_type=F32,
            ).reshape(ks.size, 2, GROUP, groups * lanes)
            turn_r, turn_i = turn_v[0, ks], turn_v[1, ks]
            for g in range(groups):
                real = out[:, 0, :, g * lanes : (g + 1) * lanes]
                imag = out[:, 1, :, g * lanes : (g + 1) * lanes]
                where = rows_at(first_row + g * GROUP)
                ybuf[ks, where, pl.ds(0, lanes)] = (real * turn_r - imag * turn_i).astype(BF16)
                ybuf[ks, where, pl.ds(lanes, lanes)] = (real * turn_i + imag * turn_r).astype(BF16)

        each_chunk(chunk)

    def stage_two(ks, first_row, count):
        operand = ybuf[ks, pl.ds(first_row, count)].reshape(ks.size * count, 2 * lanes)
        out = jnp.dot(operand, two_v[...], preferred_element_type=F32)
        return out.reshape(ks.size, count, 2 * lanes)

    def product(left, right, conj):
        left_r, left_i = left[..., :lanes], left[..., lanes:]
        right_r, right_i = right[..., :lanes], right[..., lanes:]
        if conj:
            real = left_r * right_r + left_i * right_i
            imag = left_r * right_i - left_i * right_r
        else:
            real = left_r * right_r - left_i * right_i
            imag = left_r * right_i + left_i * right_r
        return jnp.concatenate([real, imag], axis=2).astype(BF16)

    def inverse_two(ks, operand, slot):
        count = operand.shape[1]
        out = jnp.dot(
            operand.reshape(ks.size * count, 2 * lanes), two_inv_v[...], preferred_element_type=F32
        ).reshape(ks.size, count, 2 * lanes)
        turn_r, turn_i = turn_v[0, ks], turn_v[1, ks]
        for g in range(groups):
            real = out[:, g * GROUP : (g + 1) * GROUP, :lanes]
            imag = out[:, g * GROUP : (g + 1) * GROUP, lanes:]
            where = pl.ds(g * lanes, lanes)
            qbuf[slot, ks, 0, :, where] = (real * turn_r + imag * turn_i).astype(BF16)
            qbuf[slot, ks, 1, :, where] = (imag * turn_r - real * turn_i).astype(BF16)

    def inverse_one(slot):
        out = jnp.dot(
            one_inv_v[...],
            qbuf[slot].reshape(2 * blocks * GROUP, groups * lanes),
            preferred_element_type=F32,
        )
        return out.reshape(blocks, GROUP, groups * lanes)

    lane = lax.broadcasted_iota(jnp.int32, (rows, lanes), 1)

    def features_of(layer):
        def body(a, before):
            window = xbuf[layer, a].astype(F32)
            sums = [None] * 3
            rolled = []
            for j in range(TAPS):
                if j == 0:
                    moved = window
                else:
                    turned = pltpu.roll(window, j, 1)
                    rolled.append(turned)
                    moved = jnp.where(lane < j, before[j - 1], turned)
                xs_ref[layer, j, a] = moved
                for i in range(3):
                    term = tapb[layer, i * TAPS + j] * moved
                    sums[i] = term if sums[i] is None else sums[i] + term
            rounded = [total.astype(BF16) for total in sums]
            for i in range(3):
                feat[layer, i, a] = rounded[i]
            sig[a] = (rounded[1].astype(F32) * rounded[2].astype(F32)).astype(BF16)
            return tuple(rolled)

        zero = jnp.zeros((rows, lanes), F32)
        lax.fori_loop(0, blocks, body, (zero,) * (TAPS - 1), unroll=2)

    pair = 2 * rows
    for place, layer in enumerate((sec, other)):
        first_row = pl.multiple_of(layer * pair, pair)
        if place == 0:
            tables[0].wait()
            tables[4].wait()
        await_bytes(hbuf.at[layer], h_recv.at[place])
        stage_one(
            lambda g: jnp.stack(
                [
                    hbuf[layer, pl.ds(g * GROUP, GROUP), pl.ds(a * lanes, lanes)]
                    for a in range(blocks)
                ]
            ),
            first_row,
        )
        await_bytes(tbuf.at[layer], t_recv.at[place])
        values = tbuf[layer]
        for n in range(3 * TAPS):
            tapb[layer, n] = jnp.broadcast_to(values[:, n : n + 1], (rows, lanes))
        await_bytes(xbuf.at[layer], x_recv.at[layer])
        features_of(layer)
        stage_one(lambda g: sig[:, pl.ds(g * GROUP, GROUP), :], first_row + rows)
        if place == 0:
            tables[1].wait()
            tables[2].wait()
            tables[3].wait()

        def mixed_points(ks):
            both = stage_two(ks, first_row, pair)
            spec[ks, pl.ds(first_row, pair)] = both
            inverse_two(ks, product(both[:, :rows], both[:, rows:], False), 0)

        each_chunk(mixed_points)
        out = inverse_one(0)
        for g in range(groups):
            cbuf[layer, :, pl.ds(g * GROUP, GROUP), :] = out[:, :, g * lanes : (g + 1) * lanes]

    def send_home(layer, src, dst, send_sem, recv_sem):
        @pl.when(sec == layer)
        def _():
            pltpu.make_async_copy(src, dst, recv_sem).start()

        @pl.when(sec != layer)
        def _():
            remote(src, dst, send_sem, recv_sem, layer, ctx)

    def filter_grad_of(layer):
        out = inverse_one(1 + layer)
        for a in range(blocks):
            for g in range(groups):
                fgbuf[layer, pl.ds(g * GROUP, GROUP), pl.ds(a * lanes, lanes)] = out[
                    a, :, g * lanes : (g + 1) * lanes
                ].astype(BF16)
        send_home(layer, fgbuf.at[layer], fg_out.at[half(sec)], fg_send, fg_recv)

    for layer in range(sections - 1, -1, -1):
        if layer == sections - 1:
            await_bytes(ogbuf, og_recv)
            carried = ogbuf
        else:
            carried = igbuf.at[layer + 1]

        sig[...] = (carried[...].astype(F32) * feat[layer, 0].astype(F32)).astype(BF16)
        stage_one(lambda g: sig[:, pl.ds(g * GROUP, GROUP), :], 0)

        def grad_points(ks):
            d_spec = stage_two(ks, 0, rows)
            with_h = product(spec[ks, pl.ds(layer * pair, rows)], d_spec, True)
            with_w = product(spec[ks, pl.ds(layer * pair + rows, rows)], d_spec, True)
            inverse_two(ks, with_h, 0)
            inverse_two(ks, with_w, 1 + layer)

        each_chunk(grad_points)
        if layer == 0:
            filter_grad_of(layer)
        out = inverse_one(0)
        for g in range(groups):
            gwbuf[:, pl.ds(g * GROUP, GROUP), :] = out[:, :, g * lanes : (g + 1) * lanes]

        def transposed_at(step, after):
            a = blocks - 1 - step
            grad_w = gwbuf[a]
            grads = (
                carried[a].astype(F32) * cbuf[layer, a],
                grad_w * feat[layer, 2, a].astype(F32),
                grad_w * feat[layer, 1, a].astype(F32),
            )
            for i in range(3):
                gbuf[layer, i, a] = grads[i]
            total = None
            rolled = []
            for j in range(TAPS):
                part = tapb[layer, j] * grads[0]
                for i in range(1, 3):
                    part = part + tapb[layer, i * TAPS + j] * grads[i]
                if j == 0:
                    total = part
                else:
                    turned = pltpu.roll(part, lanes - j, 1)
                    rolled.append(turned)
                    total = total + jnp.where(lane < lanes - j, turned, after[j - 1])
            igbuf[layer, a] = total.astype(BF16)
            return tuple(rolled)

        zero = jnp.zeros((rows, lanes), F32)
        lax.fori_loop(0, blocks, transposed_at, (zero,) * (TAPS - 1), unroll=2)

        def send_ig(step, carry):
            to_ctx = partner(step)
            dst = ig_out.at[row_block(sec, ctx)]
            remote(igbuf.at[layer, to_ctx], dst, ig_send, ig_recv, layer, to_ctx)
            return carry

        lax.fori_loop(0, blocks - 1, send_ig, 0, unroll=True)
        send_home(layer, igbuf.at[layer, ctx], ig_out.at[row_block(sec, ctx)], ig_send, ig_recv)

        if layer == 0:
            for later in range(1, sections):
                filter_grad_of(later)

    for layer in range(sections - 1, -1, -1):
        for first in range(0, rows, 8):
            def add_taps(a, sums):
                grads = [gbuf[layer, i, a, pl.ds(first, 8)] for i in range(3)]
                new = []
                for j in range(TAPS):
                    moved = xs_ref[layer, j, a, pl.ds(first, 8)]
                    for i in range(3):
                        new.append(sums[j * 3 + i] + grads[i] * moved)
                return tuple(new)

            zero_8 = jnp.zeros((8, lanes), F32)
            sums = lax.fori_loop(0, blocks, add_taps, (zero_8,) * (3 * TAPS), unroll=4)
            lane_8 = lax.broadcasted_iota(jnp.int32, (8, lanes), 1)
            packed = zero_8
            for j in range(TAPS):
                for i in range(3):
                    column = jnp.sum(sums[j * 3 + i], axis=1, keepdims=True)
                    packed = jnp.where(lane_8 == i * TAPS + j, column, packed)
            tgbuf[layer, pl.ds(first, 8)] = packed
        send_home(layer, tgbuf.at[layer], tgin.at[half(sec)], tg_send, tg_recv)

    others = sections * blocks - 1
    await_bytes(x_ref.at[pl.ds(0, others * rows)], x_send)
    await_bytes(og_ref.at[pl.ds(0, (blocks - 1) * rows)], og_send)
    await_bytes(filt_ref.at[pl.ds(0, rows)], h_send)
    await_bytes(tbuf.at[0], t_send)
    await_bytes(ig_out.at[pl.ds(0, others * rows)], ig_send)
    await_bytes(fg_out.at[pl.ds(0, rows)], fg_send)
    await_bytes(tgbuf.at[0], tg_send)
    await_bytes(tgin, tg_recv)
    tg_out[...] = tgin[...].T[: 3 * TAPS].reshape(3 * TAPS, 1, channels)
    await_bytes(fg_out, fg_recv)
    await_bytes(ig_out, ig_recv)


def write_kernel(ig_ref, fg_ref, tg_ref, ig_out, fg_out, tg_out):
    ig_out[...] = ig_ref[...]
    fg_out[...] = fg_ref[...].astype(F32)
    tg_out[...] = tg_ref[...]


def kernel_shards(inputs, out_grad, filters, conv_taps):
    sections = lax.axis_size("section")
    blocks = lax.axis_size("ctx")
    _, depth, lanes = inputs.shape
    _, channels, length = filters.shape
    rows = channels // sections
    tables = right_angle_tables(blocks, lanes)
    taps = conv_taps.reshape(3 * TAPS, 1, depth)
    vmem = pltpu.VMEM
    dma = pltpu.SemaphoreType.DMA
    any_spec = pl.BlockSpec(memory_space=pl.ANY)
    hbm_spec = pl.BlockSpec(memory_space=pl.ANY)
    vmem_spec = pl.BlockSpec(memory_space=pltpu.VMEM)
    spectrum_rows = 2 * sections * rows
    in_grad, filter_grad, tap_sums = pl.pallas_call(
        functools.partial(mixer_kernel, sections),
        out_shape=(
            jax.ShapeDtypeStruct((depth, lanes), BF16),
            jax.ShapeDtypeStruct((channels, length), BF16),
            jax.ShapeDtypeStruct((3 * TAPS, 1, channels), F32),
        ),
        in_specs=[hbm_spec] * 9,
        out_specs=(any_spec, any_spec, vmem_spec),
        scratch_shapes=[
            vmem((depth, lanes), BF16),
            vmem((depth, lanes), BF16),
            vmem((channels, length), BF16),
            vmem((sections, blocks, rows, lanes), BF16),
            vmem((blocks, rows, lanes), BF16),
            vmem((sections, rows, length), BF16),
            vmem((3 * TAPS, 1, lanes), F32),
            vmem((lanes, lanes), F32),
            vmem((sections, rows, lanes), F32),
            vmem(tables[0].shape, BF16),
            vmem(tables[1].shape, BF16),
            vmem(tables[2].shape, BF16),
            vmem(tables[3].shape, BF16),
            vmem(tables[4].shape, F32),
            vmem((sections, 3 * TAPS, rows, lanes), F32),
            vmem((sections, TAPS, blocks, rows, lanes), F32),
            vmem((sections, 3, blocks, rows, lanes), BF16),
            vmem((blocks, rows, lanes), BF16),
            vmem((blocks, spectrum_rows, 2 * lanes), BF16),
            vmem((blocks, spectrum_rows, 2 * lanes), F32),
            vmem((1 + sections, blocks, 2, GROUP, rows // GROUP * lanes), BF16),
            vmem((sections, blocks, rows, lanes), F32),
            vmem((blocks, rows, lanes), F32),
            vmem((sections, 3, blocks, rows, lanes), F32),
            vmem((sections, blocks, rows, lanes), BF16),
            vmem((sections, rows, length), BF16),
            vmem((sections, rows, lanes), F32),
            vmem((channels, lanes), F32),
            dma(()),
            dma((sections,)),
            dma(()),
            dma(()),
            dma(()),
            dma((2,)),
            dma(()),
            dma((2,)),
            dma(()),
            dma(()),
            dma(()),
            dma(()),
            dma(()),
            dma(()),
            dma((5,)),
            dma(()),
            dma((3,)),
        ],
        compiler_params=pltpu.CompilerParams(
            collective_id=0, has_side_effects=True, vmem_limit_bytes=58 * 2**20
        ),
    )(inputs[0], out_grad, filters[0], taps, *(jnp.asarray(table) for table in tables))
    in_grad, filter_grad, tap_grad = pl.pallas_call(
        write_kernel,
        out_shape=(
            jax.ShapeDtypeStruct(in_grad.shape, BF16),
            jax.ShapeDtypeStruct(filter_grad.shape, F32),
            jax.ShapeDtypeStruct(tap_sums.shape, F32),
        ),
        in_specs=[vmem_spec] * 3,
        out_specs=(vmem_spec,) * 3,
        compiler_params=pltpu.CompilerParams(vmem_limit_bytes=58 * 2**20),
    )(in_grad, filter_grad, tap_sums)
    return (in_grad[None], filter_grad[None], tap_grad.reshape(1, 3, TAPS, channels))


def solution(mesh):
    placed = (
        P("section", None, "ctx"),
        P(None, "ctx"),
        P("section", "ctx", None),
        P("section", None, None, None),
    )

    def run(inputs, out_grad, filters, conv_taps):
        sections, blocks = mesh.shape["section"], mesh.shape["ctx"]
        rows = filters.shape[1] // (sections * blocks)
        lanes = inputs.shape[2] // blocks
        fits = sections == 2 and rows % GROUP == 0 and lanes == 128 and lanes % (sections * rows) == 0
        return jax.shard_map(
            kernel_shards if fits else shards,
            mesh=mesh,
            in_specs=placed,
            out_specs=(
                P("section", None, "ctx"),
                P("section", "ctx", None),
                P("section", None, None, "ctx"),
            ),
            check_vma=False,
        )(inputs, out_grad, filters, conv_taps)

    return run
```

```python
import functools
import math

import jax
import jax.numpy as jnp
import ml_dtypes
import numpy as np
from jax import lax
from jax.experimental import pallas as pl
from jax.experimental.pallas import tpu as pltpu
from jax.sharding import PartitionSpec as P

PRECISE = lax.Precision.HIGH


def shifted(block, axis, distance):
    devices = range(lax.axis_size(axis))
    route = [(i - distance, i) for i in devices if i - distance in devices]
    return lax.ppermute(block, axis, route)


def angle_table(row_count, col_count, modulus):
    row_ids = lax.broadcasted_iota(jnp.int32, (row_count, col_count), 0)
    col_ids = lax.broadcasted_iota(jnp.int32, (row_count, col_count), 1)
    product_mod = row_ids * col_ids % modulus
    angles = product_mod.astype(jnp.float32) * (2.0 * math.pi / modulus)
    return (jnp.cos(angles), jnp.sin(angles))


def make_tables(blocks_a, block_b):
    half_a = blocks_a // 2
    total_n = blocks_a * block_b
    return (
        angle_table(blocks_a, half_a, blocks_a),
        angle_table(half_a, blocks_a, blocks_a),
        angle_table(blocks_a, block_b, total_n),
        angle_table(block_b, block_b, block_b),
    )


def forward_spectrum(signal, tables):
    cos_one, sin_one = tables[0]
    cos_tw, sin_tw = tables[2]
    cos_two, sin_two = tables[3]
    channels = signal.shape[0]
    half_a = cos_one.shape[1]
    block_b = cos_two.shape[0]
    shaped = signal.reshape(channels, half_a, block_b)
    real_y = jnp.einsum("ka,cab->ckb", cos_one, shaped, precision=PRECISE)
    imag_y = -jnp.einsum("ka,cab->ckb", sin_one, shaped, precision=PRECISE)
    real_z = real_y * cos_tw + imag_y * sin_tw
    imag_z = imag_y * cos_tw - real_y * sin_tw
    real_x = jnp.einsum("ckb,mb->ckm", real_z, cos_two, precision=PRECISE) + jnp.einsum(
        "ckb,mb->ckm", imag_z, sin_two, precision=PRECISE
    )
    imag_x = jnp.einsum("ckb,mb->ckm", imag_z, cos_two, precision=PRECISE) - jnp.einsum(
        "ckb,mb->ckm", real_z, sin_two, precision=PRECISE
    )
    return (real_x, imag_x)


def inverse_signal(real_x, imag_x, tables):
    cos_one, sin_one = tables[1]
    cos_tw, sin_tw = tables[2]
    cos_two, sin_two = tables[3]
    channels = real_x.shape[0]
    half_a = cos_one.shape[0]
    block_b = cos_two.shape[0]
    total_n = cos_one.shape[1] * block_b
    real_p = jnp.einsum("ckm,mb->ckb", real_x, cos_two, precision=PRECISE) - jnp.einsum(
        "ckm,mb->ckb", imag_x, sin_two, precision=PRECISE
    )
    imag_p = jnp.einsum("ckm,mb->ckb", real_x, sin_two, precision=PRECISE) + jnp.einsum(
        "ckm,mb->ckb", imag_x, cos_two, precision=PRECISE
    )
    real_q = real_p * cos_tw - imag_p * sin_tw
    imag_q = real_p * sin_tw + imag_p * cos_tw
    summed = jnp.einsum("ak,ckb->cab", cos_one, real_q, precision=PRECISE) - jnp.einsum(
        "ak,ckb->cab", sin_one, imag_q, precision=PRECISE
    )
    return summed.reshape(channels, half_a * block_b) / total_n


def times_conj(real_a, imag_a, real_b, imag_b):
    return (real_a * real_b + imag_a * imag_b, real_a * imag_b - imag_a * real_b)


def features(padded, weights, length):
    summed = jnp.zeros((3, padded.shape[0], length), jnp.float32)
    for offset in range(7):
        window = padded[:, 6 - offset : 6 - offset + length].astype(jnp.float32)
        summed = summed + weights[:, offset, :, None] * window[None]
    return summed.astype(jnp.bfloat16)


def transposed(grad_all, weights):
    length = grad_all.shape[2]
    padded = jnp.pad(grad_all, ((0, 0), (0, 0), (0, 6)))
    summed = jnp.zeros(grad_all.shape[1:], jnp.float32)
    for offset in range(7):
        summed = summed + jnp.sum(
            weights[:, offset, :, None] * padded[:, :, offset : offset + length], axis=0
        )
    return summed


def tap_grads(padded, grad_all):
    length = grad_all.shape[2]
    per_offset = []
    for offset in range(7):
        window = padded[:, 6 - offset : 6 - offset + length].astype(jnp.float32)
        per_offset.append(jnp.sum(grad_all * window[None], axis=2))
    return jnp.stack(per_offset, axis=1)


def take_rows(array, first_ch, count, axis_num):
    return lax.dynamic_slice_in_dim(array, first_ch, count, axis_num)


def masked_write(array, update, first_ch, active, axis_num):
    previous = lax.dynamic_slice_in_dim(array, first_ch, update.shape[axis_num], axis_num)
    return lax.dynamic_update_slice_in_dim(
        array, jnp.where(active, update, previous), first_ch, axis_num
    )


def shards(inputs, out_grad, filters, conv_taps):
    x_rows = inputs[0]
    tok_dev = x_rows.shape[1]
    section_count = lax.axis_size("section")
    section_idx = lax.axis_index("section")
    ctx_idx = lax.axis_index("ctx")
    weights = conv_taps[0]
    channels = filters.shape[1]
    length = filters.shape[2]
    blocks_a = 2 * length // tok_dev
    own_taps = lax.dynamic_slice_in_dim(weights, ctx_idx * channels, channels, 2)
    prior_cols = shifted(x_rows[:, tok_dev - 6 :], "ctx", 1)
    featured_rows = features(jnp.concatenate([prior_cols, x_rows], axis=1), weights, tok_dev)
    x_chan, featured, grad_chan = (
        lax.all_to_all(x_rows[None], "ctx", split_axis=1, concat_axis=2, tiled=True),
        lax.all_to_all(featured_rows, "ctx", split_axis=1, concat_axis=2, tiled=True),
        lax.all_to_all(out_grad[None], "ctx", split_axis=1, concat_axis=2, tiled=True),
    )
    x_chan = x_chan[0]
    x_padded = jnp.pad(x_chan, ((0, 0), (6, 0)))
    grad_chan = grad_chan[0]
    tables = make_tables(blocks_a, tok_dev)
    key_full = featured[1].astype(jnp.float32)
    mixed_kv = key_full * featured[2].astype(jnp.float32)
    real_h, imag_h = forward_spectrum(filters[0].astype(jnp.float32), tables)
    real_w, imag_w = forward_spectrum(mixed_kv, tables)
    convolved = inverse_signal(
        real_h * real_w - imag_h * imag_w, real_h * imag_w + imag_h * real_w, tables
    )
    block_ch = 2
    block_count = channels // block_ch
    last_section = section_count - 1
    turns = block_count + section_count - 1
    dx_init = jnp.zeros((channels, length), jnp.bfloat16)

    def advance(turn_idx, carried):
        incoming, dz_all, dx_store, tap_acc = carried
        block_id = turn_idx - (last_section - section_idx)
        active = (block_id >= 0) & (block_id < block_count)
        first_ch = jnp.clip(block_id, 0, block_count - 1) * block_ch
        from_next = take_rows(grad_chan, first_ch, block_ch, 0)
        grad_in = jnp.where(section_idx == last_section, from_next, incoming).astype(jnp.float32)
        feat_blk = take_rows(featured, first_ch, block_ch, 1).astype(jnp.float32)
        grad_z = grad_in * feat_blk[0]
        grad_q = grad_in * take_rows(convolved, first_ch, block_ch, 0)
        real_d, imag_d = forward_spectrum(grad_z, tables)
        real_c, imag_c = times_conj(
            take_rows(real_h, first_ch, block_ch, 0),
            take_rows(imag_h, first_ch, block_ch, 0),
            real_d,
            imag_d,
        )
        grad_w = inverse_signal(real_c, imag_c, tables)
        grad_all = jnp.stack([grad_q, grad_w * feat_blk[2], grad_w * feat_blk[1]])
        in_blk = transposed(grad_all, take_rows(own_taps, first_ch, block_ch, 2)).astype(
            jnp.bfloat16
        )
        tap_new = tap_grads(take_rows(x_padded, first_ch, block_ch, 0), grad_all)
        tap_acc = masked_write(tap_acc, tap_new, first_ch, active, 2)
        dz_all = masked_write(dz_all, grad_z, first_ch, active, 0)
        outgoing = shifted(in_blk, "section", -1)
        dx_store = masked_write(dx_store, in_blk, first_ch, active, 0)
        return (outgoing, dz_all, dx_store, tap_acc)

    start_state = (
        jnp.zeros((block_ch, length), jnp.bfloat16),
        jnp.zeros((channels, length), jnp.float32),
        dx_init,
        jnp.zeros((3, 7, channels), jnp.float32),
    )
    final_state = lax.fori_loop(0, turns, advance, start_state)
    dz_all = final_state[1]
    dx_store = final_state[2]
    tap_acc = final_state[3]
    real_d, imag_d = forward_spectrum(dz_all, tables)
    real_c, imag_c = times_conj(real_w, imag_w, real_d, imag_d)
    filter_grad = inverse_signal(real_c, imag_c, tables)
    in_rows = lax.all_to_all(dx_store, "ctx", split_axis=1, concat_axis=0, tiled=True)
    return (in_rows[None], filter_grad[None], tap_acc[None])


TAPS = 7
GROUP = 16
CHUNK = 4
MESH = pl.DeviceIdType.MESH
F32 = jnp.float32
BF16 = jnp.bfloat16


def right_angle_tables(blocks_a, block_b):
    total_n = blocks_a * block_b
    first_k = np.arange(blocks_a)
    phase_one = 2 * np.pi * np.outer(first_k + 0.25, np.arange(blocks_a)) / blocks_a
    one = np.stack([np.cos(phase_one), -np.sin(phase_one)])
    first = np.einsum("rka,cd->krcad", one, np.eye(GROUP))
    first = first.reshape(2 * blocks_a * GROUP, blocks_a * GROUP)
    phase_turn = 2 * np.pi * np.outer(first_k + 0.25, np.arange(block_b)) / total_n
    turn = np.stack([np.cos(phase_turn), -np.sin(phase_turn)])
    turn = np.repeat(turn[:, :, None, :], GROUP, axis=2).astype(np.float32)
    phase_two = 2 * np.pi * np.outer(np.arange(block_b), np.arange(block_b)) / block_b
    real, imag = np.cos(phase_two), -np.sin(phase_two)
    second = np.concatenate(
        [np.concatenate([real, imag], axis=1), np.concatenate([-imag, real], axis=1)], axis=0
    )
    rounded = [
        array.astype(ml_dtypes.bfloat16) for array in (first, first.T / total_n, second, second.T)
    ]
    return (*rounded, turn)


def mixer_kernel(
    sections,
    x_hbm,
    og_hbm,
    filt_hbm,
    tap_ref,
    one_ref,
    one_inv_ref,
    two_ref,
    two_inv_ref,
    turn_ref,
    ig_out,
    fg_out,
    tg_out,
    x_ref,
    og_ref,
    filt_ref,
    xbuf,
    ogbuf,
    hbuf,
    tap_blk,
    tap_rows,
    tbuf,
    one_v,
    one_inv_v,
    two_v,
    two_inv_v,
    turn_v,
    tapb,
    xs_ref,
    feat,
    sig,
    ybuf,
    spec,
    qbuf,
    cbuf,
    gwbuf,
    gbuf,
    igbuf,
    fgbuf,
    tgbuf,
    tgin,
    x_send,
    x_recv,
    og_send,
    og_recv,
    h_send,
    h_recv,
    t_send,
    t_recv,
    ig_send,
    ig_recv,
    fg_send,
    fg_recv,
    tg_send,
    tg_recv,
    table_sem,
    blk_sem,
    load_sem,
):
    sec = lax.axis_index("section")
    ctx = lax.axis_index("ctx")
    blocks = xbuf.shape[1]
    rows = xbuf.shape[2]
    lanes = xbuf.shape[3]
    groups = rows // GROUP
    other = 1 - sec

    tables = [
        pltpu.make_async_copy(src, dst, table_sem.at[n])
        for n, (src, dst) in enumerate(
            ((one_ref, one_v), (two_ref, two_v), (one_inv_ref, one_inv_v), (two_inv_ref, two_inv_v), (turn_ref, turn_v))
        )
    ]

    channels = sections * rows
    tap_first = ctx * channels
    tap_lane = pl.multiple_of(tap_first // lanes * lanes, lanes)
    tap_load = pltpu.make_async_copy(tap_ref.at[:, :, pl.ds(tap_lane, lanes)], tap_blk, blk_sem)
    tap_load.start()

    loads = [
        pltpu.make_async_copy(src, dst, load_sem.at[n])
        for n, (src, dst) in enumerate(((filt_hbm, filt_ref), (x_hbm, x_ref), (og_hbm, og_ref)))
    ]
    for load in loads:
        load.start()

    barrier = pltpu.get_barrier_semaphore()

    def greet(step, carry):
        to_ctx = lax.rem(ctx + step, blocks)
        pl.semaphore_signal(barrier, inc=1, device_id=(other, to_ctx), device_id_type=MESH)

        @pl.when(step > 0)
        def _():
            pl.semaphore_signal(barrier, inc=1, device_id=(sec, to_ctx), device_id_type=MESH)

        return carry

    lax.fori_loop(0, blocks, greet, 0, unroll=True)
    for table in tables:
        table.start()
    pl.semaphore_wait(barrier, sections * blocks - 1)

    def row_block(to_sec, to_ctx):
        return pl.ds(pl.multiple_of((to_ctx * sections + to_sec) * rows, rows), rows)

    def half(which):
        return pl.ds(pl.multiple_of(which * rows, rows), rows)

    def remote(src, dst, send_sem, recv_sem, to_sec, to_ctx):
        pltpu.make_async_remote_copy(
            src_ref=src,
            dst_ref=dst,
            send_sem=send_sem,
            recv_sem=recv_sem,
            device_id=(to_sec, to_ctx),
            device_id_type=MESH,
        ).start()

    def await_bytes(ref, sem):
        pltpu.make_async_copy(ref, ref, sem).wait()

    loads[0].wait()
    remote(filt_ref.at[half(other)], hbuf.at[sec], h_send, h_recv.at[1], other, ctx)
    pltpu.make_async_copy(filt_ref.at[half(sec)], hbuf.at[sec], h_recv.at[0]).start()

    def send_x(to_sec):
        def send(step, carry):
            to_ctx = lax.rem(ctx + step, blocks)
            src = x_ref.at[row_block(to_sec, to_ctx)]
            remote(src, xbuf.at[sec, ctx], x_send, x_recv.at[sec], to_sec, to_ctx)
            return carry

        return send

    loads[1].wait()
    pltpu.make_async_copy(
        x_ref.at[row_block(sec, ctx)], xbuf.at[sec, ctx], x_recv.at[sec]
    ).start()
    lax.fori_loop(1, blocks, send_x(sec), 0, unroll=True)
    lax.fori_loop(0, blocks, send_x(other), 0, unroll=True)

    def send_og(step, carry):
        to_ctx = lax.rem(ctx + step, blocks)
        remote(og_ref.at[row_block(sec, to_ctx)], ogbuf.at[ctx], og_send, og_recv, sec, to_ctx)
        return carry

    loads[2].wait()
    pltpu.make_async_copy(og_ref.at[row_block(sec, ctx)], ogbuf.at[ctx], og_recv).start()
    lax.fori_loop(1, blocks, send_og, 0, unroll=True)

    tap_load.wait()
    tap_rows[...] = jnp.zeros_like(tap_rows)
    tap_rows[pl.ds(0, 3 * TAPS)] = tap_blk[...].reshape(3 * TAPS, lanes)
    tap_rows[...] = tap_rows[...].T

    def tap_half(which):
        first = lax.rem(tap_first, lanes) + which * rows
        return tap_rows.at[pl.ds(pl.multiple_of(first, rows), rows)]

    remote(tap_half(other), tbuf.at[sec], t_send, t_recv.at[1], other, ctx)
    pltpu.make_async_copy(tap_half(sec), tbuf.at[sec], t_recv.at[0]).start()

    def rows_at(first):
        return pl.ds(first if isinstance(first, int) else pl.multiple_of(first, GROUP), GROUP)

    chunk_size = min(CHUNK, blocks)

    def each_chunk(body):
        def step(n, carry):
            body(pl.ds(n * chunk_size, chunk_size))
            return carry

        lax.fori_loop(0, blocks // chunk_size, step, 0, unroll=True)

    def stage_one(blocks_of, first_row):
        cols = jnp.concatenate(
            [blocks_of(g).reshape(blocks * GROUP, lanes) for g in range(groups)], axis=1
        )

        def chunk(ks):
            out = jnp.dot(
                one_v[pl.ds(ks.start * 2 * GROUP, ks.size * 2 * GROUP)],
                cols,
                preferred_element_type=F32,
            ).reshape(ks.size, 2, GROUP, groups * lanes)
            turn_r, turn_i = turn_v[0, ks], turn_v[1, ks]
            for g in range(groups):
                real = out[:, 0, :, g * lanes : (g + 1) * lanes]
                imag = out[:, 1, :, g * lanes : (g + 1) * lanes]
                where = rows_at(first_row + g * GROUP)
                ybuf[ks, where, pl.ds(0, lanes)] = (real * turn_r - imag * turn_i).astype(BF16)
                ybuf[ks, where, pl.ds(lanes, lanes)] = (real * turn_i + imag * turn_r).astype(BF16)

        each_chunk(chunk)

    def stage_two(ks, first_row, count):
        operand = ybuf[ks, pl.ds(first_row, count)].reshape(ks.size * count, 2 * lanes)
        out = jnp.dot(operand, two_v[...], preferred_element_type=F32)
        return out.reshape(ks.size, count, 2 * lanes)

    def product(left, right, conj):
        left_r, left_i = left[..., :lanes], left[..., lanes:]
        right_r, right_i = right[..., :lanes], right[..., lanes:]
        if conj:
            real = left_r * right_r + left_i * right_i
            imag = left_r * right_i - left_i * right_r
        else:
            real = left_r * right_r - left_i * right_i
            imag = left_r * right_i + left_i * right_r
        return jnp.concatenate([real, imag], axis=2).astype(BF16)

    def inverse_two(ks, operand, slot):
        count = operand.shape[1]
        out = jnp.dot(
            operand.reshape(ks.size * count, 2 * lanes), two_inv_v[...], preferred_element_type=F32
        ).reshape(ks.size, count, 2 * lanes)
        turn_r, turn_i = turn_v[0, ks], turn_v[1, ks]
        for g in range(groups):
            real = out[:, g * GROUP : (g + 1) * GROUP, :lanes]
            imag = out[:, g * GROUP : (g + 1) * GROUP, lanes:]
            where = pl.ds(g * lanes, lanes)
            qbuf[slot, ks, 0, :, where] = (real * turn_r + imag * turn_i).astype(BF16)
            qbuf[slot, ks, 1, :, where] = (imag * turn_r - real * turn_i).astype(BF16)

    def inverse_one(slot):
        out = jnp.dot(
            one_inv_v[...],
            qbuf[slot].reshape(2 * blocks * GROUP, groups * lanes),
            preferred_element_type=F32,
        )
        return out.reshape(blocks, GROUP, groups * lanes)

    lane = lax.broadcasted_iota(jnp.int32, (rows, lanes), 1)

    def features_of(layer):
        def body(a, before):
            window = xbuf[layer, a].astype(F32)
            sums = [None] * 3
            rolled = []
            for j in range(TAPS):
                if j == 0:
                    moved = window
                else:
                    turned = pltpu.roll(window, j, 1)
                    rolled.append(turned)
                    moved = jnp.where(lane < j, before[j - 1], turned)
                xs_ref[layer, j, a] = moved
                for i in range(3):
                    term = tapb[layer, i * TAPS + j] * moved
                    sums[i] = term if sums[i] is None else sums[i] + term
            rounded = [total.astype(BF16) for total in sums]
            for i in range(3):
                feat[layer, i, a] = rounded[i]
            sig[a] = (rounded[1].astype(F32) * rounded[2].astype(F32)).astype(BF16)
            return tuple(rolled)

        zero = jnp.zeros((rows, lanes), F32)
        lax.fori_loop(0, blocks, body, (zero,) * (TAPS - 1), unroll=4)

    pair = 2 * rows
    for place, layer in enumerate((sec, other)):
        first_row = pl.multiple_of(layer * pair, pair)
        if place == 0:
            tables[0].wait()
            tables[4].wait()
        await_bytes(hbuf.at[layer], h_recv.at[place])
        stage_one(
            lambda g: jnp.stack(
                [
                    hbuf[layer, pl.ds(g * GROUP, GROUP), pl.ds(a * lanes, lanes)]
                    for a in range(blocks)
                ]
            ),
            first_row,
        )
        await_bytes(tbuf.at[layer], t_recv.at[place])
        values = tbuf[layer]
        for n in range(3 * TAPS):
            tapb[layer, n] = jnp.broadcast_to(values[:, n : n + 1], (rows, lanes))
        await_bytes(xbuf.at[layer], x_recv.at[layer])
        features_of(layer)
        stage_one(lambda g: sig[:, pl.ds(g * GROUP, GROUP), :], first_row + rows)
        if place == 0:
            tables[1].wait()
            tables[2].wait()
            tables[3].wait()

        def mixed_points(ks):
            both = stage_two(ks, first_row, pair)
            spec[ks, pl.ds(first_row, pair)] = both
            inverse_two(ks, product(both[:, :rows], both[:, rows:], False), 0)

        each_chunk(mixed_points)
        out = inverse_one(0)
        for g in range(groups):
            cbuf[layer, :, pl.ds(g * GROUP, GROUP), :] = out[:, :, g * lanes : (g + 1) * lanes]

    def send_home(layer, src, dst, send_sem, recv_sem):
        @pl.when(sec == layer)
        def _():
            pltpu.make_async_copy(src, dst, recv_sem).start()

        @pl.when(sec != layer)
        def _():
            remote(src, dst, send_sem, recv_sem, layer, ctx)

    def filter_grad_of(layer):
        out = inverse_one(1 + layer)
        for a in range(blocks):
            for g in range(groups):
                fgbuf[layer, pl.ds(g * GROUP, GROUP), pl.ds(a * lanes, lanes)] = out[
                    a, :, g * lanes : (g + 1) * lanes
                ].astype(BF16)
        send_home(layer, fgbuf.at[layer], fg_out.at[half(sec)], fg_send, fg_recv)

    for layer in range(sections - 1, -1, -1):
        if layer == sections - 1:
            await_bytes(ogbuf, og_recv)
            carried = ogbuf
        else:
            carried = igbuf.at[layer + 1]

        sig[...] = (carried[...].astype(F32) * feat[layer, 0].astype(F32)).astype(BF16)
        stage_one(lambda g: sig[:, pl.ds(g * GROUP, GROUP), :], 0)

        def grad_points(ks):
            d_spec = stage_two(ks, 0, rows)
            with_h = product(spec[ks, pl.ds(layer * pair, rows)], d_spec, True)
            with_w = product(spec[ks, pl.ds(layer * pair + rows, rows)], d_spec, True)
            inverse_two(ks, with_h, 0)
            inverse_two(ks, with_w, 1 + layer)

        each_chunk(grad_points)
        if layer == 0:
            filter_grad_of(layer)
        out = inverse_one(0)
        for g in range(groups):
            gwbuf[:, pl.ds(g * GROUP, GROUP), :] = out[:, :, g * lanes : (g + 1) * lanes]

        def transposed_at(step, after):
            a = blocks - 1 - step
            grad_w = gwbuf[a]
            grads = (
                carried[a].astype(F32) * cbuf[layer, a],
                grad_w * feat[layer, 2, a].astype(F32),
                grad_w * feat[layer, 1, a].astype(F32),
            )
            for i in range(3):
                gbuf[layer, i, a] = grads[i]
            total = None
            rolled = []
            for j in range(TAPS):
                part = tapb[layer, j] * grads[0]
                for i in range(1, 3):
                    part = part + tapb[layer, i * TAPS + j] * grads[i]
                if j == 0:
                    total = part
                else:
                    turned = pltpu.roll(part, lanes - j, 1)
                    rolled.append(turned)
                    total = total + jnp.where(lane < lanes - j, turned, after[j - 1])
            igbuf[layer, a] = total.astype(BF16)
            return tuple(rolled)

        zero = jnp.zeros((rows, lanes), F32)
        lax.fori_loop(0, blocks, transposed_at, (zero,) * (TAPS - 1), unroll=4)

        def send_ig(step, carry):
            to_ctx = lax.rem(ctx + step, blocks)
            dst = ig_out.at[row_block(sec, ctx)]
            remote(igbuf.at[layer, to_ctx], dst, ig_send, ig_recv, layer, to_ctx)
            return carry

        lax.fori_loop(1, blocks, send_ig, 0, unroll=True)
        send_home(layer, igbuf.at[layer, ctx], ig_out.at[row_block(sec, ctx)], ig_send, ig_recv)

        if layer == 0:
            for later in range(1, sections):
                filter_grad_of(later)

    for layer in range(sections - 1, -1, -1):
        for first in range(0, rows, 8):
            def add_taps(a, sums):
                grads = [gbuf[layer, i, a, pl.ds(first, 8)] for i in range(3)]
                new = []
                for j in range(TAPS):
                    moved = xs_ref[layer, j, a, pl.ds(first, 8)]
                    for i in range(3):
                        new.append(sums[j * 3 + i] + grads[i] * moved)
                return tuple(new)

            zero_8 = jnp.zeros((8, lanes), F32)
            sums = lax.fori_loop(0, blocks, add_taps, (zero_8,) * (3 * TAPS), unroll=True)
            lane_8 = lax.broadcasted_iota(jnp.int32, (8, lanes), 1)
            packed = zero_8
            for j in range(TAPS):
                for i in range(3):
                    column = jnp.sum(sums[j * 3 + i], axis=1, keepdims=True)
                    packed = jnp.where(lane_8 == i * TAPS + j, column, packed)
            tgbuf[layer, pl.ds(first, 8)] = packed
        send_home(layer, tgbuf.at[layer], tgin.at[half(sec)], tg_send, tg_recv)

    others = sections * blocks - 1
    await_bytes(x_ref.at[pl.ds(0, others * rows)], x_send)
    await_bytes(og_ref.at[pl.ds(0, (blocks - 1) * rows)], og_send)
    await_bytes(filt_ref.at[pl.ds(0, rows)], h_send)
    await_bytes(tbuf.at[0], t_send)
    await_bytes(ig_out.at[pl.ds(0, others * rows)], ig_send)
    await_bytes(fg_out.at[pl.ds(0, rows)], fg_send)
    await_bytes(tgbuf.at[0], tg_send)
    await_bytes(tgin, tg_recv)
    tg_out[...] = tgin[...].T[: 3 * TAPS].reshape(3 * TAPS, 1, channels)
    await_bytes(fg_out, fg_recv)
    await_bytes(ig_out, ig_recv)


def write_kernel(ig_ref, fg_ref, tg_ref, ig_out, fg_out, tg_out):
    ig_out[...] = ig_ref[...]
    fg_out[...] = fg_ref[...].astype(F32)
    tg_out[...] = tg_ref[...]


def kernel_shards(inputs, out_grad, filters, conv_taps):
    sections = lax.axis_size("section")
    blocks = lax.axis_size("ctx")
    _, depth, lanes = inputs.shape
    _, channels, length = filters.shape
    rows = channels // sections
    tables = right_angle_tables(blocks, lanes)
    taps = conv_taps.reshape(3 * TAPS, 1, depth)
    vmem = pltpu.VMEM
    dma = pltpu.SemaphoreType.DMA
    any_spec = pl.BlockSpec(memory_space=pl.ANY)
    hbm_spec = pl.BlockSpec(memory_space=pl.ANY)
    vmem_spec = pl.BlockSpec(memory_space=pltpu.VMEM)
    spectrum_rows = 2 * sections * rows
    in_grad, filter_grad, tap_sums = pl.pallas_call(
        functools.partial(mixer_kernel, sections),
        out_shape=(
            jax.ShapeDtypeStruct((depth, lanes), BF16),
            jax.ShapeDtypeStruct((channels, length), BF16),
            jax.ShapeDtypeStruct((3 * TAPS, 1, channels), F32),
        ),
        in_specs=[hbm_spec] * 9,
        out_specs=(any_spec, any_spec, vmem_spec),
        scratch_shapes=[
            vmem((depth, lanes), BF16),
            vmem((depth, lanes), BF16),
            vmem((channels, length), BF16),
            vmem((sections, blocks, rows, lanes), BF16),
            vmem((blocks, rows, lanes), BF16),
            vmem((sections, rows, length), BF16),
            vmem((3 * TAPS, 1, lanes), F32),
            vmem((lanes, lanes), F32),
            vmem((sections, rows, lanes), F32),
            vmem(tables[0].shape, BF16),
            vmem(tables[1].shape, BF16),
            vmem(tables[2].shape, BF16),
            vmem(tables[3].shape, BF16),
            vmem(tables[4].shape, F32),
            vmem((sections, 3 * TAPS, rows, lanes), F32),
            vmem((sections, TAPS, blocks, rows, lanes), F32),
            vmem((sections, 3, blocks, rows, lanes), BF16),
            vmem((blocks, rows, lanes), BF16),
            vmem((blocks, spectrum_rows, 2 * lanes), BF16),
            vmem((blocks, spectrum_rows, 2 * lanes), F32),
            vmem((1 + sections, blocks, 2, GROUP, rows // GROUP * lanes), BF16),
            vmem((sections, blocks, rows, lanes), F32),
            vmem((blocks, rows, lanes), F32),
            vmem((sections, 3, blocks, rows, lanes), F32),
            vmem((sections, blocks, rows, lanes), BF16),
            vmem((sections, rows, length), BF16),
            vmem((sections, rows, lanes), F32),
            vmem((channels, lanes), F32),
            dma(()),
            dma((sections,)),
            dma(()),
            dma(()),
            dma(()),
            dma((2,)),
            dma(()),
            dma((2,)),
            dma(()),
            dma(()),
            dma(()),
            dma(()),
            dma(()),
            dma(()),
            dma((5,)),
            dma(()),
            dma((3,)),
        ],
        compiler_params=pltpu.CompilerParams(
            collective_id=0, has_side_effects=True, vmem_limit_bytes=58 * 2**20
        ),
    )(inputs[0], out_grad, filters[0], taps, *(jnp.asarray(table) for table in tables))
    in_grad, filter_grad, tap_grad = pl.pallas_call(
        write_kernel,
        out_shape=(
            jax.ShapeDtypeStruct(in_grad.shape, BF16),
            jax.ShapeDtypeStruct(filter_grad.shape, F32),
            jax.ShapeDtypeStruct(tap_sums.shape, F32),
        ),
        in_specs=[vmem_spec] * 3,
        out_specs=(vmem_spec,) * 3,
        compiler_params=pltpu.CompilerParams(vmem_limit_bytes=58 * 2**20),
    )(in_grad, filter_grad, tap_sums)
    return (in_grad[None], filter_grad[None], tap_grad.reshape(1, 3, TAPS, channels))


def solution(mesh):
    placed = (
        P("section", None, "ctx"),
        P(None, "ctx"),
        P("section", "ctx", None),
        P("section", None, None, None),
    )

    def run(inputs, out_grad, filters, conv_taps):
        sections, blocks = mesh.shape["section"], mesh.shape["ctx"]
        rows = filters.shape[1] // (sections * blocks)
        lanes = inputs.shape[2] // blocks
        fits = sections == 2 and rows % GROUP == 0 and lanes == 128 and lanes % (sections * rows) == 0
        return jax.shard_map(
            kernel_shards if fits else shards,
            mesh=mesh,
            in_specs=placed,
            out_specs=(
                P("section", None, "ctx"),
                P("section", "ctx", None),
                P("section", None, None, "ctx"),
            ),
            check_vma=False,
        )(inputs, out_grad, filters, conv_taps)

    return run
```

```python
import functools
import math

import jax
import jax.numpy as jnp
import ml_dtypes
import numpy as np
from jax import lax
from jax.experimental import pallas as pl
from jax.experimental.pallas import tpu as pltpu
from jax.sharding import PartitionSpec as P

PRECISE = lax.Precision.HIGH


def shifted(block, axis, distance):
    devices = range(lax.axis_size(axis))
    route = [(i - distance, i) for i in devices if i - distance in devices]
    return lax.ppermute(block, axis, route)


def angle_table(row_count, col_count, modulus):
    row_ids = lax.broadcasted_iota(jnp.int32, (row_count, col_count), 0)
    col_ids = lax.broadcasted_iota(jnp.int32, (row_count, col_count), 1)
    product_mod = row_ids * col_ids % modulus
    angles = product_mod.astype(jnp.float32) * (2.0 * math.pi / modulus)
    return (jnp.cos(angles), jnp.sin(angles))


def make_tables(blocks_a, block_b):
    half_a = blocks_a // 2
    total_n = blocks_a * block_b
    return (
        angle_table(blocks_a, half_a, blocks_a),
        angle_table(half_a, blocks_a, blocks_a),
        angle_table(blocks_a, block_b, total_n),
        angle_table(block_b, block_b, block_b),
    )


def forward_spectrum(signal, tables):
    cos_one, sin_one = tables[0]
    cos_tw, sin_tw = tables[2]
    cos_two, sin_two = tables[3]
    channels = signal.shape[0]
    half_a = cos_one.shape[1]
    block_b = cos_two.shape[0]
    shaped = signal.reshape(channels, half_a, block_b)
    real_y = jnp.einsum("ka,cab->ckb", cos_one, shaped, precision=PRECISE)
    imag_y = -jnp.einsum("ka,cab->ckb", sin_one, shaped, precision=PRECISE)
    real_z = real_y * cos_tw + imag_y * sin_tw
    imag_z = imag_y * cos_tw - real_y * sin_tw
    real_x = jnp.einsum("ckb,mb->ckm", real_z, cos_two, precision=PRECISE) + jnp.einsum(
        "ckb,mb->ckm", imag_z, sin_two, precision=PRECISE
    )
    imag_x = jnp.einsum("ckb,mb->ckm", imag_z, cos_two, precision=PRECISE) - jnp.einsum(
        "ckb,mb->ckm", real_z, sin_two, precision=PRECISE
    )
    return (real_x, imag_x)


def inverse_signal(real_x, imag_x, tables):
    cos_one, sin_one = tables[1]
    cos_tw, sin_tw = tables[2]
    cos_two, sin_two = tables[3]
    channels = real_x.shape[0]
    half_a = cos_one.shape[0]
    block_b = cos_two.shape[0]
    total_n = cos_one.shape[1] * block_b
    real_p = jnp.einsum("ckm,mb->ckb", real_x, cos_two, precision=PRECISE) - jnp.einsum(
        "ckm,mb->ckb", imag_x, sin_two, precision=PRECISE
    )
    imag_p = jnp.einsum("ckm,mb->ckb", real_x, sin_two, precision=PRECISE) + jnp.einsum(
        "ckm,mb->ckb", imag_x, cos_two, precision=PRECISE
    )
    real_q = real_p * cos_tw - imag_p * sin_tw
    imag_q = real_p * sin_tw + imag_p * cos_tw
    summed = jnp.einsum("ak,ckb->cab", cos_one, real_q, precision=PRECISE) - jnp.einsum(
        "ak,ckb->cab", sin_one, imag_q, precision=PRECISE
    )
    return summed.reshape(channels, half_a * block_b) / total_n


def times_conj(real_a, imag_a, real_b, imag_b):
    return (real_a * real_b + imag_a * imag_b, real_a * imag_b - imag_a * real_b)


def features(padded, weights, length):
    summed = jnp.zeros((3, padded.shape[0], length), jnp.float32)
    for offset in range(7):
        window = padded[:, 6 - offset : 6 - offset + length].astype(jnp.float32)
        summed = summed + weights[:, offset, :, None] * window[None]
    return summed.astype(jnp.bfloat16)


def transposed(grad_all, weights):
    length = grad_all.shape[2]
    padded = jnp.pad(grad_all, ((0, 0), (0, 0), (0, 6)))
    summed = jnp.zeros(grad_all.shape[1:], jnp.float32)
    for offset in range(7):
        summed = summed + jnp.sum(
            weights[:, offset, :, None] * padded[:, :, offset : offset + length], axis=0
        )
    return summed


def tap_grads(padded, grad_all):
    length = grad_all.shape[2]
    per_offset = []
    for offset in range(7):
        window = padded[:, 6 - offset : 6 - offset + length].astype(jnp.float32)
        per_offset.append(jnp.sum(grad_all * window[None], axis=2))
    return jnp.stack(per_offset, axis=1)


def take_rows(array, first_ch, count, axis_num):
    return lax.dynamic_slice_in_dim(array, first_ch, count, axis_num)


def masked_write(array, update, first_ch, active, axis_num):
    previous = lax.dynamic_slice_in_dim(array, first_ch, update.shape[axis_num], axis_num)
    return lax.dynamic_update_slice_in_dim(
        array, jnp.where(active, update, previous), first_ch, axis_num
    )


def shards(inputs, out_grad, filters, conv_taps):
    x_rows = inputs[0]
    tok_dev = x_rows.shape[1]
    section_count = lax.axis_size("section")
    section_idx = lax.axis_index("section")
    ctx_idx = lax.axis_index("ctx")
    weights = conv_taps[0]
    channels = filters.shape[1]
    length = filters.shape[2]
    blocks_a = 2 * length // tok_dev
    own_taps = lax.dynamic_slice_in_dim(weights, ctx_idx * channels, channels, 2)
    prior_cols = shifted(x_rows[:, tok_dev - 6 :], "ctx", 1)
    featured_rows = features(jnp.concatenate([prior_cols, x_rows], axis=1), weights, tok_dev)
    x_chan, featured, grad_chan = (
        lax.all_to_all(x_rows[None], "ctx", split_axis=1, concat_axis=2, tiled=True),
        lax.all_to_all(featured_rows, "ctx", split_axis=1, concat_axis=2, tiled=True),
        lax.all_to_all(out_grad[None], "ctx", split_axis=1, concat_axis=2, tiled=True),
    )
    x_chan = x_chan[0]
    x_padded = jnp.pad(x_chan, ((0, 0), (6, 0)))
    grad_chan = grad_chan[0]
    tables = make_tables(blocks_a, tok_dev)
    key_full = featured[1].astype(jnp.float32)
    mixed_kv = key_full * featured[2].astype(jnp.float32)
    real_h, imag_h = forward_spectrum(filters[0].astype(jnp.float32), tables)
    real_w, imag_w = forward_spectrum(mixed_kv, tables)
    convolved = inverse_signal(
        real_h * real_w - imag_h * imag_w, real_h * imag_w + imag_h * real_w, tables
    )
    block_ch = 2
    block_count = channels // block_ch
    last_section = section_count - 1
    turns = block_count + section_count - 1
    dx_init = jnp.zeros((channels, length), jnp.bfloat16)

    def advance(turn_idx, carried):
        incoming, dz_all, dx_store, tap_acc = carried
        block_id = turn_idx - (last_section - section_idx)
        active = (block_id >= 0) & (block_id < block_count)
        first_ch = jnp.clip(block_id, 0, block_count - 1) * block_ch
        from_next = take_rows(grad_chan, first_ch, block_ch, 0)
        grad_in = jnp.where(section_idx == last_section, from_next, incoming).astype(jnp.float32)
        feat_blk = take_rows(featured, first_ch, block_ch, 1).astype(jnp.float32)
        grad_z = grad_in * feat_blk[0]
        grad_q = grad_in * take_rows(convolved, first_ch, block_ch, 0)
        real_d, imag_d = forward_spectrum(grad_z, tables)
        real_c, imag_c = times_conj(
            take_rows(real_h, first_ch, block_ch, 0),
            take_rows(imag_h, first_ch, block_ch, 0),
            real_d,
            imag_d,
        )
        grad_w = inverse_signal(real_c, imag_c, tables)
        grad_all = jnp.stack([grad_q, grad_w * feat_blk[2], grad_w * feat_blk[1]])
        in_blk = transposed(grad_all, take_rows(own_taps, first_ch, block_ch, 2)).astype(
            jnp.bfloat16
        )
        tap_new = tap_grads(take_rows(x_padded, first_ch, block_ch, 0), grad_all)
        tap_acc = masked_write(tap_acc, tap_new, first_ch, active, 2)
        dz_all = masked_write(dz_all, grad_z, first_ch, active, 0)
        outgoing = shifted(in_blk, "section", -1)
        dx_store = masked_write(dx_store, in_blk, first_ch, active, 0)
        return (outgoing, dz_all, dx_store, tap_acc)

    start_state = (
        jnp.zeros((block_ch, length), jnp.bfloat16),
        jnp.zeros((channels, length), jnp.float32),
        dx_init,
        jnp.zeros((3, 7, channels), jnp.float32),
    )
    final_state = lax.fori_loop(0, turns, advance, start_state)
    dz_all = final_state[1]
    dx_store = final_state[2]
    tap_acc = final_state[3]
    real_d, imag_d = forward_spectrum(dz_all, tables)
    real_c, imag_c = times_conj(real_w, imag_w, real_d, imag_d)
    filter_grad = inverse_signal(real_c, imag_c, tables)
    in_rows = lax.all_to_all(dx_store, "ctx", split_axis=1, concat_axis=0, tiled=True)
    return (in_rows[None], filter_grad[None], tap_acc[None])


TAPS = 7
GROUP = 16
CHUNK = 4
MESH = pl.DeviceIdType.MESH
F32 = jnp.float32
BF16 = jnp.bfloat16


def right_angle_tables(blocks_a, block_b):
    total_n = blocks_a * block_b
    first_k = np.arange(blocks_a)
    phase_one = 2 * np.pi * np.outer(first_k + 0.25, np.arange(blocks_a)) / blocks_a
    one = np.stack([np.cos(phase_one), -np.sin(phase_one)])
    first = np.einsum("rka,cd->krcad", one, np.eye(GROUP))
    first = first.reshape(2 * blocks_a * GROUP, blocks_a * GROUP)
    phase_turn = 2 * np.pi * np.outer(first_k + 0.25, np.arange(block_b)) / total_n
    turn = np.stack([np.cos(phase_turn), -np.sin(phase_turn)])
    turn = np.repeat(turn[:, :, None, :], GROUP, axis=2).astype(np.float32)
    phase_two = 2 * np.pi * np.outer(np.arange(block_b), np.arange(block_b)) / block_b
    real, imag = np.cos(phase_two), -np.sin(phase_two)
    second = np.concatenate(
        [np.concatenate([real, imag], axis=1), np.concatenate([-imag, real], axis=1)], axis=0
    )
    rounded = [
        array.astype(ml_dtypes.bfloat16) for array in (first, first.T / total_n, second, second.T)
    ]
    return (*rounded, turn)


def mixer_kernel(
    sections,
    x_hbm,
    og_hbm,
    filt_hbm,
    tap_ref,
    one_ref,
    one_inv_ref,
    two_ref,
    two_inv_ref,
    turn_ref,
    ig_out,
    fg_out,
    tg_out,
    x_ref,
    og_ref,
    filt_ref,
    xbuf,
    ogbuf,
    hbuf,
    tap_blk,
    tap_rows,
    tbuf,
    one_v,
    one_inv_v,
    two_v,
    two_inv_v,
    turn_v,
    tapb,
    xs_ref,
    feat,
    sig,
    ybuf,
    spec,
    qbuf,
    cbuf,
    gwbuf,
    gbuf,
    igbuf,
    fgbuf,
    tgbuf,
    tgin,
    x_send,
    x_recv,
    og_send,
    og_recv,
    h_send,
    h_recv,
    t_send,
    t_recv,
    ig_send,
    ig_recv,
    fg_send,
    fg_recv,
    tg_send,
    tg_recv,
    table_sem,
    blk_sem,
    load_sem,
):
    sec = lax.axis_index("section")
    ctx = lax.axis_index("ctx")
    blocks = xbuf.shape[1]
    rows = xbuf.shape[2]
    lanes = xbuf.shape[3]
    groups = rows // GROUP
    other = 1 - sec

    tables = [
        pltpu.make_async_copy(src, dst, table_sem.at[n])
        for n, (src, dst) in enumerate(
            ((one_ref, one_v), (two_ref, two_v), (one_inv_ref, one_inv_v), (two_inv_ref, two_inv_v), (turn_ref, turn_v))
        )
    ]

    channels = sections * rows
    tap_first = ctx * channels
    tap_lane = pl.multiple_of(tap_first // lanes * lanes, lanes)
    tap_load = pltpu.make_async_copy(tap_ref.at[:, :, pl.ds(tap_lane, lanes)], tap_blk, blk_sem)
    tap_load.start()

    loads = [
        pltpu.make_async_copy(src, dst, load_sem.at[n])
        for n, (src, dst) in enumerate(((filt_hbm, filt_ref), (x_hbm, x_ref), (og_hbm, og_ref)))
    ]
    for load in loads:
        load.start()

    barrier = pltpu.get_barrier_semaphore()

    def greet(step, carry):
        to_ctx = lax.rem(ctx + step, blocks)
        pl.semaphore_signal(barrier, inc=1, device_id=(other, to_ctx), device_id_type=MESH)

        @pl.when(step > 0)
        def _():
            pl.semaphore_signal(barrier, inc=1, device_id=(sec, to_ctx), device_id_type=MESH)

        return carry

    lax.fori_loop(0, blocks, greet, 0, unroll=True)
    for table in tables:
        table.start()
    pl.semaphore_wait(barrier, sections * blocks - 1)

    def row_block(to_sec, to_ctx):
        return pl.ds(pl.multiple_of((to_ctx * sections + to_sec) * rows, rows), rows)

    def half(which):
        return pl.ds(pl.multiple_of(which * rows, rows), rows)

    def remote(src, dst, send_sem, recv_sem, to_sec, to_ctx):
        pltpu.make_async_remote_copy(
            src_ref=src,
            dst_ref=dst,
            send_sem=send_sem,
            recv_sem=recv_sem,
            device_id=(to_sec, to_ctx),
            device_id_type=MESH,
        ).start()

    def await_bytes(ref, sem):
        pltpu.make_async_copy(ref, ref, sem).wait()

    loads[0].wait()
    remote(filt_ref.at[half(other)], hbuf.at[sec], h_send, h_recv.at[1], other, ctx)
    pltpu.make_async_copy(filt_ref.at[half(sec)], hbuf.at[sec], h_recv.at[0]).start()

    def send_x(to_sec):
        def send(step, carry):
            to_ctx = lax.rem(ctx + step, blocks)
            src = x_ref.at[row_block(to_sec, to_ctx)]
            remote(src, xbuf.at[sec, ctx], x_send, x_recv.at[sec], to_sec, to_ctx)
            return carry

        return send

    loads[1].wait()
    pltpu.make_async_copy(
        x_ref.at[row_block(sec, ctx)], xbuf.at[sec, ctx], x_recv.at[sec]
    ).start()
    lax.fori_loop(1, blocks, send_x(sec), 0, unroll=True)
    lax.fori_loop(0, blocks, send_x(other), 0, unroll=True)

    def send_og(step, carry):
        to_ctx = lax.rem(ctx + step, blocks)
        remote(og_ref.at[row_block(sec, to_ctx)], ogbuf.at[ctx], og_send, og_recv, sec, to_ctx)
        return carry

    loads[2].wait()
    pltpu.make_async_copy(og_ref.at[row_block(sec, ctx)], ogbuf.at[ctx], og_recv).start()
    lax.fori_loop(1, blocks, send_og, 0, unroll=True)

    tap_load.wait()
    tap_rows[...] = jnp.zeros_like(tap_rows)
    tap_rows[pl.ds(0, 3 * TAPS)] = tap_blk[...].reshape(3 * TAPS, lanes)
    tap_rows[...] = tap_rows[...].T

    def tap_half(which):
        first = lax.rem(tap_first, lanes) + which * rows
        return tap_rows.at[pl.ds(pl.multiple_of(first, rows), rows)]

    remote(tap_half(other), tbuf.at[sec], t_send, t_recv.at[1], other, ctx)
    pltpu.make_async_copy(tap_half(sec), tbuf.at[sec], t_recv.at[0]).start()

    def rows_at(first):
        return pl.ds(first if isinstance(first, int) else pl.multiple_of(first, GROUP), GROUP)

    chunk_size = min(CHUNK, blocks)

    def each_chunk(body):
        def step(n, carry):
            body(pl.ds(n * chunk_size, chunk_size))
            return carry

        lax.fori_loop(0, blocks // chunk_size, step, 0, unroll=True)

    def stage_one(blocks_of, first_row):
        cols = jnp.concatenate(
            [blocks_of(g).reshape(blocks * GROUP, lanes) for g in range(groups)], axis=1
        )

        def chunk(ks):
            out = jnp.dot(
                one_v[pl.ds(ks.start * 2 * GROUP, ks.size * 2 * GROUP)],
                cols,
                preferred_element_type=F32,
            ).reshape(ks.size, 2, GROUP, groups * lanes)
            turn_r, turn_i = turn_v[0, ks], turn_v[1, ks]
            for g in range(groups):
                real = out[:, 0, :, g * lanes : (g + 1) * lanes]
                imag = out[:, 1, :, g * lanes : (g + 1) * lanes]
                where = rows_at(first_row + g * GROUP)
                ybuf[ks, where, pl.ds(0, lanes)] = (real * turn_r - imag * turn_i).astype(BF16)
                ybuf[ks, where, pl.ds(lanes, lanes)] = (real * turn_i + imag * turn_r).astype(BF16)

        each_chunk(chunk)

    def stage_two(ks, first_row, count):
        operand = ybuf[ks, pl.ds(first_row, count)].reshape(ks.size * count, 2 * lanes)
        out = jnp.dot(operand, two_v[...], preferred_element_type=F32)
        return out.reshape(ks.size, count, 2 * lanes)

    def product(left, right, conj):
        left_r, left_i = left[..., :lanes], left[..., lanes:]
        right_r, right_i = right[..., :lanes], right[..., lanes:]
        if conj:
            real = left_r * right_r + left_i * right_i
            imag = left_r * right_i - left_i * right_r
        else:
            real = left_r * right_r - left_i * right_i
            imag = left_r * right_i + left_i * right_r
        return jnp.concatenate([real, imag], axis=2).astype(BF16)

    def inverse_two(ks, operand, slot):
        count = operand.shape[1]
        out = jnp.dot(
            operand.reshape(ks.size * count, 2 * lanes), two_inv_v[...], preferred_element_type=F32
        ).reshape(ks.size, count, 2 * lanes)
        turn_r, turn_i = turn_v[0, ks], turn_v[1, ks]
        for g in range(groups):
            real = out[:, g * GROUP : (g + 1) * GROUP, :lanes]
            imag = out[:, g * GROUP : (g + 1) * GROUP, lanes:]
            where = pl.ds(g * lanes, lanes)
            qbuf[slot, ks, 0, :, where] = (real * turn_r + imag * turn_i).astype(BF16)
            qbuf[slot, ks, 1, :, where] = (imag * turn_r - real * turn_i).astype(BF16)

    def inverse_one(slot):
        out = jnp.dot(
            one_inv_v[...],
            qbuf[slot].reshape(2 * blocks * GROUP, groups * lanes),
            preferred_element_type=F32,
        )
        return out.reshape(blocks, GROUP, groups * lanes)

    lane = lax.broadcasted_iota(jnp.int32, (rows, lanes), 1)

    def features_of(layer):
        def body(a, before):
            window = xbuf[layer, a].astype(F32)
            sums = [None] * 3
            rolled = []
            for j in range(TAPS):
                if j == 0:
                    moved = window
                else:
                    turned = pltpu.roll(window, j, 1)
                    rolled.append(turned)
                    moved = jnp.where(lane < j, before[j - 1], turned)
                xs_ref[layer, j, a] = moved
                for i in range(3):
                    term = tapb[layer, i * TAPS + j] * moved
                    sums[i] = term if sums[i] is None else sums[i] + term
            rounded = [total.astype(BF16) for total in sums]
            for i in range(3):
                feat[layer, i, a] = rounded[i]
            sig[a] = (rounded[1].astype(F32) * rounded[2].astype(F32)).astype(BF16)
            return tuple(rolled)

        zero = jnp.zeros((rows, lanes), F32)
        lax.fori_loop(0, blocks, body, (zero,) * (TAPS - 1), unroll=True)

    pair = 2 * rows
    for place, layer in enumerate((sec, other)):
        first_row = pl.multiple_of(layer * pair, pair)
        if place == 0:
            tables[0].wait()
            tables[4].wait()
        await_bytes(hbuf.at[layer], h_recv.at[place])
        stage_one(
            lambda g: jnp.stack(
                [
                    hbuf[layer, pl.ds(g * GROUP, GROUP), pl.ds(a * lanes, lanes)]
                    for a in range(blocks)
                ]
            ),
            first_row,
        )
        await_bytes(tbuf.at[layer], t_recv.at[place])
        values = tbuf[layer]
        for n in range(3 * TAPS):
            tapb[layer, n] = jnp.broadcast_to(values[:, n : n + 1], (rows, lanes))
        await_bytes(xbuf.at[layer], x_recv.at[layer])
        features_of(layer)
        stage_one(lambda g: sig[:, pl.ds(g * GROUP, GROUP), :], first_row + rows)
        if place == 0:
            tables[1].wait()
            tables[2].wait()
            tables[3].wait()

        def mixed_points(ks):
            both = stage_two(ks, first_row, pair)
            spec[ks, pl.ds(first_row, pair)] = both
            inverse_two(ks, product(both[:, :rows], both[:, rows:], False), 0)

        each_chunk(mixed_points)
        out = inverse_one(0)
        for g in range(groups):
            cbuf[layer, :, pl.ds(g * GROUP, GROUP), :] = out[:, :, g * lanes : (g + 1) * lanes]

    def send_home(layer, src, dst, send_sem, recv_sem):
        @pl.when(sec == layer)
        def _():
            pltpu.make_async_copy(src, dst, recv_sem).start()

        @pl.when(sec != layer)
        def _():
            remote(src, dst, send_sem, recv_sem, layer, ctx)

    def filter_grad_of(layer):
        out = inverse_one(1 + layer)
        for a in range(blocks):
            for g in range(groups):
                fgbuf[layer, pl.ds(g * GROUP, GROUP), pl.ds(a * lanes, lanes)] = out[
                    a, :, g * lanes : (g + 1) * lanes
                ].astype(BF16)
        send_home(layer, fgbuf.at[layer], fg_out.at[half(sec)], fg_send, fg_recv)

    for layer in range(sections - 1, -1, -1):
        if layer == sections - 1:
            await_bytes(ogbuf, og_recv)
            carried = ogbuf
        else:
            carried = igbuf.at[layer + 1]

        sig[...] = (carried[...].astype(F32) * feat[layer, 0].astype(F32)).astype(BF16)
        stage_one(lambda g: sig[:, pl.ds(g * GROUP, GROUP), :], 0)

        def grad_points(ks):
            d_spec = stage_two(ks, 0, rows)
            with_h = product(spec[ks, pl.ds(layer * pair, rows)], d_spec, True)
            with_w = product(spec[ks, pl.ds(layer * pair + rows, rows)], d_spec, True)
            inverse_two(ks, with_h, 0)
            inverse_two(ks, with_w, 1 + layer)

        each_chunk(grad_points)
        if layer == 0:
            filter_grad_of(layer)
        out = inverse_one(0)
        for g in range(groups):
            gwbuf[:, pl.ds(g * GROUP, GROUP), :] = out[:, :, g * lanes : (g + 1) * lanes]

        def transposed_at(step, after):
            a = blocks - 1 - step
            grad_w = gwbuf[a]
            grads = (
                carried[a].astype(F32) * cbuf[layer, a],
                grad_w * feat[layer, 2, a].astype(F32),
                grad_w * feat[layer, 1, a].astype(F32),
            )
            for i in range(3):
                gbuf[layer, i, a] = grads[i]
            total = None
            rolled = []
            for j in range(TAPS):
                part = tapb[layer, j] * grads[0]
                for i in range(1, 3):
                    part = part + tapb[layer, i * TAPS + j] * grads[i]
                if j == 0:
                    total = part
                else:
                    turned = pltpu.roll(part, lanes - j, 1)
                    rolled.append(turned)
                    total = total + jnp.where(lane < lanes - j, turned, after[j - 1])
            igbuf[layer, a] = total.astype(BF16)
            return tuple(rolled)

        zero = jnp.zeros((rows, lanes), F32)
        lax.fori_loop(0, blocks, transposed_at, (zero,) * (TAPS - 1), unroll=True)

        def send_ig(step, carry):
            to_ctx = lax.rem(ctx + step, blocks)
            dst = ig_out.at[row_block(sec, ctx)]
            remote(igbuf.at[layer, to_ctx], dst, ig_send, ig_recv, layer, to_ctx)
            return carry

        lax.fori_loop(1, blocks, send_ig, 0, unroll=True)
        send_home(layer, igbuf.at[layer, ctx], ig_out.at[row_block(sec, ctx)], ig_send, ig_recv)

        if layer == 0:
            for later in range(1, sections):
                filter_grad_of(later)

    for layer in range(sections - 1, -1, -1):
        for first in range(0, rows, 8):
            def add_taps(a, sums):
                grads = [gbuf[layer, i, a, pl.ds(first, 8)] for i in range(3)]
                new = []
                for j in range(TAPS):
                    moved = xs_ref[layer, j, a, pl.ds(first, 8)]
                    for i in range(3):
                        new.append(sums[j * 3 + i] + grads[i] * moved)
                return tuple(new)

            zero_8 = jnp.zeros((8, lanes), F32)
            sums = lax.fori_loop(0, blocks, add_taps, (zero_8,) * (3 * TAPS), unroll=True)
            lane_8 = lax.broadcasted_iota(jnp.int32, (8, lanes), 1)
            packed = zero_8
            for j in range(TAPS):
                for i in range(3):
                    column = jnp.sum(sums[j * 3 + i], axis=1, keepdims=True)
                    packed = jnp.where(lane_8 == i * TAPS + j, column, packed)
            tgbuf[layer, pl.ds(first, 8)] = packed
        send_home(layer, tgbuf.at[layer], tgin.at[half(sec)], tg_send, tg_recv)

    others = sections * blocks - 1
    await_bytes(x_ref.at[pl.ds(0, others * rows)], x_send)
    await_bytes(og_ref.at[pl.ds(0, (blocks - 1) * rows)], og_send)
    await_bytes(filt_ref.at[pl.ds(0, rows)], h_send)
    await_bytes(tbuf.at[0], t_send)
    await_bytes(ig_out.at[pl.ds(0, others * rows)], ig_send)
    await_bytes(fg_out.at[pl.ds(0, rows)], fg_send)
    await_bytes(tgbuf.at[0], tg_send)
    await_bytes(tgin, tg_recv)
    tg_out[...] = tgin[...].T[: 3 * TAPS].reshape(3 * TAPS, 1, channels)
    await_bytes(fg_out, fg_recv)
    await_bytes(ig_out, ig_recv)


def write_kernel(ig_ref, fg_ref, tg_ref, ig_out, fg_out, tg_out):
    ig_out[...] = ig_ref[...]
    fg_out[...] = fg_ref[...].astype(F32)
    tg_out[...] = tg_ref[...]


def kernel_shards(inputs, out_grad, filters, conv_taps):
    sections = lax.axis_size("section")
    blocks = lax.axis_size("ctx")
    _, depth, lanes = inputs.shape
    _, channels, length = filters.shape
    rows = channels // sections
    tables = right_angle_tables(blocks, lanes)
    taps = conv_taps.reshape(3 * TAPS, 1, depth)
    vmem = pltpu.VMEM
    dma = pltpu.SemaphoreType.DMA
    any_spec = pl.BlockSpec(memory_space=pl.ANY)
    hbm_spec = pl.BlockSpec(memory_space=pl.ANY)
    vmem_spec = pl.BlockSpec(memory_space=pltpu.VMEM)
    spectrum_rows = 2 * sections * rows
    in_grad, filter_grad, tap_sums = pl.pallas_call(
        functools.partial(mixer_kernel, sections),
        out_shape=(
            jax.ShapeDtypeStruct((depth, lanes), BF16),
            jax.ShapeDtypeStruct((channels, length), BF16),
            jax.ShapeDtypeStruct((3 * TAPS, 1, channels), F32),
        ),
        in_specs=[hbm_spec] * 9,
        out_specs=(any_spec, any_spec, vmem_spec),
        scratch_shapes=[
            vmem((depth, lanes), BF16),
            vmem((depth, lanes), BF16),
            vmem((channels, length), BF16),
            vmem((sections, blocks, rows, lanes), BF16),
            vmem((blocks, rows, lanes), BF16),
            vmem((sections, rows, length), BF16),
            vmem((3 * TAPS, 1, lanes), F32),
            vmem((lanes, lanes), F32),
            vmem((sections, rows, lanes), F32),
            vmem(tables[0].shape, BF16),
            vmem(tables[1].shape, BF16),
            vmem(tables[2].shape, BF16),
            vmem(tables[3].shape, BF16),
            vmem(tables[4].shape, F32),
            vmem((sections, 3 * TAPS, rows, lanes), F32),
            vmem((sections, TAPS, blocks, rows, lanes), F32),
            vmem((sections, 3, blocks, rows, lanes), BF16),
            vmem((blocks, rows, lanes), BF16),
            vmem((blocks, spectrum_rows, 2 * lanes), BF16),
            vmem((blocks, spectrum_rows, 2 * lanes), F32),
            vmem((1 + sections, blocks, 2, GROUP, rows // GROUP * lanes), BF16),
            vmem((sections, blocks, rows, lanes), F32),
            vmem((blocks, rows, lanes), F32),
            vmem((sections, 3, blocks, rows, lanes), F32),
            vmem((sections, blocks, rows, lanes), BF16),
            vmem((sections, rows, length), BF16),
            vmem((sections, rows, lanes), F32),
            vmem((channels, lanes), F32),
            dma(()),
            dma((sections,)),
            dma(()),
            dma(()),
            dma(()),
            dma((2,)),
            dma(()),
            dma((2,)),
            dma(()),
            dma(()),
            dma(()),
            dma(()),
            dma(()),
            dma(()),
            dma((5,)),
            dma(()),
            dma((3,)),
        ],
        compiler_params=pltpu.CompilerParams(
            collective_id=0, has_side_effects=True, vmem_limit_bytes=58 * 2**20
        ),
    )(inputs[0], out_grad, filters[0], taps, *(jnp.asarray(table) for table in tables))
    in_grad, filter_grad, tap_grad = pl.pallas_call(
        write_kernel,
        out_shape=(
            jax.ShapeDtypeStruct(in_grad.shape, BF16),
            jax.ShapeDtypeStruct(filter_grad.shape, F32),
            jax.ShapeDtypeStruct(tap_sums.shape, F32),
        ),
        in_specs=[vmem_spec] * 3,
        out_specs=(vmem_spec,) * 3,
        compiler_params=pltpu.CompilerParams(vmem_limit_bytes=58 * 2**20),
    )(in_grad, filter_grad, tap_sums)
    return (in_grad[None], filter_grad[None], tap_grad.reshape(1, 3, TAPS, channels))


def solution(mesh):
    placed = (
        P("section", None, "ctx"),
        P(None, "ctx"),
        P("section", "ctx", None),
        P("section", None, None, None),
    )

    def run(inputs, out_grad, filters, conv_taps):
        sections, blocks = mesh.shape["section"], mesh.shape["ctx"]
        rows = filters.shape[1] // (sections * blocks)
        lanes = inputs.shape[2] // blocks
        fits = sections == 2 and rows % GROUP == 0 and lanes == 128 and lanes % (sections * rows) == 0
        return jax.shard_map(
            kernel_shards if fits else shards,
            mesh=mesh,
            in_specs=placed,
            out_specs=(
                P("section", None, "ctx"),
                P("section", "ctx", None),
                P("section", None, None, "ctx"),
            ),
            check_vma=False,
        )(inputs, out_grad, filters, conv_taps)

    return run
```
